512 devices in a mesh: rows: 128 (over z, x_hi, y), grp: 4 (over x_lo, core).
Axes of the slice: x: 4 (x_hi: 2, x_lo: 2; x = x_hi * 2 + x_lo), y: 8, z: 8, core: 2. Of those that a mesh axis runs over, the one named last changes fastest.
Arguments:
- tokens: bfloat16 [512, 512, 256], P('rows', 'grp'), may hold values from -36 to 36
- norm_gain: float32 [256], replicated, may hold values from 0.1 to 1.9
- qkv_weight: bfloat16 [256, 768], replicated, may hold values from -0.375 to 0.375
- head_scale: float32 [4], replicated, may hold values from 2 to 12
- out_weight: bfloat16 [256, 256], replicated, may hold values from -0.375 to 0.375
- cotangent: bfloat16 [512, 512, 256], P('rows', 'grp'), may hold values from -6 to 6
Outputs:
- output: bfloat16 [512, 512, 256], P('rows', 'grp')
- token_grad: float32 [512, 512, 256], P('rows', 'grp')
- gain_grad: float32 [256], replicated
- qkv_grad: float32 [256, 768], replicated
- scale_grad: float32 [4], replicated
- out_grad: float32 [256, 256], replicated
The draws below stay inside these ranges and needn't reach their ends.
All inputs are finite; a program needn't handle non-finite values.
Results may differ from the reference program's by a relative error of at most 0.011.
Values may be sent and summed in bfloat16 or wider, within the bound.
No kernel may reach another device: no remote copies, remote signals or barrier semaphores. Data moves between devices by JAX's collectives and lax.ppermute only.
A program may use at most 64 MiB of HBM per device.

```python
import math
import jax
import jax.numpy as jnp
from jax import lax

HEADS = 4
HEAD = 64
C = 256
WIN = 3
GR = 512
GC = 512
TOKENS = 262144


def draw_tokens(key, part):
    key = jax.random.fold_in(key, 11)
    key_rows, key_cols, key_noise = jax.random.split(key, 3)
    low = math.log(0.3)
    high = math.log(3.0)
    row_scale = jnp.exp(jax.random.uniform(key_rows, (GR, GC, 1), jnp.float32, low, high))
    col_scale = jnp.exp(jax.random.uniform(key_cols, (1, 1, C), jnp.float32, low, high))
    noise = jnp.clip(jax.random.normal(key_noise, (GR, GC, C), jnp.float32), -4.0, 4.0)
    values = row_scale * col_scale * noise
    return values.astype(jnp.bfloat16)


def block_scale(rng, shape, pieces, smallest, high):
    gain, own = 1.0, jax.random.fold_in(rng, 6)
    for dim, parts in pieces:
        steps = jnp.exp(jax.random.uniform(jax.random.fold_in(own, dim), (parts,), jnp.float32, smallest / len(pieces), high / len(pieces)))
        gain = gain * jnp.repeat(steps, shape[dim] // parts).reshape([-1 if axis == dim else 1 for axis in range(len(shape))])
    return gain


def scatter_about(stream_key, extent, width, reach, cuts=(), dtype=jnp.bfloat16):
    entries = width * jax.random.normal(stream_key, extent, jnp.float32)
    if cuts:
        entries = entries * block_scale(stream_key, extent, cuts, -0.22, 0.18)
    return jnp.clip(entries, -reach, reach).astype(dtype)


def setup_inputs(seed: int = 0) -> dict:
    seeds = jax.random.split(jax.random.key(seed), 7)
    tokens = draw_tokens(jax.random.fold_in(seeds[6], 71), 0)
    norm_gain = jnp.clip(1.0 + 0.18 * jax.random.normal(seeds[1], (C,), jnp.float32), 0.1, 1.9)
    qkv_weight = scatter_about(seeds[2], (C, 3 * C), C ** -0.5, 0.375)
    head_scale = jnp.clip(jnp.exp(jax.random.uniform(seeds[3], (HEADS,), jnp.float32, math.log(2.0), math.log(12.0))), 2.0, 12.0)
    out_weight = scatter_about(seeds[4], (C, C), C ** -0.5, 0.375)
    cotangent = scatter_about(seeds[5], (GR, GC, C), 1.0, 6.0, ((0, 128), (1, 4)))
    return {"tokens": tokens, "norm_gain": norm_gain, "qkv_weight": qkv_weight, "head_scale": head_scale, "out_weight": out_weight, "cotangent": cotangent}


EPS = 1e-06

def window(array, row_off, col_off):
    return array[row_off:row_off + GR, col_off:col_off + GC]

def reference(tokens, norm_gain, qkv_weight, head_scale, out_weight, cotangent):
    tok_f32 = tokens.astype(jnp.float32)
    row_inverse = lax.rsqrt(lax.optimization_barrier(jnp.mean(tok_f32 * tok_f32, axis=-1, keepdims=True)) + EPS)
    normed = (tok_f32 * row_inverse * norm_gain).astype(jnp.bfloat16)
    projected = jnp.dot(normed.reshape(-1, C), qkv_weight, preferred_element_type=jnp.float32)
    projected = projected.reshape(GR, GC, 3, HEADS, HEAD)
    query_raw = projected[:, :, 0]
    key_raw = projected[:, :, 1]
    value_raw = projected[:, :, 2]
    factor = (head_scale / HEAD)[:, None]
    query_inverse = lax.rsqrt(lax.optimization_barrier(jnp.mean(query_raw * query_raw, axis=-1, keepdims=True)) + EPS)
    key_inverse = lax.rsqrt(lax.optimization_barrier(jnp.mean(key_raw * key_raw, axis=-1, keepdims=True)) + EPS)
    query_heads = (query_raw * query_inverse * factor).astype(jnp.bfloat16)
    key_heads = (key_raw * key_inverse).astype(jnp.bfloat16)
    value_heads = value_raw.astype(jnp.bfloat16)
    grad_att = jnp.dot(cotangent.reshape(-1, C), out_weight.T, preferred_element_type=jnp.float32)
    grad_att = grad_att.astype(jnp.bfloat16).reshape(GR, GC, HEADS, HEAD)
    widths = ((WIN, WIN), (WIN, WIN), (0, 0), (0, 0))
    key_pad = jnp.pad(key_heads.astype(jnp.float32), widths)
    value_pad = jnp.pad(value_heads.astype(jnp.float32), widths)
    valid_pad = jnp.pad(jnp.ones((GR, GC), jnp.float32), WIN)
    query_f = query_heads.astype(jnp.float32)
    grad_f = grad_att.astype(jnp.float32)
    offsets = [(row_off, col_off) for row_off in range(2 * WIN + 1) for col_off in range(2 * WIN + 1)]
    scores = jnp.stack([lax.optimization_barrier(jnp.sum(query_f * window(key_pad, ro, co), axis=-1)) for ro, co in offsets])
    allowed = jnp.stack([window(valid_pad, ro, co) for ro, co in offsets])[..., None]
    exp_scores = jnp.exp(scores) * allowed
    denom_sum = lax.optimization_barrier(jnp.sum(exp_scores, axis=0))
    attend = exp_scores / denom_sum
    attend_b = lax.optimization_barrier(attend.astype(jnp.bfloat16)).astype(jnp.float32)
    attended = jnp.zeros((GR, GC, HEADS, HEAD), jnp.float32)
    for index, (ro, co) in enumerate(offsets):
        attended = attended + attend_b[index][..., None] * window(value_pad, ro, co)
    attended = attended.astype(jnp.bfloat16)
    output = (tok_f32 + jnp.dot(attended.reshape(-1, C), out_weight, preferred_element_type=jnp.float32).reshape(GR, GC, C)).astype(jnp.bfloat16)
    grad_probs = jnp.stack([lax.optimization_barrier(jnp.sum(grad_f * window(value_pad, ro, co), axis=-1)) for ro, co in offsets])
    delta_sum = lax.optimization_barrier(jnp.sum(attend * grad_probs, axis=0))
    grad_scores = lax.optimization_barrier((attend * (grad_probs - delta_sum)).astype(jnp.bfloat16)).astype(jnp.float32)
    grad_query = jnp.zeros((GR, GC, HEADS, HEAD), jnp.float32)
    key_grad_pad = jnp.zeros((GR + 2 * WIN, GC + 2 * WIN, HEADS, HEAD), jnp.float32)
    value_grad_pad = jnp.zeros((GR + 2 * WIN, GC + 2 * WIN, HEADS, HEAD), jnp.float32)
    for index, (ro, co) in enumerate(offsets):
        grad_query = grad_query + grad_scores[index][..., None] * window(key_pad, ro, co)
        key_grad_pad = key_grad_pad.at[ro:ro + GR, co:co + GC].add(grad_scores[index][..., None] * query_f)
        value_grad_pad = value_grad_pad.at[ro:ro + GR, co:co + GC].add(attend_b[index][..., None] * grad_f)
    grad_keys = key_grad_pad[WIN:WIN + GR, WIN:WIN + GC]
    grad_values = value_grad_pad[WIN:WIN + GR, WIN:WIN + GC]
    grad_q = factor * query_inverse * grad_query - factor * query_inverse ** 3 * query_raw * lax.optimization_barrier(jnp.mean(grad_query * query_raw, axis=-1, keepdims=True))
    grad_k = key_inverse * grad_keys - key_inverse ** 3 * key_raw * lax.optimization_barrier(jnp.mean(grad_keys * key_raw, axis=-1, keepdims=True))
    scale_sum = lax.optimization_barrier(jnp.sum(grad_query * query_raw * query_inverse, axis=(0, 1, 3))) / HEAD
    grad_proj = jnp.stack([grad_q, grad_k, grad_values], axis=2).reshape(-1, 3 * C).astype(jnp.bfloat16)
    qkv_sum = jnp.dot(normed.reshape(-1, C).T, grad_proj, preferred_element_type=jnp.float32)
    out_sum = jnp.dot(attended.reshape(-1, C).T, cotangent.reshape(-1, C), preferred_element_type=jnp.float32)
    grad_normed = jnp.dot(grad_proj, qkv_weight.T, preferred_element_type=jnp.float32).reshape(GR, GC, C)
    gain_sum = lax.optimization_barrier(jnp.sum(grad_normed * tok_f32 * row_inverse, axis=(0, 1)))
    scaled = norm_gain * grad_normed
    token_grad = cotangent.astype(jnp.float32) + row_inverse * scaled - row_inverse ** 3 * tok_f32 * lax.optimization_barrier(jnp.mean(scaled * tok_f32, axis=-1, keepdims=True))
    norm_factor = 1.0 / math.sqrt(TOKENS)
    return (output, token_grad, gain_sum * norm_factor, qkv_sum * norm_factor, scale_sum * norm_factor, out_sum * norm_factor)
```

```python
import math

import jax
import jax.numpy as jnp
from jax import lax
from jax.experimental import pallas as pl
from jax.experimental.pallas import tpu as pltpu
from jax.sharding import Mesh, PartitionSpec as P

HEADS = 4
HEAD = 64
C = 256
WIN = 3
BR = 4
BC = 128
GRID = 512

EPS = 1e-06

PAD = 8
ER = BR + 2 * WIN
EC = BC + 2 * PAD
QC = 32
KC = 48
BLOCKS = BC // QC
NQ = BR * QC
NK = ER * KC
PAIRS = HEADS // 2
LANES = 2 * HEAD

AXES = ("z", "xh", "y", "xl", "core")
AXIS_SIZES = (8, 2, 8, 2, 2)
ROWS = ("z", "xh", "y")
GRP = ("xl", "core")
SPLIT = ("z", "y")
REST = ("xh", "xl", "core")
PARTS = 64
PART = 4 * C // PARTS
EXTRA = 16
PART_ROWS = 2 * PART + EXTRA

F32 = jnp.float32
BF16 = jnp.bfloat16


def mm(a, b, dims=((1,), (0,))):
    return lax.dot_general(a, b, (dims, ((), ())), preferred_element_type=F32)


def split_bf16(a):
    high = a.astype(BF16)
    return high, (a - high.astype(F32)).astype(BF16)


def row_stats(t):
    n = lax.rsqrt(jnp.mean(t * t, axis=-1, keepdims=True) + EPS)
    return n, t * n


def norm_grad(u, n, hat):
    return n * (u - hat * jnp.mean(u * hat, axis=-1, keepdims=True))


def kernel(
    place,
    up,
    own,
    down,
    left,
    right,
    cot,
    gain_ref,
    factor_ref,
    wqkv,
    wo,
    out,
    grad_own,
    grad_up,
    grad_down,
    grad_left,
    grad_right,
    sums,
    ext,
    normed_ext,
    k_hat,
    k_inv,
    k_b,
    v_b,
    gk,
    gv,
    normed_own,
    q_hat,
    q_inv,
    q_b,
    d_b,
    att_b,
    gq,
    acc_q,
    acc_kv,
    acc_out,
    acc_row,
    head_mean,
    base,
):
    gain = gain_ref[...]
    factor = factor_ref[...]

    lane_head = lax.broadcasted_iota(jnp.int32, (C, C), 1) // HEAD
    row_head = lax.broadcasted_iota(jnp.int32, (C, C), 0) // HEAD
    head_mean[...] = jnp.where(lane_head == row_head, 1.0 / HEAD, 0.0).astype(BF16)

    def per_head_mean(a):
        high, low = split_bf16(a)
        return mm(high, head_mean[...]) + mm(low, head_mean[...])

    own_cols = slice(PAD, PAD + BC)
    ext[0:WIN, own_cols] = up[...].astype(F32)
    ext[WIN : WIN + BR, own_cols] = own[...].astype(F32)
    ext[WIN + BR : ER, own_cols] = down[...].astype(F32)
    ext[:, 0:PAD] = left[...].astype(F32)
    ext[:, PAD + BC : EC] = right[...].astype(F32)

    gk[...] = jnp.zeros_like(gk)
    gv[...] = jnp.zeros_like(gv)
    acc_q[...] = jnp.zeros_like(acc_q)
    acc_kv[...] = jnp.zeros_like(acc_kv)
    acc_out[...] = jnp.zeros_like(acc_out)
    acc_row[...] = jnp.zeros_like(acc_row)

    @pl.loop(0, ER // 2)
    def _(i):
        rows = pl.ds(2 * i, 2)
        shape = (2, EC, C)
        _, hat = row_stats(ext[rows].reshape(2 * EC, C))
        normed = (hat * gain).astype(BF16)
        normed_ext[rows] = normed.reshape(shape)
        kv = mm(normed, wqkv[:, C:])
        k = kv[:, :C]
        inv = lax.rsqrt(per_head_mean(k * k) + EPS)
        hat_k = k * inv
        k_hat[rows] = hat_k.reshape(shape)
        k_inv[rows] = inv.reshape(shape)
        k_b[rows] = hat_k.astype(BF16).reshape(shape)
        v_b[rows] = kv[:, C:].astype(BF16).reshape(shape)

    @pl.loop(0, BR // 2)
    def _(i):
        rows = pl.ds(2 * i, 2)
        shape = (2, BC, C)
        _, hat = row_stats(own[rows].reshape(2 * BC, C).astype(F32))
        normed = (hat * gain).astype(BF16)
        normed_own[rows] = normed.reshape(shape)
        q = mm(normed, wqkv[:, :C])
        inv = lax.rsqrt(per_head_mean(q * q) + EPS)
        hat_q = q * inv
        q_hat[rows] = hat_q.reshape(shape)
        q_inv[rows] = inv.reshape(shape)
        q_b[rows] = (hat_q * factor).astype(BF16).reshape(shape)
        d = mm(cot[rows].reshape(2 * BC, C), wo[...], ((1,), (1,)))
        d_b[rows] = d.astype(BF16).reshape(shape)

    key_row = lax.broadcasted_iota(jnp.int32, (ER, KC, NQ), 0)
    key_col = lax.broadcasted_iota(jnp.int32, (ER, KC, NQ), 1)
    query = lax.broadcasted_iota(jnp.int32, (ER, KC, NQ), 2)
    row_gap = key_row - query // QC
    col_gap = key_col - query % QC - (PAD - WIN)
    in_rows = (key_row + place[0] - WIN >= 0) & (key_row + place[0] - WIN < GRID)
    near = (row_gap >= 0) & (row_gap <= 2 * WIN) & (col_gap >= 0) & (col_gap <= 2 * WIN)
    base[...] = jnp.where(near & in_rows, 1.0, 0.0)

    lane = lax.broadcasted_iota(jnp.int32, (NQ, LANES), 1)
    first = lane < HEAD
    row = lax.broadcasted_iota(jnp.int32, (LANES, NQ), 0)
    top = row < HEAD

    def both(a):
        zero = jnp.zeros_like(a)
        return jnp.concatenate([jnp.where(first, a, zero), jnp.where(first, zero, a)], axis=0)

    def own_head(a):
        return jnp.where(top, a[:, :NQ], a[:, NQ:]).T

    @pl.loop(0, BLOCKS)
    def _(b):
        q_cols = pl.ds(pl.multiple_of(b * QC, QC), QC)
        k_cols = pl.ds(pl.multiple_of(b * QC, QC), KC)
        col = lax.broadcasted_iota(jnp.int32, (ER, KC, NQ), 1) + (place[1] - PAD + b * QC)
        mask = jnp.where((col >= 0) & (col < GRID), base[...], 0.0).reshape(NK, NQ)
        mask = jnp.concatenate([mask, mask], axis=1)
        for p in range(PAIRS):
            lanes = slice(p * LANES, (p + 1) * LANES)
            k2 = k_b[:, k_cols, lanes].reshape(NK, LANES)
            v2 = v_b[:, k_cols, lanes].reshape(NK, LANES)
            q2 = both(q_b[:, q_cols, lanes].reshape(NQ, LANES))
            d2 = both(d_b[:, q_cols, lanes].reshape(NQ, LANES))
            e = jnp.exp(mm(k2, q2, ((1,), (1,)))) * mask
            attend = e * (1.0 / jnp.sum(e, axis=0, keepdims=True))
            attend_b = attend.astype(BF16)
            grad_probs = mm(v2, d2, ((1,), (1,)))
            delta = jnp.sum(attend * grad_probs, axis=0, keepdims=True)
            grad_scores = (attend * (grad_probs - delta)).astype(BF16)
            attended = own_head(mm(v2, attend_b, ((0,), (0,))))
            att_b[:, q_cols, lanes] = attended.astype(BF16).reshape(BR, QC, LANES)
            grad_query = own_head(mm(k2, grad_scores, ((0,), (0,))))
            gq[:, q_cols, lanes] = grad_query.reshape(BR, QC, LANES)
            gk[:, k_cols, lanes] += mm(grad_scores, q2).reshape(ER, KC, LANES)
            gv[:, k_cols, lanes] += mm(attend_b, d2).reshape(ER, KC, LANES)

    @pl.loop(0, BR // 2)
    def _(i):
        rows = pl.ds(2 * i, 2)
        shape = (2, BC, C)
        grad_query = gq[rows].reshape(2 * BC, C)
        hat_q = q_hat[rows].reshape(2 * BC, C)
        mean = per_head_mean(grad_query * hat_q)
        inv = q_inv[rows].reshape(2 * BC, C)
        g = (factor * inv * (grad_query - hat_q * mean)).astype(BF16)
        acc_row[0:1] += jnp.sum(mean, axis=0, keepdims=True)
        cot_b = cot[rows].reshape(2 * BC, C)
        att = att_b[rows].reshape(2 * BC, C)
        tok = own[rows].reshape(2 * BC, C).astype(F32)
        out[rows] = (tok + mm(att, wo[...])).astype(BF16).reshape(shape)
        acc_out[...] += mm(att, cot_b, ((0,), (0,)))
        acc_q[...] += mm(normed_own[rows].reshape(2 * BC, C), g, ((0,), (0,)))
        grad_normed = mm(g, wqkv[:, :C], ((1,), (1,)))
        n, hat = row_stats(tok)
        acc_row[1:2] += jnp.sum(grad_normed * hat, axis=0, keepdims=True)
        grad = cot_b.astype(F32) + norm_grad(gain * grad_normed, n, hat)
        grad_own[rows] = grad.reshape(shape)

    @pl.loop(0, ER // 2)
    def _(i):
        rows = pl.ds(2 * i, 2)
        grad_key = gk[rows].reshape(2 * EC, C)
        hat_k = k_hat[rows].reshape(2 * EC, C)
        mean = per_head_mean(grad_key * hat_k)
        g_k = k_inv[rows].reshape(2 * EC, C) * (grad_key - hat_k * mean)
        g = jnp.concatenate([g_k, gv[rows].reshape(2 * EC, C)], axis=1).astype(BF16)
        acc_kv[...] += mm(normed_ext[rows].reshape(2 * EC, C), g, ((0,), (0,)))
        grad_normed = mm(g, wqkv[:, C:], ((1,), (1,)))
        n, hat = row_stats(ext[rows].reshape(2 * EC, C))
        acc_row[1:2] += jnp.sum(grad_normed * hat, axis=0, keepdims=True)
        ext[rows] = norm_grad(gain * grad_normed, n, hat).reshape(2, EC, C)

    grad_own[...] += ext[WIN : WIN + BR, own_cols]
    grad_up[...] = ext[0:WIN].astype(BF16)
    grad_down[...] = ext[WIN + BR : ER].astype(BF16)
    grad_left[...] = ext[WIN : WIN + BR, 0:PAD]
    grad_right[...] = ext[WIN : WIN + BR, PAD + BC : EC]

    scale_high, scale_low = split_bf16(acc_row[0:1])
    gain_high, gain_low = split_bf16(acc_row[1:2])
    small = jnp.concatenate(
        [a.astype(F32)[:, h * 128 : h * 128 + 128] for a in (scale_high, scale_low, gain_high, gain_low) for h in (0, 1)]
        + [jnp.zeros((EXTRA - 8, 128), F32)],
        axis=0,
    ).astype(BF16)
    blocks = (acc_q, acc_kv, acc_kv, acc_out)
    offsets = (0, 0, C, 0)
    for part in range(PARTS):
        block, start = divmod(part * PART, C)
        ref, at = blocks[block], offsets[block]
        for h in (0, 1):
            piece = ref[start : start + PART, at + h * 128 : at + h * 128 + 128]
            sums[part, h * PART : h * PART + PART] = piece.astype(BF16)
        sums[part, 2 * PART :] = small


def run_kernel(place, up, own, down, left, right, cot, gain, factor, wqkv, wo):
    vmem = pl.BlockSpec(memory_space=pltpu.VMEM)
    shape = jax.ShapeDtypeStruct
    out_shape = (
        shape((BR, BC, C), BF16),
        shape((BR, BC, C), F32),
        shape((WIN, EC, C), BF16),
        shape((WIN, EC, C), BF16),
        shape((BR, PAD, C), F32),
        shape((BR, PAD, C), F32),
        shape((PARTS, PART_ROWS, 128), BF16),
    )
    ext_f, ext_b = pltpu.VMEM((ER, EC, C), F32), pltpu.VMEM((ER, EC, C), BF16)
    own_f, own_b = pltpu.VMEM((BR, BC, C), F32), pltpu.VMEM((BR, BC, C), BF16)
    scratch = [ext_f, ext_b, ext_f, ext_f, ext_b, ext_b, ext_f, ext_f]
    scratch += [own_b, own_f, own_f, own_b, own_b, own_b, own_f]
    scratch += [pltpu.VMEM((C, C), F32), pltpu.VMEM((C, 2 * C), F32), pltpu.VMEM((C, C), F32)]
    scratch += [pltpu.VMEM((8, C), F32), pltpu.VMEM((C, C), BF16), pltpu.VMEM((ER, KC, NQ), F32)]
    return pl.pallas_call(
        kernel,
        out_shape=out_shape,
        in_specs=[pl.BlockSpec(memory_space=pltpu.SMEM)] + [vmem] * 10,
        out_specs=[vmem] * 7,
        scratch_shapes=scratch,
        compiler_params=pltpu.CompilerParams(vmem_limit_bytes=40 * 1024 * 1024),
        cost_estimate=pl.CostEstimate(flops=6_000_000_000, bytes_accessed=6_000_000, transcendentals=1_000_000),
    )(place, up, own, down, left, right, cot, gain, factor, wqkv, wo)


def exchange(last, first, axes):
    size = math.prod(AXIS_SIZES[AXES.index(a)] for a in axes)
    forward = [(i, i + 1) for i in range(size - 1)]
    backward = [(i + 1, i) for i in range(size - 1)]
    return lax.ppermute(last, axes, forward), lax.ppermute(first, axes, backward)


def to_all(x, axes, size):
    return lax.all_to_all(jnp.broadcast_to(x[None], (size,) + x.shape), axes, 0, 0)


def reduce_sums(sums):
    part = jnp.sum(lax.all_to_all(sums, SPLIT, 0, 0).astype(F32), axis=0).astype(BF16)
    rest = 512 // PARTS
    part = jnp.sum(to_all(part, REST, rest).astype(F32), axis=0)
    small = part[2 * PART :]
    whole = to_all(part[: 2 * PART].astype(BF16), SPLIT, PARTS)
    whole = whole.reshape(4, C // PART, 2, PART, 128).transpose(0, 1, 3, 2, 4).reshape(4, C, C)
    return whole.astype(F32), small


def body(tokens, norm_gain, qkv_weight, head_scale, out_weight, cotangent):
    place = jnp.stack([lax.axis_index(ROWS) * BR, lax.axis_index(GRP) * BC]).astype(jnp.int32)
    up, down = exchange(tokens[BR - WIN :], tokens[:WIN], ROWS)
    last_cols = jnp.concatenate([a[:, BC - PAD :] for a in (up, tokens, down)], axis=0)
    first_cols = jnp.concatenate([a[:, :PAD] for a in (up, tokens, down)], axis=0)
    left, right = exchange(last_cols, first_cols, GRP)
    factor = jnp.repeat(head_scale / HEAD, HEAD)[None]
    out, grad_own, grad_up, grad_down, grad_left, grad_right, sums = run_kernel(
        place, up, tokens, down, left, right, cotangent, norm_gain[None], factor, qkv_weight, out_weight
    )
    from_up, from_down = exchange(grad_down, grad_up, ROWS)
    from_up = jnp.pad(from_up.astype(F32), ((0, BR - WIN), (0, 0), (0, 0)))
    from_down = jnp.pad(from_down.astype(F32), ((BR - WIN, 0), (0, 0), (0, 0)))
    rows_back = from_up + from_down
    from_left, from_right = exchange(
        (grad_right + rows_back[:, PAD + BC :]).astype(BF16),
        (grad_left + rows_back[:, :PAD]).astype(BF16),
        GRP,
    )
    token_grad = (
        grad_own
        + rows_back[:, PAD : PAD + BC]
        + jnp.pad(from_left.astype(F32), ((0, 0), (0, BC - PAD), (0, 0)))
        + jnp.pad(from_right.astype(F32), ((0, 0), (BC - PAD, 0), (0, 0)))
    )
    whole, small = reduce_sums(sums)
    norm_factor = 1.0 / GRID
    qkv_grad = jnp.concatenate([whole[0], whole[1], whole[2]], axis=1) * norm_factor
    small = small[:8].reshape(2, 2, C).sum(axis=1) * norm_factor
    scale_grad = small[0].reshape(HEADS, HEAD)[:, 0]
    return out, token_grad, small[1], qkv_grad, scale_grad, whole[3] * norm_factor


def solution(mesh):
    fine = Mesh(mesh.devices.reshape(AXIS_SIZES), AXES)
    tiles = P(ROWS, GRP, None)
    return jax.shard_map(
        body,
        mesh=fine,
        in_specs=(tiles, P(), P(), P(), P(), tiles),
        out_specs=(tiles, tiles, P(), P(), P(), P()),
        check_vma=False,
    )
```

```python
import math

import jax
import jax.numpy as jnp
from jax import lax
from jax.experimental import pallas as pl
from jax.experimental.pallas import tpu as pltpu
from jax.sharding import Mesh, PartitionSpec as P

HEADS = 4
HEAD = 64
C = 256
WIN = 3
BR = 4
BC = 128
GRID = 512

EPS = 1e-06

PAD = 8
ER = BR + 2 * WIN
EC = BC + 2 * PAD
QC = 32
KC = 48
BLOCKS = BC // QC
NQ = BR * QC
NK = ER * KC
PAIRS = HEADS // 2
LANES = 2 * HEAD

AXES = ("z", "xh", "y", "xl", "core")
AXIS_SIZES = (8, 2, 8, 2, 2)
ROWS = ("z", "xh", "y")
GRP = ("xl", "core")
SPLIT = ("z", "y")
REST = ("xh", "xl", "core")
PARTS = 64
PART = 4 * C // PARTS
EXTRA = 16
PART_ROWS = 2 * PART + EXTRA

F32 = jnp.float32
BF16 = jnp.bfloat16


def mm(a, b, dims=((1,), (0,))):
    return lax.dot_general(a, b, (dims, ((), ())), preferred_element_type=F32)


def split_bf16(a):
    high = a.astype(BF16)
    return high, (a - high.astype(F32)).astype(BF16)


def row_stats(t):
    n = lax.rsqrt(jnp.mean(t * t, axis=-1, keepdims=True) + EPS)
    return n, t * n


def norm_grad(u, n, hat):
    return n * (u - hat * jnp.mean(u * hat, axis=-1, keepdims=True))


def ones_per_head():
    lane_head = lax.broadcasted_iota(jnp.int32, (C, C), 1) // HEAD
    row_head = lax.broadcasted_iota(jnp.int32, (C, C), 0) // HEAD
    return jnp.where(lane_head == row_head, 1.0 / HEAD, 0.0).astype(BF16)


def per_head_mean(a, ones):
    high, low = split_bf16(a)
    return mm(high, ones) + mm(low, ones)


def normalise(raw, ones):
    inv = lax.rsqrt(per_head_mean(raw * raw, ones) + EPS)
    return raw * inv, inv


def widen(a, rows):
    edge = jnp.zeros((rows, PAD, C), F32)
    return jnp.concatenate([edge, a.reshape(rows, BC, C), edge], axis=1).astype(BF16)


def own_kernel(own, cot, gain, factor, wqkv, wo, q_b, d_b, normed_own, q_inv, normed_ext, k_b, v_b, k_inv, ones):
    ones[...] = ones_per_head()

    @pl.loop(0, BR // 2)
    def _(i):
        rows = pl.ds(2 * i, 2)
        shape = (2, BC, C)
        _, hat = row_stats(own[rows].reshape(2 * BC, C).astype(F32))
        scaled = hat * gain[...]
        normed = scaled.astype(BF16)
        projected = mm(normed, wqkv[...])
        q, inv = normalise(projected[:, :C], ones[...])
        k, inv_k = normalise(projected[:, C : 2 * C], ones[...])
        normed_own[rows] = normed.reshape(shape)
        q_inv[rows] = inv.reshape(shape)
        q_b[rows] = (q * factor[...]).astype(BF16).reshape(shape)
        normed_ext[rows] = widen(scaled, 2)
        k_b[rows] = widen(k, 2)
        k_inv[rows] = widen(inv_k, 2)
        v_b[rows] = widen(projected[:, 2 * C :], 2)
        d = mm(cot[rows].reshape(2 * BC, C), wo[...], ((1,), (1,)))
        d_b[rows] = d.astype(BF16).reshape(shape)


def halo_kernel(up, down, gain, wqkv, normed_ext, k_b, v_b, k_inv, ones):
    ones[...] = ones_per_head()
    for half, ref in enumerate((up, down)):
        rows = slice(half * WIN, half * WIN + WIN)
        _, hat = row_stats(ref[...].reshape(WIN * BC, C).astype(F32))
        scaled = hat * gain[...]
        projected = mm(scaled.astype(BF16), wqkv[:, C:])
        k, inv_k = normalise(projected[:, :C], ones[...])
        normed_ext[rows] = widen(scaled, WIN)
        k_b[rows] = widen(k, WIN)
        k_inv[rows] = widen(inv_k, WIN)
        v_b[rows] = widen(projected[:, C:], WIN)


def attention_kernel(
    place,
    left,
    right,
    cot,
    gain,
    factor,
    wqkv,
    q_b,
    d_b,
    normed_own,
    q_inv,
    normed_mid,
    k_mid,
    v_mid,
    k_inv_mid,
    normed_halo,
    k_halo,
    v_halo,
    k_inv_halo,
    sums,
    att_b,
    g_q,
    g_kv,
    normed_ext,
    k_b,
    v_b,
    k_inv,
    gk,
    gv,
    gq,
    acc_q,
    acc_kv,
    acc_out,
    acc_scale,
    ones,
    base,
):
    ones[...] = ones_per_head()

    edges = jnp.concatenate([left[...].astype(F32), right[...].astype(F32)], axis=0)
    _, hat = row_stats(edges.reshape(2 * ER * PAD, C))
    scaled = hat * gain[...]
    projected = mm(scaled.astype(BF16), wqkv[:, C:])
    k, inv_k = normalise(projected[:, :C], ones[...])
    for ext, mid, halo, edge in (
        (normed_ext, normed_mid, normed_halo, scaled),
        (k_b, k_mid, k_halo, k),
        (v_b, v_mid, v_halo, projected[:, C:]),
        (k_inv, k_inv_mid, k_inv_halo, inv_k),
    ):
        edge = edge.reshape(2 * ER, PAD, C)
        ext[0:WIN] = halo[0:WIN]
        ext[WIN : WIN + BR] = mid[...]
        ext[WIN + BR : ER] = halo[WIN : 2 * WIN]
        near = ext[:, 0 : 2 * PAD].astype(F32)[:, PAD:]
        ext[:, 0 : 2 * PAD] = jnp.concatenate([edge[:ER], near], axis=1).astype(BF16)
        near = ext[:, EC - 2 * PAD : EC].astype(F32)[:, :PAD]
        ext[:, EC - 2 * PAD : EC] = jnp.concatenate([near, edge[ER:]], axis=1).astype(BF16)

    gk[...] = jnp.zeros_like(gk)
    gv[...] = jnp.zeros_like(gv)

    key_row = lax.broadcasted_iota(jnp.int32, (ER, KC, NQ), 0)
    key_col = lax.broadcasted_iota(jnp.int32, (ER, KC, NQ), 1)
    query = lax.broadcasted_iota(jnp.int32, (ER, KC, NQ), 2)
    row_gap = key_row - query // QC
    col_gap = key_col - query % QC - (PAD - WIN)
    in_rows = (key_row + place[0] - WIN >= 0) & (key_row + place[0] - WIN < GRID)
    near = (row_gap >= 0) & (row_gap <= 2 * WIN) & (col_gap >= 0) & (col_gap <= 2 * WIN)
    base[...] = jnp.where(near & in_rows, 1.0, 0.0)

    first = lax.broadcasted_iota(jnp.int32, (NQ, LANES), 1) < HEAD
    top = lax.broadcasted_iota(jnp.int32, (LANES, NQ), 0) < HEAD

    def both(a):
        zero = jnp.zeros_like(a)
        return jnp.concatenate([jnp.where(first, a, zero), jnp.where(first, zero, a)], axis=0)

    def own_head(a):
        return jnp.where(top, a[:, :NQ], a[:, NQ:]).T

    @pl.loop(0, BLOCKS)
    def _(b):
        q_cols = pl.ds(pl.multiple_of(b * QC, QC), QC)
        k_cols = pl.ds(pl.multiple_of(b * QC, QC), KC)
        col = lax.broadcasted_iota(jnp.int32, (ER, KC, NQ), 1) + (place[1] - PAD + b * QC)
        mask = jnp.where((col >= 0) & (col < GRID), base[...], 0.0).reshape(NK, NQ)
        mask = jnp.concatenate([mask, mask], axis=1)
        for p in range(PAIRS):
            lanes = slice(p * LANES, (p + 1) * LANES)
            k2 = k_b[:, k_cols, lanes].reshape(NK, LANES)
            v2 = v_b[:, k_cols, lanes].reshape(NK, LANES)
            q2 = both(q_b[:, q_cols, lanes].reshape(NQ, LANES))
            d2 = both(d_b[:, q_cols, lanes].reshape(NQ, LANES))
            e = jnp.exp(mm(k2, q2, ((1,), (1,)))) * mask
            attend = e * (1.0 / jnp.sum(e, axis=0, keepdims=True))
            attend_b = attend.astype(BF16)
            grad_probs = mm(v2, d2, ((1,), (1,)))
            delta = jnp.sum(attend * grad_probs, axis=0, keepdims=True)
            grad_scores = (attend * (grad_probs - delta)).astype(BF16)
            attended = own_head(mm(v2, attend_b, ((0,), (0,))))
            att_b[:, q_cols, lanes] = attended.astype(BF16).reshape(BR, QC, LANES)
            grad_query = own_head(mm(k2, grad_scores, ((0,), (0,))))
            gq[:, q_cols, lanes] = grad_query.reshape(BR, QC, LANES)
            gk[:, k_cols, lanes] += mm(grad_scores, q2).reshape(ER, KC, LANES)
            gv[:, k_cols, lanes] += mm(attend_b, d2).reshape(ER, KC, LANES)

    inv_factor = 1.0 / factor[...]
    grad_query = gq[...].reshape(BR * BC, C)
    q_f = q_b[...].reshape(BR * BC, C).astype(F32)
    mean = per_head_mean(grad_query * q_f, ones[...]) * inv_factor
    acc_scale[...] = jnp.sum(mean, axis=0, keepdims=True)
    g = q_inv[...].reshape(BR * BC, C) * (factor[...] * grad_query - q_f * mean)
    g = g.astype(BF16)
    g_q[...] = g.reshape(BR, BC, C)
    acc_out[...] = mm(att_b[...].reshape(BR * BC, C), cot[...].reshape(BR * BC, C), ((0,), (0,)))
    acc_q[...] = mm(normed_own[...].reshape(BR * BC, C), g, ((0,), (0,)))

    @pl.loop(0, ER // 2)
    def _(i):
        rows = pl.ds(2 * i, 2)
        shape = (2, EC, C)
        grad_key = gk[rows].reshape(2 * EC, C)
        k_f = k_b[rows].reshape(2 * EC, C).astype(F32)
        mean = per_head_mean(grad_key * k_f, ones[...])
        g_k = k_inv[rows].reshape(2 * EC, C).astype(F32) * (grad_key - k_f * mean)
        g_kv[rows, :, :C] = g_k.astype(BF16).reshape(shape)
        g_kv[rows, :, C:] = gv[rows].astype(BF16)

    acc_kv[...] = mm(normed_ext[...].reshape(ER * EC, C), g_kv[...].reshape(ER * EC, 2 * C), ((0,), (0,)))

    by_feature = (
        wqkv[:, :C].astype(F32) * acc_q[...]
        + wqkv[:, C : 2 * C].astype(F32) * acc_kv[:, :C]
        + wqkv[:, 2 * C :].astype(F32) * acc_kv[:, C:]
    )
    high, low = split_bf16(by_feature)
    every = jnp.ones((8, C), BF16)
    gain_sum = mm(every, high, ((1,), (1,))) + mm(every, low, ((1,), (1,)))
    gain_sum = gain_sum[0:1] / gain[...]

    small = [part.astype(F32) for a in (acc_scale[...], gain_sum) for part in split_bf16(a)]
    small = [a[:, h * 128 : h * 128 + 128] for a in small for h in (0, 1)]
    small = jnp.concatenate(small + [jnp.zeros((EXTRA - 8, 128), F32)], axis=0).astype(BF16)
    blocks = (acc_q, acc_kv, acc_kv, acc_out)
    offsets = (0, 0, C, 0)
    for part in range(PARTS):
        block, start = divmod(part * PART, C)
        ref, at = blocks[block], offsets[block]
        for h in (0, 1):
            piece = ref[start : start + PART, at + h * 128 : at + h * 128 + 128]
            sums[part, h * PART : h * PART + PART] = piece.astype(BF16)
        sums[part, 2 * PART :] = small


def token_kernel(
    up,
    own,
    down,
    left,
    right,
    cot,
    gain,
    wqkv,
    wo,
    att_b,
    g_q,
    g_kv,
    out,
    grad_own,
    grad_up,
    grad_down,
    grad_left,
    grad_right,
    ext,
):
    own_cols = slice(PAD, PAD + BC)
    ext[0:WIN, own_cols] = up[...].astype(F32)
    ext[WIN : WIN + BR, own_cols] = own[...].astype(F32)
    ext[WIN + BR : ER, own_cols] = down[...].astype(F32)
    ext[:, 0:PAD] = left[...].astype(F32)
    ext[:, PAD + BC : EC] = right[...].astype(F32)

    @pl.loop(0, ER // 2)
    def _(i):
        rows = pl.ds(2 * i, 2)
        grad_normed = mm(g_kv[rows].reshape(2 * EC, 2 * C), wqkv[:, C:], ((1,), (1,)))
        n, hat = row_stats(ext[rows].reshape(2 * EC, C))
        ext[rows] = norm_grad(gain[...] * grad_normed, n, hat).reshape(2, EC, C)

    grad_up[...] = ext[0:WIN].astype(BF16)
    grad_down[...] = ext[WIN + BR : ER].astype(BF16)
    grad_left[...] = ext[WIN : WIN + BR, 0:PAD]
    grad_right[...] = ext[WIN : WIN + BR, PAD + BC : EC]

    @pl.loop(0, BR // 2)
    def _(i):
        rows = pl.ds(2 * i, 2)
        shape = (2, BC, C)
        tok = own[rows].reshape(2 * BC, C).astype(F32)
        att = att_b[rows].reshape(2 * BC, C)
        out[rows] = (tok + mm(att, wo[...])).astype(BF16).reshape(shape)
        grad_normed = mm(g_q[rows].reshape(2 * BC, C), wqkv[:, :C], ((1,), (1,)))
        n, hat = row_stats(tok)
        grad = cot[rows].reshape(2 * BC, C).astype(F32) + norm_grad(gain[...] * grad_normed, n, hat)
        grad_own[rows] = grad.reshape(shape) + ext[pl.ds(WIN + 2 * i, 2), own_cols]


def call(fn, out_shape, scratch, megabytes, microseconds, *args):
    vmem = pl.BlockSpec(memory_space=pltpu.VMEM)
    smem = pl.BlockSpec(memory_space=pltpu.SMEM)
    return pl.pallas_call(
        fn,
        out_shape=tuple(jax.ShapeDtypeStruct(s, d) for s, d in out_shape),
        in_specs=[smem if a.dtype == jnp.int32 else vmem for a in args],
        out_specs=tuple(vmem for _ in out_shape),
        scratch_shapes=[pltpu.VMEM(s, d) for s, d in scratch],
        compiler_params=pltpu.CompilerParams(vmem_limit_bytes=megabytes * 1024 * 1024),
        cost_estimate=pl.CostEstimate(flops=microseconds * 1_000_000_000, bytes_accessed=1_000_000, transcendentals=0),
    )(*args)


OWN = (BR, BC, C)
EXT = (ER, EC, C)
ONES = ((C, C), BF16)


def run_own(tokens, cotangent, gain, factor, wqkv, wo):
    mid = ((BR, EC, C), BF16)
    outs = [(OWN, BF16), (OWN, BF16), (OWN, BF16), (OWN, F32), mid, mid, mid, mid]
    return call(own_kernel, outs, [ONES], 12, 3, tokens, cotangent, gain, factor, wqkv, wo)


def run_halo(up, down, gain, wqkv):
    halo = ((2 * WIN, EC, C), BF16)
    return call(halo_kernel, [halo] * 4, [ONES], 12, 3, up, down, gain, wqkv)


def run_attention(place, left, right, cot, gain, factor, wqkv, own, halo):
    outs = [((PARTS, PART_ROWS, 128), BF16), (OWN, BF16), (OWN, BF16), ((ER, EC, 2 * C), BF16)]
    scratch = [(EXT, BF16)] * 4 + [(EXT, F32)] * 2 + [(OWN, F32)]
    scratch += [((C, C), F32), ((C, 2 * C), F32), ((C, C), F32), ((1, C), F32), ONES, ((ER, KC, NQ), F32)]
    return call(attention_kernel, outs, scratch, 28, 9, place, left, right, cot, gain, factor, wqkv, *own, *halo)


def run_tokens(up, own, down, left, right, cot, gain, wqkv, wo, att_b, g_q, g_kv):
    halo = ((WIN, EC, C), BF16)
    edge = ((BR, PAD, C), F32)
    outs = [(OWN, BF16), (OWN, F32), halo, halo, edge, edge]
    return call(token_kernel, outs, [(EXT, F32)], 16, 4, up, own, down, left, right, cot, gain, wqkv, wo, att_b, g_q, g_kv)


def exchange(last, first, axes):
    size = math.prod(AXIS_SIZES[AXES.index(a)] for a in axes)
    forward = [(i, i + 1) for i in range(size - 1)]
    backward = [(i + 1, i) for i in range(size - 1)]
    return lax.ppermute(last, axes, forward), lax.ppermute(first, axes, backward)


def to_all(x, axes, size):
    return lax.all_to_all(jnp.broadcast_to(x[None], (size,) + x.shape), axes, 0, 0)


def reduce_sums(sums):
    part = jnp.sum(lax.all_to_all(sums, SPLIT, 0, 0).astype(F32), axis=0).astype(BF16)
    rest = 512 // PARTS
    part = jnp.sum(to_all(part, REST, rest).astype(F32), axis=0)
    small = part[2 * PART :]
    whole = to_all(part[: 2 * PART].astype(BF16), SPLIT, PARTS)
    whole = whole.reshape(4, C // PART, 2, PART, 128).transpose(0, 1, 3, 2, 4).reshape(4, C, C)
    return whole.astype(F32), small


def body(tokens, norm_gain, qkv_weight, head_scale, out_weight, cotangent):
    place = jnp.stack([lax.axis_index(ROWS) * BR, lax.axis_index(GRP) * BC]).astype(jnp.int32)
    gain = norm_gain[None]
    factor = jnp.repeat(head_scale / HEAD, HEAD)[None]
    up, down = exchange(tokens[BR - WIN :], tokens[:WIN], ROWS)
    own = run_own(tokens, cotangent, gain, factor, qkv_weight, out_weight)
    last_cols = jnp.concatenate([a[:, BC - PAD :] for a in (up, tokens, down)], axis=0)
    first_cols = jnp.concatenate([a[:, :PAD] for a in (up, tokens, down)], axis=0)
    left, right = exchange(last_cols, first_cols, GRP)
    halo = run_halo(up, down, gain, qkv_weight)
    sums, att_b, g_q, g_kv = run_attention(place, left, right, cotangent, gain, factor, qkv_weight, own, halo)
    out, grad_own, grad_up, grad_down, grad_left, grad_right = run_tokens(
        up, tokens, down, left, right, cotangent, gain, qkv_weight, out_weight, att_b, g_q, g_kv
    )
    from_up, from_down = exchange(grad_down, grad_up, ROWS)
    from_up = jnp.pad(from_up.astype(F32), ((0, BR - WIN), (0, 0), (0, 0)))
    from_down = jnp.pad(from_down.astype(F32), ((BR - WIN, 0), (0, 0), (0, 0)))
    rows_back = from_up + from_down
    from_left, from_right = exchange(
        (grad_right + rows_back[:, PAD + BC :]).astype(BF16),
        (grad_left + rows_back[:, :PAD]).astype(BF16),
        GRP,
    )
    token_grad = (
        grad_own
        + rows_back[:, PAD : PAD + BC]
        + jnp.pad(from_left.astype(F32), ((0, 0), (0, BC - PAD), (0, 0)))
        + jnp.pad(from_right.astype(F32), ((0, 0), (BC - PAD, 0), (0, 0)))
    )
    whole, small = reduce_sums(sums)
    norm_factor = 1.0 / GRID
    qkv_grad = jnp.concatenate([whole[0], whole[1], whole[2]], axis=1) * norm_factor
    small = small[:8].reshape(2, 2, C).sum(axis=1) * norm_factor
    scale_grad = small[0].reshape(HEADS, HEAD)[:, 0]
    return out, token_grad, small[1], qkv_grad, scale_grad, whole[3] * norm_factor


def solution(mesh):
    fine = Mesh(mesh.devices.reshape(AXIS_SIZES), AXES)
    tiles = P(ROWS, GRP, None)
    return jax.shard_map(
        body,
        mesh=fine,
        in_specs=(tiles, P(), P(), P(), P(), tiles),
        out_specs=(tiles, tiles, P(), P(), P(), P()),
        check_vma=False,
    )
```

```python
import math

import jax
import jax.numpy as jnp
from jax import lax
from jax.experimental import pallas as pl
from jax.experimental.pallas import tpu as pltpu
from jax.sharding import Mesh, PartitionSpec as P

HEADS = 4
HEAD = 64
C = 256
WIN = 3
BR = 4
BC = 128
GRID = 512

EPS = 1e-06

PAD = 8
ER = BR + 2 * WIN
EC = BC + 2 * PAD
QC = 32
KC = 48
BLOCKS = BC // QC
NQ = BR * QC
NK = ER * KC
PAIRS = HEADS // 2
LANES = 2 * HEAD

AXES = ("z", "xh", "y", "xl", "core")
AXIS_SIZES = (8, 2, 8, 2, 2)
ROWS = ("z", "xh", "y")
GRP = ("xl", "core")
SPLIT = ("z", "xh", "xl")
REST = ("y",)
PARTS = 32
RESTS = 8
HALF = 2 * C
PART = HALF // PARTS
EXTRA = 8

F32 = jnp.float32
BF16 = jnp.bfloat16


def mm(a, b, dims=((1,), (0,))):
    return lax.dot_general(a, b, (dims, ((), ())), preferred_element_type=F32)


def split_bf16(a):
    high = a.astype(BF16)
    return high, (a - high.astype(F32)).astype(BF16)


def row_stats(t):
    n = lax.rsqrt(jnp.mean(t * t, axis=-1, keepdims=True) + EPS)
    return n, t * n


def norm_grad(u, n, hat):
    return n * (u - hat * jnp.mean(u * hat, axis=-1, keepdims=True))


def ones_per_head():
    lane_head = lax.broadcasted_iota(jnp.int32, (C, C), 1) // HEAD
    row_head = lax.broadcasted_iota(jnp.int32, (C, C), 0) // HEAD
    return jnp.where(lane_head == row_head, 1.0 / HEAD, 0.0).astype(BF16)


def per_head_mean(a, ones):
    high, low = split_bf16(a)
    return mm(high, ones) + mm(low, ones)


def normalise(raw, ones):
    inv = lax.rsqrt(per_head_mean(raw * raw, ones) + EPS)
    return raw * inv, inv


def widen(a, rows):
    edge = jnp.zeros((rows, PAD, C), F32)
    return jnp.concatenate([edge, a.reshape(rows, BC, C), edge], axis=1).astype(BF16)


def own_kernel(own, cot, gain, factor, wqkv, wo, q_b, d_b, normed_own, q_inv, normed_ext, k_b, v_b, k_inv, ones):
    ones[...] = ones_per_head()

    @pl.loop(0, BR // 2)
    def _(i):
        rows = pl.ds(2 * i, 2)
        shape = (2, BC, C)
        _, hat = row_stats(own[rows].reshape(2 * BC, C).astype(F32))
        scaled = hat * gain[...]
        normed = scaled.astype(BF16)
        projected = mm(normed, wqkv[...])
        q, inv = normalise(projected[:, :C], ones[...])
        k, inv_k = normalise(projected[:, C : 2 * C], ones[...])
        normed_own[rows] = normed.reshape(shape)
        q_inv[rows] = inv.reshape(shape)
        q_b[rows] = (q * factor[...]).astype(BF16).reshape(shape)
        normed_ext[rows] = widen(scaled, 2)
        k_b[rows] = widen(k, 2)
        k_inv[rows] = widen(inv_k, 2)
        v_b[rows] = widen(projected[:, 2 * C :], 2)
        d = mm(cot[rows].reshape(2 * BC, C), wo[...], ((1,), (1,)))
        d_b[rows] = d.astype(BF16).reshape(shape)


def halo_kernel(up, down, gain, wqkv, normed_ext, k_b, v_b, k_inv, ones):
    ones[...] = ones_per_head()
    for half, ref in enumerate((up, down)):
        rows = slice(half * WIN, half * WIN + WIN)
        _, hat = row_stats(ref[...].reshape(WIN * BC, C).astype(F32))
        scaled = hat * gain[...]
        projected = mm(scaled.astype(BF16), wqkv[:, C:])
        k, inv_k = normalise(projected[:, :C], ones[...])
        normed_ext[rows] = widen(scaled, WIN)
        k_b[rows] = widen(k, WIN)
        k_inv[rows] = widen(inv_k, WIN)
        v_b[rows] = widen(projected[:, C:], WIN)


def attention_kernel(
    place,
    left,
    right,
    cot,
    gain,
    factor,
    wqkv,
    q_b,
    d_b,
    normed_own,
    q_inv,
    normed_mid,
    k_mid,
    v_mid,
    k_inv_mid,
    normed_halo,
    k_halo,
    v_halo,
    k_inv_halo,
    keep,
    send,
    att_b,
    g_q,
    g_kv_out,
    normed_ext,
    k_b,
    v_b,
    k_inv,
    gk,
    gv,
    gq,
    g_kv,
    acc,
    ones,
    base,
    copied,
):
    ones[...] = ones_per_head()

    edges = jnp.concatenate([left[...].astype(F32), right[...].astype(F32)], axis=0)
    _, hat = row_stats(edges.reshape(2 * ER * PAD, C))
    scaled = hat * gain[...]
    projected = mm(scaled.astype(BF16), wqkv[:, C:])
    k, inv_k = normalise(projected[:, :C], ones[...])
    for ext, mid, halo, edge in (
        (normed_ext, normed_mid, normed_halo, scaled),
        (k_b, k_mid, k_halo, k),
        (v_b, v_mid, v_halo, projected[:, C:]),
        (k_inv, k_inv_mid, k_inv_halo, inv_k),
    ):
        edge = edge.reshape(2 * ER, PAD, C)
        ext[0:WIN] = halo[0:WIN]
        ext[WIN : WIN + BR] = mid[...]
        ext[WIN + BR : ER] = halo[WIN : 2 * WIN]
        near = ext[:, 0 : 2 * PAD].astype(F32)[:, PAD:]
        ext[:, 0 : 2 * PAD] = jnp.concatenate([edge[:ER], near], axis=1).astype(BF16)
        near = ext[:, EC - 2 * PAD : EC].astype(F32)[:, :PAD]
        ext[:, EC - 2 * PAD : EC] = jnp.concatenate([near, edge[ER:]], axis=1).astype(BF16)

    gk[...] = jnp.zeros_like(gk)
    gv[...] = jnp.zeros_like(gv)

    key_row = lax.broadcasted_iota(jnp.int32, (ER, KC, NQ), 0)
    key_col = lax.broadcasted_iota(jnp.int32, (ER, KC, NQ), 1)
    query = lax.broadcasted_iota(jnp.int32, (ER, KC, NQ), 2)
    row_gap = key_row - query // QC
    col_gap = key_col - query % QC - (PAD - WIN)
    in_rows = (key_row + place[0] - WIN >= 0) & (key_row + place[0] - WIN < GRID)
    near = (row_gap >= 0) & (row_gap <= 2 * WIN) & (col_gap >= 0) & (col_gap <= 2 * WIN)
    base[...] = jnp.where(near & in_rows, 1.0, 0.0)

    first = lax.broadcasted_iota(jnp.int32, (NQ, LANES), 1) < HEAD
    top = lax.broadcasted_iota(jnp.int32, (LANES, NQ), 0) < HEAD

    def both(a):
        zero = jnp.zeros_like(a)
        return jnp.concatenate([jnp.where(first, a, zero), jnp.where(first, zero, a)], axis=0)

    def own_head(a):
        return jnp.where(top, a[:, :NQ], a[:, NQ:]).T

    @pl.loop(0, BLOCKS)
    def _(b):
        q_cols = pl.ds(pl.multiple_of(b * QC, QC), QC)
        k_cols = pl.ds(pl.multiple_of(b * QC, QC), KC)
        col = lax.broadcasted_iota(jnp.int32, (ER, KC, NQ), 1) + (place[1] - PAD + b * QC)
        mask = jnp.where((col >= 0) & (col < GRID), base[...], 0.0).reshape(NK, NQ)
        mask = jnp.concatenate([mask, mask], axis=1)
        for p in range(PAIRS):
            lanes = slice(p * LANES, (p + 1) * LANES)
            k2 = k_b[:, k_cols, lanes].reshape(NK, LANES)
            v2 = v_b[:, k_cols, lanes].reshape(NK, LANES)
            q2 = both(q_b[:, q_cols, lanes].reshape(NQ, LANES))
            d2 = both(d_b[:, q_cols, lanes].reshape(NQ, LANES))
            e = jnp.exp(mm(k2, q2, ((1,), (1,)))) * mask
            attend = e * (1.0 / jnp.sum(e, axis=0, keepdims=True))
            attend_b = attend.astype(BF16)
            grad_probs = mm(v2, d2, ((1,), (1,)))
            delta = jnp.sum(attend * grad_probs, axis=0, keepdims=True)
            grad_scores = (attend * (grad_probs - delta)).astype(BF16)
            attended = own_head(mm(v2, attend_b, ((0,), (0,))))
            att_b[:, q_cols, lanes] = attended.astype(BF16).reshape(BR, QC, LANES)
            grad_query = own_head(mm(k2, grad_scores, ((0,), (0,))))
            gq[:, q_cols, lanes] = grad_query.reshape(BR, QC, LANES)
            gk[:, k_cols, lanes] += mm(grad_scores, q2).reshape(ER, KC, LANES)
            gv[:, k_cols, lanes] += mm(attend_b, d2).reshape(ER, KC, LANES)

    inv_factor = 1.0 / factor[...]
    grad_query = gq[...].reshape(BR * BC, C)
    q_f = q_b[...].reshape(BR * BC, C).astype(F32)
    mean = per_head_mean(grad_query * q_f, ones[...]) * inv_factor
    scale_sum = jnp.sum(mean, axis=0, keepdims=True)
    g = q_inv[...].reshape(BR * BC, C) * (factor[...] * grad_query - q_f * mean)
    g = g.astype(BF16)
    g_q[...] = g.reshape(BR, BC, C)
    acc[3 * C :] = mm(att_b[...].reshape(BR * BC, C), cot[...].reshape(BR * BC, C), ((0,), (0,)))
    acc[:C] = mm(normed_own[...].reshape(BR * BC, C), g, ((0,), (0,)))

    @pl.loop(0, ER // 2)
    def _(i):
        rows = pl.ds(2 * i, 2)
        shape = (2, EC, C)
        grad_key = gk[rows].reshape(2 * EC, C)
        k_f = k_b[rows].reshape(2 * EC, C).astype(F32)
        mean = per_head_mean(grad_key * k_f, ones[...])
        g_k = k_inv[rows].reshape(2 * EC, C).astype(F32) * (grad_key - k_f * mean)
        g_kv[rows, :, :C] = g_k.astype(BF16).reshape(shape)
        g_kv[rows, :, C:] = gv[rows].astype(BF16)

    copy = pltpu.make_async_copy(g_kv, g_kv_out, copied)
    copy.start()
    acc_kv = mm(normed_ext[...].reshape(ER * EC, C), g_kv[...].reshape(ER * EC, 2 * C), ((0,), (0,)))
    acc[C : 2 * C] = acc_kv[:, :C]
    acc[2 * C : 3 * C] = acc_kv[:, C:]

    by_feature = (
        wqkv[:, :C].astype(F32) * acc[:C]
        + wqkv[:, C : 2 * C].astype(F32) * acc[C : 2 * C]
        + wqkv[:, 2 * C :].astype(F32) * acc[2 * C : 3 * C]
    )
    high, low = split_bf16(by_feature)
    every = jnp.ones((8, C), BF16)
    gain_sum = mm(every, high, ((1,), (1,))) + mm(every, low, ((1,), (1,)))
    gain_sum = gain_sum[0:1] / gain[...]

    for ref, half in ((keep, place[2]), (send, 1 - place[2])):
        for part in range(PARTS):
            rows = pl.ds(pl.multiple_of(half * HALF + part * PART, PART), PART)
            for h in (0, 1):
                piece = acc[rows, h * 128 : h * 128 + 128]
                ref[part, h * PART : h * PART + PART] = piece.astype(ref.dtype)
    small = [part.astype(F32) for part in split_bf16(jnp.concatenate([scale_sum, gain_sum], axis=0))]
    small = [a[i : i + 1, h * 128 : h * 128 + 128] for a in small for i in (0, 1) for h in (0, 1)]
    small = jnp.concatenate(small + [jnp.zeros((2 * PART - EXTRA, 128), F32)], axis=0)
    keep[PARTS] = small
    send[PARTS] = small.astype(BF16)
    copy.wait()


def token_kernel(
    up,
    own,
    down,
    left,
    right,
    cot,
    gain,
    wqkv,
    wo,
    att_b,
    g_q,
    g_kv,
    out,
    grad_own,
    grad_up,
    grad_down,
    grad_left,
    grad_right,
    ext,
):
    own_cols = slice(PAD, PAD + BC)
    ext[0:WIN, own_cols] = up[...].astype(F32)
    ext[WIN : WIN + BR, own_cols] = own[...].astype(F32)
    ext[WIN + BR : ER, own_cols] = down[...].astype(F32)
    ext[:, 0:PAD] = left[...].astype(F32)
    ext[:, PAD + BC : EC] = right[...].astype(F32)

    @pl.loop(0, ER // 2)
    def _(i):
        rows = pl.ds(2 * i, 2)
        grad_normed = mm(g_kv[rows].reshape(2 * EC, 2 * C), wqkv[:, C:], ((1,), (1,)))
        n, hat = row_stats(ext[rows].reshape(2 * EC, C))
        ext[rows] = norm_grad(gain[...] * grad_normed, n, hat).reshape(2, EC, C)

    grad_up[...] = ext[0:WIN].astype(BF16)
    grad_down[...] = ext[WIN + BR : ER].astype(BF16)
    grad_left[...] = ext[WIN : WIN + BR, 0:PAD]
    grad_right[...] = ext[WIN : WIN + BR, PAD + BC : EC]

    @pl.loop(0, BR // 2)
    def _(i):
        rows = pl.ds(2 * i, 2)
        shape = (2, BC, C)
        tok = own[rows].reshape(2 * BC, C).astype(F32)
        att = att_b[rows].reshape(2 * BC, C)
        out[rows] = (tok + mm(att, wo[...])).astype(BF16).reshape(shape)
        grad_normed = mm(g_q[rows].reshape(2 * BC, C), wqkv[:, :C], ((1,), (1,)))
        n, hat = row_stats(tok)
        grad = cot[rows].reshape(2 * BC, C).astype(F32) + norm_grad(gain[...] * grad_normed, n, hat)
        grad_own[rows] = grad.reshape(shape) + ext[pl.ds(WIN + 2 * i, 2), own_cols]


def result_kernel(place, mine, other, qkv, out):
    def write(halves):
        for block in range(4):
            half = halves[block // 2]
            for part in range(C // PART):
                rows = slice(part * PART, part * PART + PART)
                for h in (0, 1):
                    piece = half[block % 2 * (C // PART) + part, h * PART : h * PART + PART].astype(F32) / GRID
                    if block < 3:
                        qkv[rows, block * C + h * 128 : block * C + h * 128 + 128] = piece
                    else:
                        out[rows, h * 128 : h * 128 + 128] = piece

    @pl.when(place[2] == 0)
    def _():
        write((mine, other))

    @pl.when(place[2] == 1)
    def _():
        write((other, mine))


def call(fn, out_shape, scratch, megabytes, microseconds, *args, in_hbm=()):
    vmem = pl.BlockSpec(memory_space=pltpu.VMEM)
    smem = pl.BlockSpec(memory_space=pltpu.SMEM)
    return pl.pallas_call(
        fn,
        out_shape=tuple(jax.ShapeDtypeStruct(s, d) for s, d in out_shape),
        in_specs=[smem if a.dtype == jnp.int32 else vmem for a in args],
        out_specs=tuple(pl.BlockSpec(memory_space=pltpu.HBM) if i in in_hbm else vmem for i in range(len(out_shape))),
        scratch_shapes=[pltpu.VMEM(s, d) for s, d in scratch] + [pltpu.SemaphoreType.DMA for _ in in_hbm],
        compiler_params=pltpu.CompilerParams(vmem_limit_bytes=megabytes * 1024 * 1024),
        cost_estimate=pl.CostEstimate(flops=microseconds * 1_000_000_000, bytes_accessed=1_000_000, transcendentals=0),
    )(*args)


OWN = (BR, BC, C)
EXT = (ER, EC, C)
ONES = ((C, C), BF16)


def run_own(tokens, cotangent, gain, factor, wqkv, wo):
    mid = ((BR, EC, C), BF16)
    outs = [(OWN, BF16), (OWN, BF16), (OWN, BF16), (OWN, F32), mid, mid, mid, mid]
    return call(own_kernel, outs, [ONES], 12, 3, tokens, cotangent, gain, factor, wqkv, wo)


def run_halo(up, down, gain, wqkv):
    halo = ((2 * WIN, EC, C), BF16)
    return call(halo_kernel, [halo] * 4, [ONES], 12, 3, up, down, gain, wqkv)


def run_attention(place, left, right, cot, gain, factor, wqkv, own, halo):
    half = (PARTS + 1, 2 * PART, 128)
    g_kv = ((ER, EC, 2 * C), BF16)
    outs = [(half, F32), (half, BF16), (OWN, BF16), (OWN, BF16), g_kv]
    scratch = [(EXT, BF16)] * 4 + [(EXT, F32)] * 2 + [(OWN, F32), g_kv]
    scratch += [((4 * C, C), F32), ONES, ((ER, KC, NQ), F32)]
    args = (place, left, right, cot, gain, factor, wqkv, *own, *halo)
    return call(attention_kernel, outs, scratch, 28, 9, *args, in_hbm=(4,))


def run_result(place, mine, other):
    return call(result_kernel, [((C, 3 * C), F32), ((C, C), F32)], [], 8, 1, place, mine, other)


def run_tokens(up, own, down, left, right, cot, gain, wqkv, wo, att_b, g_q, g_kv):
    halo = ((WIN, EC, C), BF16)
    edge = ((BR, PAD, C), F32)
    outs = [(OWN, BF16), (OWN, F32), halo, halo, edge, edge]
    return call(token_kernel, outs, [(EXT, F32)], 16, 4, up, own, down, left, right, cot, gain, wqkv, wo, att_b, g_q, g_kv)


def exchange(last, first, axes):
    size = math.prod(AXIS_SIZES[AXES.index(a)] for a in axes)
    forward = [(i, i + 1) for i in range(size - 1)]
    backward = [(i + 1, i) for i in range(size - 1)]
    return lax.ppermute(last, axes, forward), lax.ppermute(first, axes, backward)


def to_all(x, axes, size):
    return lax.all_to_all(jnp.broadcast_to(x[None], (size,) + x.shape), axes, 0, 0)


def resplit(small):
    total = small[: EXTRA // 2] + small[EXTRA // 2 :]
    high = lax.reduce_precision(total, 8, 7)
    return jnp.concatenate([high, total - high], axis=0)


def reduce_sums(keep, send):
    swap = [(0, 1), (1, 0)]
    chip = keep + lax.ppermute(send, "core", swap).astype(F32)
    small = jnp.broadcast_to(resplit(chip[PARTS, :EXTRA])[None], (PARTS, EXTRA, 128))
    parts = jnp.concatenate([chip[:PARTS], small], axis=1).astype(BF16)
    part = jnp.sum(lax.all_to_all(parts, SPLIT, 0, 0).astype(F32), axis=0)
    part = jnp.concatenate([part[: 2 * PART], resplit(part[2 * PART :])], axis=0).astype(BF16)
    part = jnp.sum(to_all(part, REST, RESTS).astype(F32), axis=0)
    mine = to_all(part[: 2 * PART].astype(BF16), SPLIT, PARTS)
    other = lax.ppermute(mine, "core", swap)
    return mine, other, part[2 * PART :]


def body(tokens, norm_gain, qkv_weight, head_scale, out_weight, cotangent):
    place = jnp.stack([lax.axis_index(ROWS) * BR, lax.axis_index(GRP) * BC, lax.axis_index("core")]).astype(jnp.int32)
    gain = norm_gain[None]
    factor = jnp.repeat(head_scale / HEAD, HEAD)[None]
    up, down = exchange(tokens[BR - WIN :], tokens[:WIN], ROWS)
    own = run_own(tokens, cotangent, gain, factor, qkv_weight, out_weight)
    last_cols = jnp.concatenate([a[:, BC - PAD :] for a in (up, tokens, down)], axis=0)
    first_cols = jnp.concatenate([a[:, :PAD] for a in (up, tokens, down)], axis=0)
    left, right = exchange(last_cols, first_cols, GRP)
    halo = run_halo(up, down, gain, qkv_weight)
    keep, send, att_b, g_q, g_kv = run_attention(place, left, right, cotangent, gain, factor, qkv_weight, own, halo)
    out, grad_own, grad_up, grad_down, grad_left, grad_right = run_tokens(
        up, tokens, down, left, right, cotangent, gain, qkv_weight, out_weight, att_b, g_q, g_kv
    )
    from_up, from_down = exchange(grad_down, grad_up, ROWS)
    from_up = jnp.pad(from_up.astype(F32), ((0, BR - WIN), (0, 0), (0, 0)))
    from_down = jnp.pad(from_down.astype(F32), ((BR - WIN, 0), (0, 0), (0, 0)))
    rows_back = from_up + from_down
    from_left, from_right = exchange(
        (grad_right + rows_back[:, PAD + BC :]).astype(BF16),
        (grad_left + rows_back[:, :PAD]).astype(BF16),
        GRP,
    )
    token_grad = (
        grad_own
        + rows_back[:, PAD : PAD + BC]
        + jnp.pad(from_left.astype(F32), ((0, 0), (0, BC - PAD), (0, 0)))
        + jnp.pad(from_right.astype(F32), ((0, 0), (BC - PAD, 0), (0, 0)))
    )
    mine, other, small = reduce_sums(keep, send)
    qkv_grad, out_grad = run_result(place, mine, other)
    small = (small[: EXTRA // 2] + small[EXTRA // 2 :]).reshape(2, C) / GRID
    return out, token_grad, small[1], qkv_grad, small[0].reshape(HEADS, HEAD)[:, 0], out_grad


def solution(mesh):
    fine = Mesh(mesh.devices.reshape(AXIS_SIZES), AXES)
    tiles = P(ROWS, GRP, None)
    return jax.shard_map(
        body,
        mesh=fine,
        in_specs=(tiles, P(), P(), P(), P(), tiles),
        out_specs=(tiles, tiles, P(), P(), P(), P()),
        check_vma=False,
    )
```

```python
import math

import jax
import jax.numpy as jnp
from jax import lax
from jax.experimental import pallas as pl
from jax.experimental.pallas import tpu as pltpu
from jax.sharding import Mesh, PartitionSpec as P

HEADS = 4
HEAD = 64
C = 256
WIN = 3
BR = 4
BC = 128
GRID = 512

EPS = 1e-06

PAD = 8
ER = BR + 2 * WIN
EC = BC + 2 * PAD
QC = 32
KC = 48
BLOCKS = BC // QC
NQ = BR * QC
NK = ER * KC
PAIRS = HEADS // 2
LANES = 2 * HEAD

AXES = ("z", "xh", "y", "xl", "core")
AXIS_SIZES = (8, 2, 8, 2, 2)
ROWS = ("z", "xh", "y")
GRP = ("xl", "core")
SPLIT = ("z", "xh", "xl")
REST = ("y",)
PARTS = 32
RESTS = 8
HALF = 2 * C
PART = HALF // PARTS
EXTRA = 8

F32 = jnp.float32
BF16 = jnp.bfloat16


def mm(a, b, dims=((1,), (0,))):
    return lax.dot_general(a, b, (dims, ((), ())), preferred_element_type=F32)


def split_bf16(a):
    high = a.astype(BF16)
    return high, (a - high.astype(F32)).astype(BF16)


def row_stats(t):
    n = lax.rsqrt(jnp.mean(t * t, axis=-1, keepdims=True) + EPS)
    return n, t * n


def norm_grad(u, n, hat):
    return n * (u - hat * jnp.mean(u * hat, axis=-1, keepdims=True))


def ones_per_head():
    lane_head = lax.broadcasted_iota(jnp.int32, (C, C), 1) // HEAD
    row_head = lax.broadcasted_iota(jnp.int32, (C, C), 0) // HEAD
    return jnp.where(lane_head == row_head, 1.0 / HEAD, 0.0).astype(BF16)


def per_head_mean(a, ones):
    high, low = split_bf16(a)
    return mm(high, ones) + mm(low, ones)


def normalise(raw, ones):
    inv = lax.rsqrt(per_head_mean(raw * raw, ones) + EPS)
    return raw * inv, inv


def widen(a, rows):
    edge = jnp.zeros((rows, PAD, C), F32)
    return jnp.concatenate([edge, a.reshape(rows, BC, C), edge], axis=1).astype(BF16)


def own_kernel(
    place, own, cot, gain, factor, wqkv, wo, q_b, d_b, normed_own, q_inv, near_mask, normed_ext, k_b, v_b, k_inv, ones
):
    ones[...] = ones_per_head()

    key_row = lax.broadcasted_iota(jnp.int32, (ER, KC, NQ), 0)
    key_col = lax.broadcasted_iota(jnp.int32, (ER, KC, NQ), 1)
    query = lax.broadcasted_iota(jnp.int32, (ER, KC, NQ), 2)
    row_gap = key_row - query // QC
    col_gap = key_col - query % QC - (PAD - WIN)
    in_rows = (key_row + place[0] - WIN >= 0) & (key_row + place[0] - WIN < GRID)
    near = (row_gap >= 0) & (row_gap <= 2 * WIN) & (col_gap >= 0) & (col_gap <= 2 * WIN)
    near_mask[...] = jnp.where(near & in_rows, 1.0, 0.0)

    @pl.loop(0, BR // 2)
    def _(i):
        rows = pl.ds(2 * i, 2)
        shape = (2, BC, C)
        _, hat = row_stats(own[rows].reshape(2 * BC, C).astype(F32))
        scaled = hat * gain[...]
        normed = scaled.astype(BF16)
        projected = mm(normed, wqkv[...])
        q, inv = normalise(projected[:, :C], ones[...])
        k, inv_k = normalise(projected[:, C : 2 * C], ones[...])
        normed_own[rows] = normed.reshape(shape)
        q_inv[rows] = inv.reshape(shape)
        q_b[rows] = (q * factor[...]).astype(BF16).reshape(shape)
        normed_ext[rows] = widen(scaled, 2)
        k_b[rows] = widen(k, 2)
        k_inv[rows] = widen(inv_k, 2)
        v_b[rows] = widen(projected[:, 2 * C :], 2)
        d = mm(cot[rows].reshape(2 * BC, C), wo[...], ((1,), (1,)))
        d_b[rows] = d.astype(BF16).reshape(shape)


def halo_kernel(place, from_a, from_b, gain, wqkv, normed_ext, k_b, v_b, k_inv, ones):
    ones[...] = ones_per_head()
    for ref, at in ((from_a, place[3]), (from_b, 1 - place[3])):
        rows = pl.ds(at * WIN, WIN)
        _, hat = row_stats(ref[...].reshape(WIN * BC, C).astype(F32))
        scaled = hat * gain[...]
        projected = mm(scaled.astype(BF16), wqkv[:, C:])
        k, inv_k = normalise(projected[:, :C], ones[...])
        normed_ext[rows] = widen(scaled, WIN)
        k_b[rows] = widen(k, WIN)
        k_inv[rows] = widen(inv_k, WIN)
        v_b[rows] = widen(projected[:, C:], WIN)


def attention_kernel(
    place,
    from_a,
    from_b,
    cot,
    gain,
    factor,
    wqkv,
    q_b,
    d_b,
    normed_own,
    q_inv,
    near_mask,
    normed_mid,
    k_mid,
    v_mid,
    k_inv_mid,
    normed_halo,
    k_halo,
    v_halo,
    k_inv_halo,
    keep,
    send,
    att_b,
    g_q,
    g_kv_own,
    to_a,
    to_b,
    normed_ext,
    k_b,
    v_b,
    k_inv,
    gk,
    gv,
    gq,
    g_kv,
    acc,
    ones,
):
    ones[...] = ones_per_head()

    odd = place[4] == 1
    left = jnp.where(odd, from_b[...].astype(F32), from_a[...].astype(F32))
    right = jnp.where(odd, from_a[...].astype(F32), from_b[...].astype(F32))
    edges = jnp.concatenate([left, right], axis=0)
    _, hat = row_stats(edges.reshape(2 * ER * PAD, C))
    scaled = hat * gain[...]
    projected = mm(scaled.astype(BF16), wqkv[:, C:])
    k, inv_k = normalise(projected[:, :C], ones[...])
    for ext, mid, halo, edge in (
        (normed_ext, normed_mid, normed_halo, scaled),
        (k_b, k_mid, k_halo, k),
        (v_b, v_mid, v_halo, projected[:, C:]),
        (k_inv, k_inv_mid, k_inv_halo, inv_k),
    ):
        edge = edge.reshape(2 * ER, PAD, C)
        ext[0:WIN] = halo[0:WIN]
        ext[WIN : WIN + BR] = mid[...]
        ext[WIN + BR : ER] = halo[WIN : 2 * WIN]
        near = ext[:, 0 : 2 * PAD].astype(F32)[:, PAD:]
        ext[:, 0 : 2 * PAD] = jnp.concatenate([edge[:ER], near], axis=1).astype(BF16)
        near = ext[:, EC - 2 * PAD : EC].astype(F32)[:, :PAD]
        ext[:, EC - 2 * PAD : EC] = jnp.concatenate([near, edge[ER:]], axis=1).astype(BF16)

    gk[...] = jnp.zeros_like(gk)
    gv[...] = jnp.zeros_like(gv)

    first = lax.broadcasted_iota(jnp.int32, (NQ, LANES), 1) < HEAD
    top = lax.broadcasted_iota(jnp.int32, (LANES, NQ), 0) < HEAD

    def both(a):
        zero = jnp.zeros_like(a)
        return jnp.concatenate([jnp.where(first, a, zero), jnp.where(first, zero, a)], axis=0)

    def own_head(a):
        return jnp.where(top, a[:, :NQ], a[:, NQ:]).T

    @pl.loop(0, BLOCKS, unroll=BLOCKS)
    def _(b):
        q_cols = pl.ds(pl.multiple_of(b * QC, QC), QC)
        k_cols = pl.ds(pl.multiple_of(b * QC, QC), KC)
        col = lax.broadcasted_iota(jnp.int32, (ER, KC, NQ), 1) + (place[1] - PAD + b * QC)
        mask = jnp.where((col >= 0) & (col < GRID), near_mask[...], 0.0).reshape(NK, NQ)
        mask = jnp.concatenate([mask, mask], axis=1)
        for p in range(PAIRS):
            lanes = slice(p * LANES, (p + 1) * LANES)
            k2 = k_b[:, k_cols, lanes].reshape(NK, LANES)
            v2 = v_b[:, k_cols, lanes].reshape(NK, LANES)
            q2 = both(q_b[:, q_cols, lanes].reshape(NQ, LANES))
            d2 = both(d_b[:, q_cols, lanes].reshape(NQ, LANES))
            e = jnp.exp(mm(k2, q2, ((1,), (1,)))) * mask
            attend = e * (1.0 / jnp.sum(e, axis=0, keepdims=True))
            attend_b = attend.astype(BF16)
            grad_probs = mm(v2, d2, ((1,), (1,)))
            delta = jnp.sum(attend * grad_probs, axis=0, keepdims=True)
            grad_scores = (attend * (grad_probs - delta)).astype(BF16)
            attended = own_head(mm(v2, attend_b, ((0,), (0,))))
            att_b[:, q_cols, lanes] = attended.astype(BF16).reshape(BR, QC, LANES)
            grad_query = own_head(mm(k2, grad_scores, ((0,), (0,))))
            gq[:, q_cols, lanes] = grad_query.reshape(BR, QC, LANES)
            gk[:, k_cols, lanes] += mm(grad_scores, q2).reshape(ER, KC, LANES)
            gv[:, k_cols, lanes] += mm(attend_b, d2).reshape(ER, KC, LANES)

    inv_factor = 1.0 / factor[...]
    grad_query = gq[...].reshape(BR * BC, C)
    q_f = q_b[...].reshape(BR * BC, C).astype(F32)
    mean = per_head_mean(grad_query * q_f, ones[...]) * inv_factor
    scale_sum = jnp.sum(mean, axis=0, keepdims=True)
    g = q_inv[...].reshape(BR * BC, C) * (factor[...] * grad_query - q_f * mean)
    g = g.astype(BF16)
    g_q[...] = g.reshape(BR, BC, C)
    acc[3 * C :] = mm(att_b[...].reshape(BR * BC, C), cot[...].reshape(BR * BC, C), ((0,), (0,)))
    acc[:C] = mm(normed_own[...].reshape(BR * BC, C), g, ((0,), (0,)))

    @pl.loop(0, ER // 2, unroll=ER // 2)
    def _(i):
        rows = pl.ds(2 * i, 2)
        shape = (2, EC, C)
        grad_key = gk[rows].reshape(2 * EC, C)
        k_f = k_b[rows].reshape(2 * EC, C).astype(F32)
        mean = per_head_mean(grad_key * k_f, ones[...])
        g_k = k_inv[rows].reshape(2 * EC, C).astype(F32) * (grad_key - k_f * mean)
        g_kv[rows, :, :C] = g_k.astype(BF16).reshape(shape)
        g_kv[rows, :, C:] = gv[rows].astype(BF16)

    g_kv_own[...] = g_kv[WIN : WIN + BR]
    for ref, at in ((to_a, place[3]), (to_b, 1 - place[3])):
        g = g_kv[pl.ds(at * (WIN + BR), WIN)].reshape(WIN * EC, 2 * C)
        ref[...] = mm(g, wqkv[:, C:], ((1,), (1,))).astype(BF16).reshape(WIN, EC, C)

    acc_kv = mm(normed_ext[...].reshape(ER * EC, C), g_kv[...].reshape(ER * EC, 2 * C), ((0,), (0,)))
    acc[C : 2 * C] = acc_kv[:, :C]
    acc[2 * C : 3 * C] = acc_kv[:, C:]

    by_feature = (
        wqkv[:, :C].astype(F32) * acc[:C]
        + wqkv[:, C : 2 * C].astype(F32) * acc[C : 2 * C]
        + wqkv[:, 2 * C :].astype(F32) * acc[2 * C : 3 * C]
    )
    high, low = split_bf16(by_feature)
    every = jnp.ones((8, C), BF16)
    gain_sum = mm(every, high, ((1,), (1,))) + mm(every, low, ((1,), (1,)))
    gain_sum = gain_sum[0:1] / gain[...]

    for ref, half in ((keep, place[2]), (send, 1 - place[2])):
        for part in range(PARTS):
            rows = pl.ds(pl.multiple_of(half * HALF + part * PART, PART), PART)
            for h in (0, 1):
                piece = acc[rows, h * 128 : h * 128 + 128]
                ref[part, h * PART : h * PART + PART] = piece.astype(ref.dtype)
    small = [part.astype(F32) for part in split_bf16(jnp.concatenate([scale_sum, gain_sum], axis=0))]
    small = [a[i : i + 1, h * 128 : h * 128 + 128] for a in small for i in (0, 1) for h in (0, 1)]
    small = jnp.concatenate(small + [jnp.zeros((2 * PART - EXTRA, 128), F32)], axis=0)
    keep[PARTS] = small
    send[PARTS] = small.astype(BF16)


def own_grad_kernel(
    place, own, wqkv, wo, att_b, g_q, g_kv_own, from_a, from_b, out, grad_normed, to_a, to_b, total
):
    total[...] = mm(g_kv_own[...].reshape(BR * EC, 2 * C), wqkv[:, C:], ((1,), (1,))).reshape(BR, EC, C)
    total[pl.ds(place[3], WIN)] += from_a[...].astype(F32)
    total[pl.ds(1 - place[3], WIN)] += from_b[...].astype(F32)
    left = total[:, :PAD]
    right = total[:, PAD + BC :]
    odd = place[4] == 1
    to_a[...] = jnp.where(odd, right, left).astype(BF16)
    to_b[...] = jnp.where(odd, left, right).astype(BF16)
    by_query = mm(g_q[...].reshape(BR * BC, C), wqkv[:, :C], ((1,), (1,)))
    grad_normed[...] = by_query.reshape(OWN) + total[:, PAD : PAD + BC]
    projected = mm(att_b[...].reshape(BR * BC, C), wo[...])
    out[...] = (own[...].astype(F32) + projected.reshape(OWN)).astype(BF16)


def token_kernel(place, own, cot, gain, grad_normed, from_a, from_b, token_grad, total):
    odd = place[4] == 1
    total[...] = grad_normed[...]
    total[:, :PAD] += jnp.where(odd, from_b[...].astype(F32), from_a[...].astype(F32))
    total[:, BC - PAD :] += jnp.where(odd, from_a[...].astype(F32), from_b[...].astype(F32))
    n, hat = row_stats(own[...].reshape(BR * BC, C).astype(F32))
    grad = norm_grad(gain[...] * total[...].reshape(BR * BC, C), n, hat)
    token_grad[...] = cot[...].astype(F32) + grad.reshape(OWN)


def edge_kernel(place, rows_a, rows_b, own, to_a, to_b, last, first):
    parts = ((rows_a, place[3] * (WIN + BR)), (rows_b, (1 - place[3]) * (WIN + BR)), (own, WIN))
    for ref, at in parts:
        rows = pl.ds(at, ref.shape[0])
        last[rows] = ref[:, BC - 2 * PAD :].astype(F32)[:, PAD:]
        first[rows] = ref[:, : 2 * PAD].astype(F32)[:, :PAD]
    odd = place[4] == 1
    to_a[...] = jnp.where(odd, last[...], first[...]).astype(BF16)
    to_b[...] = jnp.where(odd, first[...], last[...]).astype(BF16)


def resplit(small):
    total = small[: EXTRA // 2] + small[EXTRA // 2 :]
    high, low = split_bf16(total)
    return jnp.concatenate([high.astype(F32), low.astype(F32)], axis=0)


def chip_kernel(keep, received, parts):
    total = keep[:PARTS] + received[:PARTS].astype(F32)
    small = resplit((keep[PARTS] + received[PARTS].astype(F32))[:EXTRA])
    small = jnp.broadcast_to(small[None], (PARTS, EXTRA, 128))
    parts[...] = jnp.concatenate([total, small], axis=1).astype(BF16)


def part_kernel(parts, copies):
    part = jnp.sum(parts[...].astype(F32), axis=0)
    part = jnp.concatenate([part[: 2 * PART], resplit(part[2 * PART :])], axis=0)
    copies[...] = jnp.broadcast_to(part[None], copies.shape).astype(BF16)


def whole_kernel(parts, copies, small):
    part = jnp.sum(parts[...].astype(F32), axis=0)
    copies[...] = jnp.broadcast_to(part[None, : 2 * PART], copies.shape).astype(BF16)
    last = part[2 * PART :]
    small[...] = (last[: EXTRA // 2] + last[EXTRA // 2 :]) / GRID


def result_kernel(place, mine, other, qkv, out):
    def write(halves):
        for block in range(4):
            half = halves[block // 2]
            for part in range(C // PART):
                rows = slice(part * PART, part * PART + PART)
                for h in (0, 1):
                    piece = half[block % 2 * (C // PART) + part, h * PART : h * PART + PART].astype(F32) / GRID
                    if block < 3:
                        qkv[rows, block * C + h * 128 : block * C + h * 128 + 128] = piece
                    else:
                        out[rows, h * 128 : h * 128 + 128] = piece

    @pl.when(place[2] == 0)
    def _():
        write((mine, other))

    @pl.when(place[2] == 1)
    def _():
        write((other, mine))


def call(fn, out_shape, scratch, megabytes, microseconds, *args):
    vmem = pl.BlockSpec(memory_space=pltpu.VMEM)
    smem = pl.BlockSpec(memory_space=pltpu.SMEM)
    return pl.pallas_call(
        fn,
        out_shape=tuple(jax.ShapeDtypeStruct(s, d) for s, d in out_shape),
        in_specs=[smem if a.dtype == jnp.int32 else vmem for a in args],
        out_specs=tuple(vmem for _ in out_shape),
        scratch_shapes=[pltpu.VMEM(s, d) for s, d in scratch],
        compiler_params=pltpu.CompilerParams(vmem_limit_bytes=megabytes * 1024 * 1024),
        cost_estimate=pl.CostEstimate(flops=microseconds * 1_000_000_000, bytes_accessed=1_000_000, transcendentals=0),
    )(*args)


OWN = (BR, BC, C)
EXT = (ER, EC, C)
ONES = ((C, C), BF16)


def run_own(place, tokens, cotangent, gain, factor, wqkv, wo):
    mid = ((BR, EC, C), BF16)
    outs = [(OWN, BF16), (OWN, BF16), (OWN, BF16), (OWN, F32), ((ER, KC, NQ), F32), mid, mid, mid, mid]
    return call(own_kernel, outs, [ONES], 12, 3, place, tokens, cotangent, gain, factor, wqkv, wo)


def run_halo(place, from_a, from_b, gain, wqkv):
    halo = ((2 * WIN, EC, C), BF16)
    return call(halo_kernel, [halo] * 4, [ONES], 12, 3, place, from_a, from_b, gain, wqkv)


def run_attention(place, from_a, from_b, cot, gain, factor, wqkv, own, halo):
    half = (PARTS + 1, 2 * PART, 128)
    to_rows = ((WIN, EC, C), BF16)
    outs = [(half, F32), (half, BF16), (OWN, BF16), (OWN, BF16), ((BR, EC, 2 * C), BF16), to_rows, to_rows]
    scratch = [(EXT, BF16)] * 4 + [(EXT, F32)] * 2 + [(OWN, F32), ((ER, EC, 2 * C), BF16)]
    scratch += [((4 * C, C), F32), ONES]
    return call(attention_kernel, outs, scratch, 28, 9, place, from_a, from_b, cot, gain, factor, wqkv, *own, *halo)


def run_own_grad(place, own, wqkv, wo, att_b, g_q, g_kv_own, from_a, from_b):
    to_cols = ((BR, PAD, C), BF16)
    outs = [(OWN, BF16), (OWN, F32), to_cols, to_cols]
    scratch = [((BR, EC, C), F32)]
    return call(own_grad_kernel, outs, scratch, 12, 3, place, own, wqkv, wo, att_b, g_q, g_kv_own, from_a, from_b)


def run_tokens(place, own, cot, gain, grad_normed, from_a, from_b):
    return call(token_kernel, [(OWN, F32)], [(OWN, F32)], 12, 2, place, own, cot, gain, grad_normed, from_a, from_b)[0]


def run_result(place, mine, other):
    return call(result_kernel, [((C, 3 * C), F32), ((C, C), F32)], [], 8, 1, place, mine, other)


def swap(a, b, axes):
    size = math.prod(AXIS_SIZES[AXES.index(axis)] for axis in axes)
    pairs = [[(i, i + 1) for i in range(at, size - 1, 2)] for at in (1, 0)]
    pairs = [[*some, *((j, i) for i, j in some)] for some in pairs]
    return lax.ppermute(a, axes, pairs[0]), lax.ppermute(b, axes, pairs[1])


def body(tokens, norm_gain, qkv_weight, head_scale, out_weight, cotangent):
    row, col = lax.axis_index(ROWS), lax.axis_index(GRP)
    odd_row, odd_col = row % 2, col % 2
    place = jnp.stack([row * BR, col * BC, lax.axis_index("core"), odd_row, odd_col]).astype(jnp.int32)
    gain = norm_gain[None]
    factor = jnp.repeat(head_scale / HEAD, HEAD)[None]
    cores = [(0, 1), (1, 0)]

    rows_a, rows_b = swap(
        lax.dynamic_slice_in_dim(tokens, odd_row, WIN, 0), lax.dynamic_slice_in_dim(tokens, 1 - odd_row, WIN, 0), ROWS
    )
    own = run_own(place, tokens, cotangent, gain, factor, qkv_weight, out_weight)
    edges = [((ER, PAD, C), BF16)] * 2
    cols_a, cols_b = call(edge_kernel, edges, [((ER, PAD, C), F32)] * 2, 8, 1, place, rows_a, rows_b, tokens)
    cols_a, cols_b = swap(cols_a, cols_b, GRP)
    halo = run_halo(place, rows_a, rows_b, gain, qkv_weight)
    keep, send, att_b, g_q, g_kv_own, rows_a, rows_b = run_attention(
        place, cols_a, cols_b, cotangent, gain, factor, qkv_weight, own, halo
    )

    received = lax.ppermute(send, "core", cores)
    rows = 2 * PART + EXTRA
    (parts,) = call(chip_kernel, [((PARTS, rows, 128), BF16)], [], 8, 1, keep, received)
    parts, rows_a, rows_b = lax.optimization_barrier((parts, rows_a, rows_b))
    parts = lax.all_to_all(parts, SPLIT, 0, 0)
    rows_a, rows_b = swap(rows_a, rows_b, ROWS)
    (copies,) = call(part_kernel, [((RESTS, rows, 128), BF16)], [], 8, 1, parts)
    copies, att_b, g_kv_own = lax.optimization_barrier((copies, att_b, g_kv_own))
    parts = lax.all_to_all(copies, REST, 0, 0)
    out, grad_normed, cols_a, cols_b = run_own_grad(
        place, tokens, qkv_weight, out_weight, att_b, g_q, g_kv_own, rows_a, rows_b
    )
    copies, small = call(whole_kernel, [((PARTS, 2 * PART, 128), BF16), ((EXTRA // 2, 128), F32)], [], 8, 1, parts)
    copies, cols_a, cols_b = lax.optimization_barrier((copies, cols_a, cols_b))
    mine = lax.all_to_all(copies, SPLIT, 0, 0)
    cols_a, cols_b = swap(cols_a, cols_b, GRP)
    token_grad = run_tokens(place, tokens, cotangent, gain, grad_normed, cols_a, cols_b)
    other = lax.ppermute(mine, "core", cores)
    qkv_grad, out_grad = run_result(place, mine, other)
    small = small.reshape(2, C)
    return out, token_grad, small[1], qkv_grad, small[0].reshape(HEADS, HEAD)[:, 0], out_grad


def solution(mesh):
    fine = Mesh(mesh.devices.reshape(AXIS_SIZES), AXES)
    tiles = P(ROWS, GRP, None)
    return jax.shard_map(
        body,
        mesh=fine,
        in_specs=(tiles, P(), P(), P(), P(), tiles),
        out_specs=(tiles, tiles, P(), P(), P(), P()),
        check_vma=False,
    )
```

```python
import math

import jax
import jax.numpy as jnp
from jax import lax
from jax.experimental import pallas as pl
from jax.experimental.pallas import tpu as pltpu
from jax.sharding import Mesh, PartitionSpec as P

HEADS = 4
HEAD = 64
C = 256
WIN = 3
BR = 4
BC = 128
GRID = 512

EPS = 1e-06

PAD = 8
ER = BR + 2 * WIN
EC = BC + 2 * PAD
QC = 32
KC = 48
BLOCKS = BC // QC
NQ = BR * QC
NK = ER * KC
PAIRS = HEADS // 2
LANES = 2 * HEAD

AXES = ("z", "xh", "y", "xl", "core")
AXIS_SIZES = (8, 2, 8, 2, 2)
ROWS = ("z", "xh", "y")
GRP = ("xl", "core")
SPLIT = ("z", "xh", "xl")
REST = ("y",)
PARTS = 32
RESTS = 8
HALF = 2 * C
PART = HALF // PARTS
EXTRA = 8

F32 = jnp.float32
BF16 = jnp.bfloat16


def mm(a, b, dims=((1,), (0,))):
    return lax.dot_general(a, b, (dims, ((), ())), preferred_element_type=F32)


def split_bf16(a):
    high = a.astype(BF16)
    return high, (a - high.astype(F32)).astype(BF16)


def row_stats(t):
    n = lax.rsqrt(jnp.mean(t * t, axis=-1, keepdims=True) + EPS)
    return n, t * n


def norm_grad(u, n, hat):
    return n * (u - hat * jnp.mean(u * hat, axis=-1, keepdims=True))


def ones_per_head():
    lane_head = lax.broadcasted_iota(jnp.int32, (C, C), 1) // HEAD
    row_head = lax.broadcasted_iota(jnp.int32, (C, C), 0) // HEAD
    return jnp.where(lane_head == row_head, 1.0 / HEAD, 0.0).astype(BF16)


def per_head_mean(a, ones):
    return mm(a.astype(BF16), ones)


def normalise(raw, ones):
    inv = lax.rsqrt(per_head_mean(raw * raw, ones) + EPS)
    return raw * inv, inv


def widen(a, rows):
    edge = jnp.zeros((rows, PAD, C), F32)
    return jnp.concatenate([edge, a.reshape(rows, BC, C), edge], axis=1).astype(BF16)


def own_kernel(
    place, own, cot, gain, factor, wqkv, wo, q_b, d_b, normed_own, q_inv, near_mask, normed_ext, k_b, v_b, k_inv, ones
):
    ones[...] = ones_per_head()

    key_row = lax.broadcasted_iota(jnp.int32, (ER, KC, NQ), 0)
    key_col = lax.broadcasted_iota(jnp.int32, (ER, KC, NQ), 1)
    query = lax.broadcasted_iota(jnp.int32, (ER, KC, NQ), 2)
    row_gap = key_row - query // QC
    col_gap = key_col - query % QC - (PAD - WIN)
    in_rows = (key_row + place[0] - WIN >= 0) & (key_row + place[0] - WIN < GRID)
    near = (row_gap >= 0) & (row_gap <= 2 * WIN) & (col_gap >= 0) & (col_gap <= 2 * WIN)
    near_mask[...] = jnp.where(near & in_rows, 1.0, 0.0)

    @pl.loop(0, BR // 2)
    def _(i):
        rows = pl.ds(2 * i, 2)
        shape = (2, BC, C)
        _, hat = row_stats(own[rows].reshape(2 * BC, C).astype(F32))
        scaled = hat * gain[...]
        normed = scaled.astype(BF16)
        projected = mm(normed, wqkv[...])
        q, inv = normalise(projected[:, :C], ones[...])
        k, inv_k = normalise(projected[:, C : 2 * C], ones[...])
        normed_own[rows] = normed.reshape(shape)
        q_inv[rows] = inv.reshape(shape)
        q_b[rows] = (q * factor[...]).astype(BF16).reshape(shape)
        normed_ext[rows] = widen(scaled, 2)
        k_b[rows] = widen(k, 2)
        k_inv[rows] = widen(inv_k, 2)
        v_b[rows] = widen(projected[:, 2 * C :], 2)
        d = mm(cot[rows].reshape(2 * BC, C), wo[...], ((1,), (1,)))
        d_b[rows] = d.astype(BF16).reshape(shape)


def halo_kernel(rows, gain, wqkv, normed_ext, k_b, v_b, k_inv, ones):
    ones[...] = ones_per_head()
    _, hat = row_stats(rows[...].reshape(WIN * BC, C).astype(F32))
    scaled = hat * gain[...]
    projected = mm(scaled.astype(BF16), wqkv[:, C:])
    k, inv_k = normalise(projected[:, :C], ones[...])
    normed_ext[...] = widen(scaled, WIN)
    k_b[...] = widen(k, WIN)
    k_inv[...] = widen(inv_k, WIN)
    v_b[...] = widen(projected[:, C:], WIN)


def attention_kernel(
    place,
    from_a,
    from_b,
    cot,
    gain,
    factor,
    wqkv,
    q_b,
    d_b,
    normed_own,
    q_inv,
    near_mask,
    normed_mid,
    k_mid,
    v_mid,
    k_inv_mid,
    normed_a,
    k_a,
    v_a,
    k_inv_a,
    normed_b,
    k_from_b,
    v_from_b,
    k_inv_b,
    keep,
    send,
    att_b,
    g_q,
    g_kv_own,
    to_a,
    to_b,
    normed_ext,
    k_b,
    v_b,
    k_inv,
    gk,
    gv,
    gq,
    g_kv,
    acc,
    ones,
):
    ones[...] = ones_per_head()

    odd = place[4] == 1
    left = jnp.where(odd, from_b[...].astype(F32), from_a[...].astype(F32))
    right = jnp.where(odd, from_a[...].astype(F32), from_b[...].astype(F32))
    edges = jnp.concatenate([left, right], axis=0)
    _, hat = row_stats(edges.reshape(2 * ER * PAD, C))
    scaled = hat * gain[...]
    projected = mm(scaled.astype(BF16), wqkv[:, C:])
    k, inv_k = normalise(projected[:, :C], ones[...])
    for ext, mid, halo_a, halo_b, edge in (
        (normed_ext, normed_mid, normed_a, normed_b, scaled),
        (k_b, k_mid, k_a, k_from_b, k),
        (v_b, v_mid, v_a, v_from_b, projected[:, C:]),
        (k_inv, k_inv_mid, k_inv_a, k_inv_b, inv_k),
    ):
        edge = edge.reshape(2 * ER, PAD, C)
        ext[pl.ds(place[3] * (WIN + BR), WIN)] = halo_a[...]
        ext[pl.ds((1 - place[3]) * (WIN + BR), WIN)] = halo_b[...]
        ext[WIN : WIN + BR] = mid[...]
        near = ext[:, 0 : 2 * PAD].astype(F32)[:, PAD:]
        ext[:, 0 : 2 * PAD] = jnp.concatenate([edge[:ER], near], axis=1).astype(BF16)
        near = ext[:, EC - 2 * PAD : EC].astype(F32)[:, :PAD]
        ext[:, EC - 2 * PAD : EC] = jnp.concatenate([near, edge[ER:]], axis=1).astype(BF16)

    gk[...] = jnp.zeros_like(gk)
    gv[...] = jnp.zeros_like(gv)

    first = lax.broadcasted_iota(jnp.int32, (NQ, LANES), 1) < HEAD
    top = lax.broadcasted_iota(jnp.int32, (LANES, NQ), 0) < HEAD

    def both(a):
        zero = jnp.zeros_like(a)
        return jnp.concatenate([jnp.where(first, a, zero), jnp.where(first, zero, a)], axis=0)

    def own_head(a):
        return jnp.where(top, a[:, :NQ], a[:, NQ:]).T

    @pl.loop(0, BLOCKS, unroll=BLOCKS)
    def _(b):
        q_cols = pl.ds(pl.multiple_of(b * QC, QC), QC)
        k_cols = pl.ds(pl.multiple_of(b * QC, QC), KC)
        col = lax.broadcasted_iota(jnp.int32, (ER, KC, NQ), 1) + (place[1] - PAD + b * QC)
        mask = jnp.where((col >= 0) & (col < GRID), near_mask[...], 0.0).reshape(NK, NQ)
        mask = jnp.concatenate([mask, mask], axis=1)
        for p in range(PAIRS):
            lanes = slice(p * LANES, (p + 1) * LANES)
            k2 = k_b[:, k_cols, lanes].reshape(NK, LANES)
            v2 = v_b[:, k_cols, lanes].reshape(NK, LANES)
            q2 = both(q_b[:, q_cols, lanes].reshape(NQ, LANES))
            d2 = both(d_b[:, q_cols, lanes].reshape(NQ, LANES))
            e = jnp.exp(mm(k2, q2, ((1,), (1,)))) * mask
            attend = e * (1.0 / jnp.sum(e, axis=0, keepdims=True))
            attend_b = attend.astype(BF16)
            grad_probs = mm(v2, d2, ((1,), (1,)))
            delta = jnp.sum(attend * grad_probs, axis=0, keepdims=True)
            grad_scores = (attend * (grad_probs - delta)).astype(BF16)
            attended = own_head(mm(v2, attend_b, ((0,), (0,))))
            att_b[:, q_cols, lanes] = attended.astype(BF16).reshape(BR, QC, LANES)
            grad_query = own_head(mm(k2, grad_scores, ((0,), (0,))))
            gq[:, q_cols, lanes] = grad_query.reshape(BR, QC, LANES)
            gk[:, k_cols, lanes] += mm(grad_scores, q2).reshape(ER, KC, LANES)
            gv[:, k_cols, lanes] += mm(attend_b, d2).reshape(ER, KC, LANES)

    inv_factor = 1.0 / factor[...]
    grad_query = gq[...].reshape(BR * BC, C)
    q_f = q_b[...].reshape(BR * BC, C).astype(F32)
    mean = per_head_mean(grad_query * q_f, ones[...]) * inv_factor
    scale_sum = jnp.sum(mean, axis=0, keepdims=True)
    g = q_inv[...].reshape(BR * BC, C) * (factor[...] * grad_query - q_f * mean)
    g = g.astype(BF16)
    g_q[...] = g.reshape(BR, BC, C)
    acc[3 * C :] = mm(att_b[...].reshape(BR * BC, C), cot[...].reshape(BR * BC, C), ((0,), (0,)))
    acc[:C] = mm(normed_own[...].reshape(BR * BC, C), g, ((0,), (0,)))

    @pl.loop(0, ER // 2, unroll=ER // 2)
    def _(i):
        rows = pl.ds(2 * i, 2)
        shape = (2, EC, C)
        grad_key = gk[rows].reshape(2 * EC, C)
        k_f = k_b[rows].reshape(2 * EC, C).astype(F32)
        mean = per_head_mean(grad_key * k_f, ones[...])
        g_k = k_inv[rows].reshape(2 * EC, C).astype(F32) * (grad_key - k_f * mean)
        g_kv[rows, :, :C] = g_k.astype(BF16).reshape(shape)
        g_kv[rows, :, C:] = gv[rows].astype(BF16)

    g_kv_own[...] = g_kv[WIN : WIN + BR]
    for ref, at in ((to_a, place[3]), (to_b, 1 - place[3])):
        g = g_kv[pl.ds(at * (WIN + BR), WIN)].reshape(WIN * EC, 2 * C)
        ref[...] = mm(g, wqkv[:, C:], ((1,), (1,))).astype(BF16).reshape(WIN, EC, C)

    acc_kv = mm(normed_ext[...].reshape(ER * EC, C), g_kv[...].reshape(ER * EC, 2 * C), ((0,), (0,)))
    acc[C : 2 * C] = acc_kv[:, :C]
    acc[2 * C : 3 * C] = acc_kv[:, C:]

    by_feature = (
        wqkv[:, :C].astype(F32) * acc[:C]
        + wqkv[:, C : 2 * C].astype(F32) * acc[C : 2 * C]
        + wqkv[:, 2 * C :].astype(F32) * acc[2 * C : 3 * C]
    )
    high, low = split_bf16(by_feature)
    every = jnp.ones((8, C), BF16)
    gain_sum = mm(every, high, ((1,), (1,))) + mm(every, low, ((1,), (1,)))
    gain_sum = gain_sum[0:1] / gain[...]

    for ref, half in ((keep, place[2]), (send, 1 - place[2])):
        for part in range(PARTS):
            rows = pl.ds(pl.multiple_of(half * HALF + part * PART, PART), PART)
            for h in (0, 1):
                piece = acc[rows, h * 128 : h * 128 + 128]
                ref[part, h * PART : h * PART + PART] = piece.astype(ref.dtype)
    small = [part.astype(F32) for part in split_bf16(jnp.concatenate([scale_sum, gain_sum], axis=0))]
    small = [a[i : i + 1, h * 128 : h * 128 + 128] for a in small for i in (0, 1) for h in (0, 1)]
    small = jnp.concatenate(small + [jnp.zeros((2 * PART - EXTRA, 128), F32)], axis=0)
    keep[PARTS] = small
    send[PARTS] = small.astype(BF16)


def own_grad_kernel(
    place, own, wqkv, wo, att_b, g_q, g_kv_own, from_a, from_b, out, grad_normed, to_a, to_b, total
):
    total[...] = mm(g_kv_own[...].reshape(BR * EC, 2 * C), wqkv[:, C:], ((1,), (1,))).reshape(BR, EC, C)
    total[pl.ds(place[3], WIN)] += from_a[...].astype(F32)
    total[pl.ds(1 - place[3], WIN)] += from_b[...].astype(F32)
    left = total[:, :PAD]
    right = total[:, PAD + BC :]
    odd = place[4] == 1
    to_a[...] = jnp.where(odd, right, left).astype(BF16)
    to_b[...] = jnp.where(odd, left, right).astype(BF16)
    by_query = mm(g_q[...].reshape(BR * BC, C), wqkv[:, :C], ((1,), (1,)))
    grad_normed[...] = by_query.reshape(OWN) + total[:, PAD : PAD + BC]
    projected = mm(att_b[...].reshape(BR * BC, C), wo[...])
    out[...] = (own[...].astype(F32) + projected.reshape(OWN)).astype(BF16)


def token_kernel(place, own, cot, gain, grad_normed, from_a, from_b, token_grad, total):
    odd = place[4] == 1
    total[...] = grad_normed[...]
    total[:, :PAD] += jnp.where(odd, from_b[...].astype(F32), from_a[...].astype(F32))
    total[:, BC - PAD :] += jnp.where(odd, from_a[...].astype(F32), from_b[...].astype(F32))
    n, hat = row_stats(own[...].reshape(BR * BC, C).astype(F32))
    grad = norm_grad(gain[...] * total[...].reshape(BR * BC, C), n, hat)
    token_grad[...] = cot[...].astype(F32) + grad.reshape(OWN)


def edge_kernel(place, rows_a, rows_b, own, to_a, to_b, last, first):
    parts = ((rows_a, place[3] * (WIN + BR)), (rows_b, (1 - place[3]) * (WIN + BR)), (own, WIN))
    for ref, at in parts:
        rows = pl.ds(at, ref.shape[0])
        last[rows] = ref[:, BC - 2 * PAD :].astype(F32)[:, PAD:]
        first[rows] = ref[:, : 2 * PAD].astype(F32)[:, :PAD]
    odd = place[4] == 1
    to_a[...] = jnp.where(odd, last[...], first[...]).astype(BF16)
    to_b[...] = jnp.where(odd, first[...], last[...]).astype(BF16)


def resplit(small):
    total = small[: EXTRA // 2] + small[EXTRA // 2 :]
    high, low = split_bf16(total)
    return jnp.concatenate([high.astype(F32), low.astype(F32)], axis=0)


def chip_kernel(keep, received, parts):
    total = keep[:PARTS] + received[:PARTS].astype(F32)
    small = resplit((keep[PARTS] + received[PARTS].astype(F32))[:EXTRA])
    small = jnp.broadcast_to(small[None], (PARTS, EXTRA, 128))
    parts[...] = jnp.concatenate([total, small], axis=1).astype(BF16)


def part_kernel(parts, copies):
    part = jnp.sum(parts[...].astype(F32), axis=0)
    part = jnp.concatenate([part[: 2 * PART], resplit(part[2 * PART :])], axis=0)
    copies[...] = jnp.broadcast_to(part[None], copies.shape).astype(BF16)


def whole_kernel(parts, copies, small):
    part = jnp.sum(parts[...].astype(F32), axis=0)
    copies[...] = jnp.broadcast_to(part[None, : 2 * PART], copies.shape).astype(BF16)
    last = part[2 * PART :]
    small[...] = (last[: EXTRA // 2] + last[EXTRA // 2 :]) / GRID


def result_kernel(place, mine, other, qkv, out):
    def write(halves):
        for block in range(4):
            half = halves[block // 2]
            for part in range(C // PART):
                rows = slice(part * PART, part * PART + PART)
                for h in (0, 1):
                    piece = half[block % 2 * (C // PART) + part, h * PART : h * PART + PART].astype(F32) / GRID
                    if block < 3:
                        qkv[rows, block * C + h * 128 : block * C + h * 128 + 128] = piece
                    else:
                        out[rows, h * 128 : h * 128 + 128] = piece

    @pl.when(place[2] == 0)
    def _():
        write((mine, other))

    @pl.when(place[2] == 1)
    def _():
        write((other, mine))


def call(fn, out_shape, scratch, megabytes, microseconds, *args):
    vmem = pl.BlockSpec(memory_space=pltpu.VMEM)
    smem = pl.BlockSpec(memory_space=pltpu.SMEM)
    return pl.pallas_call(
        fn,
        out_shape=tuple(jax.ShapeDtypeStruct(s, d) for s, d in out_shape),
        in_specs=[smem if a.dtype == jnp.int32 else vmem for a in args],
        out_specs=tuple(vmem for _ in out_shape),
        scratch_shapes=[pltpu.VMEM(s, d) for s, d in scratch],
        compiler_params=pltpu.CompilerParams(vmem_limit_bytes=megabytes * 1024 * 1024),
        cost_estimate=pl.CostEstimate(flops=microseconds * 1_000_000_000, bytes_accessed=1_000_000, transcendentals=0),
    )(*args)


OWN = (BR, BC, C)
EXT = (ER, EC, C)
ONES = ((C, C), BF16)


def run_own(place, tokens, cotangent, gain, factor, wqkv, wo):
    mid = ((BR, EC, C), BF16)
    outs = [(OWN, BF16), (OWN, BF16), (OWN, BF16), (OWN, F32), ((ER, KC, NQ), F32), mid, mid, mid, mid]
    return call(own_kernel, outs, [ONES], 12, 3, place, tokens, cotangent, gain, factor, wqkv, wo)


def run_halo(rows, gain, wqkv):
    halo = ((WIN, EC, C), BF16)
    return call(halo_kernel, [halo] * 4, [ONES], 12, 1, rows, gain, wqkv)


def run_attention(place, from_a, from_b, cot, gain, factor, wqkv, own, halo):
    half = (PARTS + 1, 2 * PART, 128)
    to_rows = ((WIN, EC, C), BF16)
    outs = [(half, F32), (half, BF16), (OWN, BF16), (OWN, BF16), ((BR, EC, 2 * C), BF16), to_rows, to_rows]
    scratch = [(EXT, BF16)] * 4 + [(EXT, F32)] * 2 + [(OWN, F32), ((ER, EC, 2 * C), BF16)]
    scratch += [((4 * C, C), F32), ONES]
    return call(attention_kernel, outs, scratch, 28, 9, place, from_a, from_b, cot, gain, factor, wqkv, *own, *halo)


def run_own_grad(place, own, wqkv, wo, att_b, g_q, g_kv_own, from_a, from_b):
    to_cols = ((BR, PAD, C), BF16)
    outs = [(OWN, BF16), (OWN, F32), to_cols, to_cols]
    scratch = [((BR, EC, C), F32)]
    return call(own_grad_kernel, outs, scratch, 12, 3, place, own, wqkv, wo, att_b, g_q, g_kv_own, from_a, from_b)


def run_tokens(place, own, cot, gain, grad_normed, from_a, from_b):
    return call(token_kernel, [(OWN, F32)], [(OWN, F32)], 12, 2, place, own, cot, gain, grad_normed, from_a, from_b)[0]


def run_result(place, mine, other):
    return call(result_kernel, [((C, 3 * C), F32), ((C, C), F32)], [], 8, 1, place, mine, other)


def swap(a, b, axes):
    size = math.prod(AXIS_SIZES[AXES.index(axis)] for axis in axes)
    pairs = [[(i, i + 1) for i in range(at, size - 1, 2)] for at in (1, 0)]
    pairs = [[*some, *((j, i) for i, j in some)] for some in pairs]
    b = lax.ppermute(b, axes, pairs[1])
    return lax.ppermute(a, axes, pairs[0]), b


def body(tokens, norm_gain, qkv_weight, head_scale, out_weight, cotangent):
    row, col = lax.axis_index(ROWS), lax.axis_index(GRP)
    odd_row, odd_col = row % 2, col % 2
    place = jnp.stack([row * BR, col * BC, lax.axis_index("core"), odd_row, odd_col]).astype(jnp.int32)
    gain = norm_gain[None]
    factor = jnp.repeat(head_scale / HEAD, HEAD)[None]
    cores = [(0, 1), (1, 0)]

    rows_a, rows_b = swap(
        lax.dynamic_slice_in_dim(tokens, odd_row, WIN, 0), lax.dynamic_slice_in_dim(tokens, 1 - odd_row, WIN, 0), ROWS
    )
    own = run_own(place, tokens, cotangent, gain, factor, qkv_weight, out_weight)
    edges = [((ER, PAD, C), BF16)] * 2
    cols_a, cols_b = call(edge_kernel, edges, [((ER, PAD, C), F32)] * 2, 8, 1, place, rows_a, rows_b, tokens)
    cols_a, cols_b = swap(cols_a, cols_b, GRP)
    halo = (*run_halo(rows_a, gain, qkv_weight), *run_halo(rows_b, gain, qkv_weight))
    keep, send, att_b, g_q, g_kv_own, rows_a, rows_b = run_attention(
        place, cols_a, cols_b, cotangent, gain, factor, qkv_weight, own, halo
    )

    received = lax.ppermute(send, "core", cores)
    rows = 2 * PART + EXTRA
    (parts,) = call(chip_kernel, [((PARTS, rows, 128), BF16)], [], 8, 1, keep, received)
    parts, rows_a, rows_b = lax.optimization_barrier((parts, rows_a, rows_b))
    parts = lax.all_to_all(parts, SPLIT, 0, 0)
    rows_a, rows_b = swap(rows_a, rows_b, ROWS)
    (copies,) = call(part_kernel, [((RESTS, rows, 128), BF16)], [], 8, 1, parts)
    copies, att_b, g_kv_own = lax.optimization_barrier((copies, att_b, g_kv_own))
    parts = lax.all_to_all(copies, REST, 0, 0)
    out, grad_normed, cols_a, cols_b = run_own_grad(
        place, tokens, qkv_weight, out_weight, att_b, g_q, g_kv_own, rows_a, rows_b
    )
    copies, small = call(whole_kernel, [((PARTS, 2 * PART, 128), BF16), ((EXTRA // 2, 128), F32)], [], 8, 1, parts)
    copies, cols_a, cols_b = lax.optimization_barrier((copies, cols_a, cols_b))
    mine = lax.all_to_all(copies, SPLIT, 0, 0)
    small = small.reshape(2, C)
    scale_grad, gain_grad = small[0].reshape(HEADS, HEAD)[:, 0], small[1]
    cols_a, cols_b = swap(cols_a, cols_b, GRP)
    token_grad = run_tokens(place, tokens, cotangent, gain, grad_normed, cols_a, cols_b)
    mine, token_grad = lax.optimization_barrier((mine, token_grad))
    other = lax.ppermute(mine, "core", cores)
    qkv_grad, out_grad = run_result(place, mine, other)
    return out, token_grad, gain_grad, qkv_grad, scale_grad, out_grad


def solution(mesh):
    fine = Mesh(mesh.devices.reshape(AXIS_SIZES), AXES)
    tiles = P(ROWS, GRP, None)
    return jax.shard_map(
        body,
        mesh=fine,
        in_specs=(tiles, P(), P(), P(), P(), tiles),
        out_specs=(tiles, tiles, P(), P(), P(), P()),
        check_vma=False,
    )
```

```python
import math

import jax
import jax.numpy as jnp
from jax import lax
from jax.experimental import pallas as pl
from jax.experimental.pallas import tpu as pltpu
from jax.sharding import Mesh, PartitionSpec as P

HEADS = 4
HEAD = 64
C = 256
WIN = 3
BR = 4
BC = 128
GRID = 512

EPS = 1e-06

PAD = 8
ER = BR + 2 * WIN
EC = BC + 2 * PAD
QC = 32
KC = 48
BLOCKS = BC // QC
NQ = BR * QC
NK = ER * KC
PAIRS = HEADS // 2
LANES = 2 * HEAD

AXES = ("z", "xh", "y", "xl", "core")
AXIS_SIZES = (8, 2, 8, 2, 2)
ROWS = ("z", "xh", "y")
GRP = ("xl", "core")
SPLIT = ("z", "xh", "xl")
REST = ("y",)
PARTS = 32
RESTS = 8
HALF = 2 * C
PART = HALF // PARTS
EXTRA = 8

F32 = jnp.float32
BF16 = jnp.bfloat16


def mm(a, b, dims=((1,), (0,))):
    return lax.dot_general(a, b, (dims, ((), ())), preferred_element_type=F32)


def split_bf16(a):
    high = a.astype(BF16)
    return high, (a - high.astype(F32)).astype(BF16)


def row_stats(t):
    n = lax.rsqrt(jnp.mean(t * t, axis=-1, keepdims=True) + EPS)
    return n, t * n


def norm_grad(u, n, hat):
    return n * (u - hat * jnp.mean(u * hat, axis=-1, keepdims=True))


def ones_per_head():
    lane_head = lax.broadcasted_iota(jnp.int32, (C, C), 1) // HEAD
    row_head = lax.broadcasted_iota(jnp.int32, (C, C), 0) // HEAD
    return jnp.where(lane_head == row_head, 1.0 / HEAD, 0.0).astype(BF16)


def per_head_mean(a, ones):
    return mm(a.astype(BF16), ones)


def normalise(raw, ones):
    inv = lax.rsqrt(per_head_mean(raw * raw, ones) + EPS)
    return raw * inv, inv


def widen(a, rows):
    edge = jnp.zeros((rows, PAD, C), F32)
    return jnp.concatenate([edge, a.reshape(rows, BC, C), edge], axis=1).astype(BF16)


def own_kernel(
    place, own, cot, gain, factor, wqkv, wo, q_b, d_b, normed_own, q_inv, near_mask, normed_ext, k_b, v_b, k_inv, ones
):
    ones[...] = ones_per_head()

    key_row = lax.broadcasted_iota(jnp.int32, (ER, KC, NQ), 0)
    key_col = lax.broadcasted_iota(jnp.int32, (ER, KC, NQ), 1)
    query = lax.broadcasted_iota(jnp.int32, (ER, KC, NQ), 2)
    row_gap = key_row - query // QC
    col_gap = key_col - query % QC - (PAD - WIN)
    in_rows = (key_row + place[0] - WIN >= 0) & (key_row + place[0] - WIN < GRID)
    near = (row_gap >= 0) & (row_gap <= 2 * WIN) & (col_gap >= 0) & (col_gap <= 2 * WIN)
    near_mask[...] = jnp.where(near & in_rows, 1.0, 0.0)

    @pl.loop(0, BR // 2)
    def _(i):
        rows = pl.ds(2 * i, 2)
        shape = (2, BC, C)
        _, hat = row_stats(own[rows].reshape(2 * BC, C).astype(F32))
        scaled = hat * gain[...]
        normed = scaled.astype(BF16)
        projected = mm(normed, wqkv[...])
        q, inv = normalise(projected[:, :C], ones[...])
        k, inv_k = normalise(projected[:, C : 2 * C], ones[...])
        normed_own[rows] = normed.reshape(shape)
        q_inv[rows] = inv.reshape(shape)
        q_b[rows] = (q * factor[...]).astype(BF16).reshape(shape)
        normed_ext[rows] = widen(scaled, 2)
        k_b[rows] = widen(k, 2)
        k_inv[rows] = widen(inv_k, 2)
        v_b[rows] = widen(projected[:, 2 * C :], 2)
        d = mm(cot[rows].reshape(2 * BC, C), wo[...], ((1,), (1,)))
        d_b[rows] = d.astype(BF16).reshape(shape)


def halo_kernel(rows, gain, wqkv, normed_ext, k_b, v_b, k_inv, ones):
    ones[...] = ones_per_head()
    _, hat = row_stats(rows[...].reshape(WIN * BC, C).astype(F32))
    scaled = hat * gain[...]
    projected = mm(scaled.astype(BF16), wqkv[:, C:])
    k, inv_k = normalise(projected[:, :C], ones[...])
    normed_ext[...] = widen(scaled, WIN)
    k_b[...] = widen(k, WIN)
    k_inv[...] = widen(inv_k, WIN)
    v_b[...] = widen(projected[:, C:], WIN)


def attention_kernel(
    place,
    from_a,
    from_b,
    cot,
    gain,
    factor,
    wqkv,
    q_b,
    d_b,
    normed_own,
    q_inv,
    near_mask,
    normed_mid,
    k_mid,
    v_mid,
    k_inv_mid,
    normed_a,
    k_a,
    v_a,
    k_inv_a,
    normed_b,
    k_from_b,
    v_from_b,
    k_inv_b,
    keep,
    send,
    att_b,
    g_q,
    g_kv_own,
    to_a,
    to_b,
    normed_ext,
    k_b,
    v_b,
    k_inv,
    gk,
    gv,
    gq,
    g_kv,
    acc,
    ones,
):
    ones[...] = ones_per_head()

    odd = place[4] == 1
    left = jnp.where(odd, from_b[...].astype(F32), from_a[...].astype(F32))
    right = jnp.where(odd, from_a[...].astype(F32), from_b[...].astype(F32))
    edges = jnp.concatenate([left, right], axis=0)
    _, hat = row_stats(edges.reshape(2 * ER * PAD, C))
    scaled = hat * gain[...]
    projected = mm(scaled.astype(BF16), wqkv[:, C:])
    k, inv_k = normalise(projected[:, :C], ones[...])
    for ext, mid, halo_a, halo_b, edge in (
        (normed_ext, normed_mid, normed_a, normed_b, scaled),
        (k_b, k_mid, k_a, k_from_b, k),
        (v_b, v_mid, v_a, v_from_b, projected[:, C:]),
        (k_inv, k_inv_mid, k_inv_a, k_inv_b, inv_k),
    ):
        edge = edge.reshape(2 * ER, PAD, C)
        ext[pl.ds(place[3] * (WIN + BR), WIN)] = halo_a[...]
        ext[pl.ds((1 - place[3]) * (WIN + BR), WIN)] = halo_b[...]
        ext[WIN : WIN + BR] = mid[...]
        near = ext[:, 0 : 2 * PAD].astype(F32)[:, PAD:]
        ext[:, 0 : 2 * PAD] = jnp.concatenate([edge[:ER], near], axis=1).astype(BF16)
        near = ext[:, EC - 2 * PAD : EC].astype(F32)[:, :PAD]
        ext[:, EC - 2 * PAD : EC] = jnp.concatenate([near, edge[ER:]], axis=1).astype(BF16)

    gk[...] = jnp.zeros_like(gk)
    gv[...] = jnp.zeros_like(gv)

    first = lax.broadcasted_iota(jnp.int32, (NQ, LANES), 1) < HEAD
    top = lax.broadcasted_iota(jnp.int32, (LANES, NQ), 0) < HEAD

    def both(a):
        zero = jnp.zeros_like(a)
        return jnp.concatenate([jnp.where(first, a, zero), jnp.where(first, zero, a)], axis=0)

    def own_head(a):
        return jnp.where(top, a[:, :NQ], a[:, NQ:]).T

    @pl.loop(0, BLOCKS, unroll=BLOCKS)
    def _(b):
        q_cols = pl.ds(pl.multiple_of(b * QC, QC), QC)
        k_cols = pl.ds(pl.multiple_of(b * QC, QC), KC)
        col = lax.broadcasted_iota(jnp.int32, (ER, KC, NQ), 1) + (place[1] - PAD + b * QC)
        mask = jnp.where((col >= 0) & (col < GRID), near_mask[...], 0.0).reshape(NK, NQ)
        mask = jnp.concatenate([mask, mask], axis=1)
        for p in range(PAIRS):
            lanes = slice(p * LANES, (p + 1) * LANES)
            k2 = k_b[:, k_cols, lanes].reshape(NK, LANES)
            v2 = v_b[:, k_cols, lanes].reshape(NK, LANES)
            q2 = both(q_b[:, q_cols, lanes].reshape(NQ, LANES))
            d2 = both(d_b[:, q_cols, lanes].reshape(NQ, LANES))
            e = jnp.exp(mm(k2, q2, ((1,), (1,)))) * mask
            attend = e * (1.0 / jnp.sum(e, axis=0, keepdims=True))
            attend_b = attend.astype(BF16)
            grad_probs = mm(v2, d2, ((1,), (1,)))
            delta = jnp.sum(attend * grad_probs, axis=0, keepdims=True)
            grad_scores = (attend * (grad_probs - delta)).astype(BF16)
            attended = own_head(mm(v2, attend_b, ((0,), (0,))))
            att_b[:, q_cols, lanes] = attended.astype(BF16).reshape(BR, QC, LANES)
            grad_query = own_head(mm(k2, grad_scores, ((0,), (0,))))
            gq[:, q_cols, lanes] = grad_query.reshape(BR, QC, LANES)
            gk[:, k_cols, lanes] += mm(grad_scores, q2).reshape(ER, KC, LANES)
            gv[:, k_cols, lanes] += mm(attend_b, d2).reshape(ER, KC, LANES)

    inv_factor = 1.0 / factor[...]
    grad_query = gq[...].reshape(BR * BC, C)
    q_f = q_b[...].reshape(BR * BC, C).astype(F32)
    high, low = split_bf16(grad_query * q_f)
    mean = (mm(high, ones[...]) + mm(low, ones[...])) * inv_factor
    scale_sum = jnp.sum(mean, axis=0, keepdims=True)
    g = q_inv[...].reshape(BR * BC, C) * (factor[...] * grad_query - q_f * mean)
    g = g.astype(BF16)
    g_q[...] = g.reshape(BR, BC, C)
    acc[3 * C :] = mm(att_b[...].reshape(BR * BC, C), cot[...].reshape(BR * BC, C), ((0,), (0,)))
    acc[:C] = mm(normed_own[...].reshape(BR * BC, C), g, ((0,), (0,)))

    @pl.loop(0, ER // 2, unroll=ER // 2)
    def _(i):
        rows = pl.ds(2 * i, 2)
        shape = (2, EC, C)
        grad_key = gk[rows].reshape(2 * EC, C)
        k_f = k_b[rows].reshape(2 * EC, C).astype(F32)
        mean = per_head_mean(grad_key * k_f, ones[...])
        g_k = k_inv[rows].reshape(2 * EC, C).astype(F32) * (grad_key - k_f * mean)
        g_kv[rows, :, :C] = g_k.astype(BF16).reshape(shape)
        g_kv[rows, :, C:] = gv[rows].astype(BF16)

    g_kv_own[...] = g_kv[WIN : WIN + BR]
    for ref, at in ((to_a, place[3]), (to_b, 1 - place[3])):
        g = g_kv[pl.ds(at * (WIN + BR), WIN)].reshape(WIN * EC, 2 * C)
        ref[...] = mm(g, wqkv[:, C:], ((1,), (1,))).astype(BF16).reshape(WIN, EC, C)

    acc_kv = mm(normed_ext[...].reshape(ER * EC, C), g_kv[...].reshape(ER * EC, 2 * C), ((0,), (0,)))
    acc[C : 2 * C] = acc_kv[:, :C]
    acc[2 * C : 3 * C] = acc_kv[:, C:]

    by_feature = (
        wqkv[:, :C].astype(F32) * acc[:C]
        + wqkv[:, C : 2 * C].astype(F32) * acc[C : 2 * C]
        + wqkv[:, 2 * C :].astype(F32) * acc[2 * C : 3 * C]
    )
    high, low = split_bf16(by_feature)
    every = jnp.ones((8, C), BF16)
    gain_sum = mm(every, high, ((1,), (1,))) + mm(every, low, ((1,), (1,)))
    gain_sum = gain_sum[0:1] / gain[...]

    for ref, half in ((keep, place[2]), (send, 1 - place[2])):
        for part in range(PARTS):
            rows = pl.ds(pl.multiple_of(half * HALF + part * PART, PART), PART)
            for h in (0, 1):
                piece = acc[rows, h * 128 : h * 128 + 128]
                ref[part, h * PART : h * PART + PART] = piece.astype(ref.dtype)
    small = [part.astype(F32) for part in split_bf16(jnp.concatenate([scale_sum, gain_sum], axis=0))]
    small = [a[i : i + 1, h * 128 : h * 128 + 128] for a in small for i in (0, 1) for h in (0, 1)]
    small = jnp.concatenate(small + [jnp.zeros((2 * PART - EXTRA, 128), F32)], axis=0)
    keep[PARTS] = small
    send[PARTS] = small.astype(BF16)


def own_grad_kernel(
    place, own, wqkv, wo, att_b, g_q, g_kv_own, from_a, from_b, out, grad_normed, to_a, to_b, total
):
    total[...] = mm(g_kv_own[...].reshape(BR * EC, 2 * C), wqkv[:, C:], ((1,), (1,))).reshape(BR, EC, C)
    total[pl.ds(place[3], WIN)] += from_a[...].astype(F32)
    total[pl.ds(1 - place[3], WIN)] += from_b[...].astype(F32)
    left = total[:, :PAD]
    right = total[:, PAD + BC :]
    odd = place[4] == 1
    to_a[...] = jnp.where(odd, right, left).astype(BF16)
    to_b[...] = jnp.where(odd, left, right).astype(BF16)
    by_query = mm(g_q[...].reshape(BR * BC, C), wqkv[:, :C], ((1,), (1,)))
    grad_normed[...] = by_query.reshape(OWN) + total[:, PAD : PAD + BC]
    projected = mm(att_b[...].reshape(BR * BC, C), wo[...])
    out[...] = (own[...].astype(F32) + projected.reshape(OWN)).astype(BF16)


def token_kernel(place, own, cot, gain, grad_normed, from_a, from_b, token_grad, total):
    odd = place[4] == 1
    total[...] = grad_normed[...]
    total[:, :PAD] += jnp.where(odd, from_b[...].astype(F32), from_a[...].astype(F32))
    total[:, BC - PAD :] += jnp.where(odd, from_a[...].astype(F32), from_b[...].astype(F32))
    n, hat = row_stats(own[...].reshape(BR * BC, C).astype(F32))
    grad = norm_grad(gain[...] * total[...].reshape(BR * BC, C), n, hat)
    token_grad[...] = cot[...].astype(F32) + grad.reshape(OWN)


def edge_kernel(place, rows_b, rows_a, own, to_a, to_b, last, first):
    parts = ((rows_a, place[3] * (WIN + BR)), (rows_b, (1 - place[3]) * (WIN + BR)), (own, WIN))
    for ref, at in parts:
        rows = pl.ds(at, ref.shape[0])
        last[rows] = ref[:, BC - 2 * PAD :].astype(F32)[:, PAD:]
        first[rows] = ref[:, : 2 * PAD].astype(F32)[:, :PAD]
    odd = place[4] == 1
    to_a[...] = jnp.where(odd, last[...], first[...]).astype(BF16)
    to_b[...] = jnp.where(odd, first[...], last[...]).astype(BF16)


def resplit(small):
    total = small[: EXTRA // 2] + small[EXTRA // 2 :]
    high, low = split_bf16(total)
    return jnp.concatenate([high.astype(F32), low.astype(F32)], axis=0)


def chip_kernel(keep, received, parts):
    total = keep[:PARTS] + received[:PARTS].astype(F32)
    small = resplit((keep[PARTS] + received[PARTS].astype(F32))[:EXTRA])
    small = jnp.broadcast_to(small[None], (PARTS, EXTRA, 128))
    parts[...] = jnp.concatenate([total, small], axis=1).astype(BF16)


def part_kernel(parts, copies):
    part = jnp.sum(parts[...].astype(F32), axis=0)
    part = jnp.concatenate([part[: 2 * PART], resplit(part[2 * PART :])], axis=0)
    copies[...] = jnp.broadcast_to(part[None], copies.shape).astype(BF16)


def whole_kernel(parts, copies, small):
    part = jnp.sum(parts[...].astype(F32), axis=0)
    copies[...] = jnp.broadcast_to(part[None, : 2 * PART], copies.shape).astype(BF16)
    last = part[2 * PART :]
    small[...] = (last[: EXTRA // 2] + last[EXTRA // 2 :]) / GRID


def result_kernel(place, mine, other, qkv, out):
    def write(halves):
        for block in range(4):
            half = halves[block // 2]
            for part in range(C // PART):
                rows = slice(part * PART, part * PART + PART)
                for h in (0, 1):
                    piece = half[block % 2 * (C // PART) + part, h * PART : h * PART + PART].astype(F32) / GRID
                    if block < 3:
                        qkv[rows, block * C + h * 128 : block * C + h * 128 + 128] = piece
                    else:
                        out[rows, h * 128 : h * 128 + 128] = piece

    @pl.when(place[2] == 0)
    def _():
        write((mine, other))

    @pl.when(place[2] == 1)
    def _():
        write((other, mine))


def call(fn, out_shape, scratch, megabytes, microseconds, *args):
    vmem = pl.BlockSpec(memory_space=pltpu.VMEM)
    smem = pl.BlockSpec(memory_space=pltpu.SMEM)
    return pl.pallas_call(
        fn,
        out_shape=tuple(jax.ShapeDtypeStruct(s, d) for s, d in out_shape),
        in_specs=[smem if a.dtype == jnp.int32 else vmem for a in args],
        out_specs=tuple(vmem for _ in out_shape),
        scratch_shapes=[pltpu.VMEM(s, d) for s, d in scratch],
        compiler_params=pltpu.CompilerParams(vmem_limit_bytes=megabytes * 1024 * 1024),
        cost_estimate=pl.CostEstimate(flops=microseconds * 1_000_000_000, bytes_accessed=1_000_000, transcendentals=0),
    )(*args)


OWN = (BR, BC, C)
EXT = (ER, EC, C)
ONES = ((C, C), BF16)


def run_own(place, tokens, cotangent, gain, factor, wqkv, wo):
    mid = ((BR, EC, C), BF16)
    outs = [(OWN, BF16), (OWN, BF16), (OWN, BF16), (OWN, F32), ((ER, KC, NQ), F32), mid, mid, mid, mid]
    return call(own_kernel, outs, [ONES], 12, 3, place, tokens, cotangent, gain, factor, wqkv, wo)


def run_halo(rows, gain, wqkv):
    halo = ((WIN, EC, C), BF16)
    return call(halo_kernel, [halo] * 4, [ONES], 12, 1, rows, gain, wqkv)


def run_attention(place, from_a, from_b, cot, gain, factor, wqkv, own, halo):
    half = (PARTS + 1, 2 * PART, 128)
    to_rows = ((WIN, EC, C), BF16)
    outs = [(half, F32), (half, BF16), (OWN, BF16), (OWN, BF16), ((BR, EC, 2 * C), BF16), to_rows, to_rows]
    scratch = [(EXT, BF16)] * 4 + [(EXT, F32)] * 2 + [(OWN, F32), ((ER, EC, 2 * C), BF16)]
    scratch += [((4 * C, C), F32), ONES]
    return call(attention_kernel, outs, scratch, 28, 9, place, from_a, from_b, cot, gain, factor, wqkv, *own, *halo)


def run_own_grad(place, own, wqkv, wo, att_b, g_q, g_kv_own, from_a, from_b):
    to_cols = ((BR, PAD, C), BF16)
    outs = [(OWN, BF16), (OWN, F32), to_cols, to_cols]
    scratch = [((BR, EC, C), F32)]
    return call(own_grad_kernel, outs, scratch, 12, 3, place, own, wqkv, wo, att_b, g_q, g_kv_own, from_a, from_b)


def run_tokens(place, own, cot, gain, grad_normed, from_a, from_b):
    return call(token_kernel, [(OWN, F32)], [(OWN, F32)], 12, 2, place, own, cot, gain, grad_normed, from_a, from_b)[0]


def run_result(place, mine, other):
    return call(result_kernel, [((C, 3 * C), F32), ((C, C), F32)], [], 8, 1, place, mine, other)


def swap(a, b, axes):
    size = math.prod(AXIS_SIZES[AXES.index(axis)] for axis in axes)
    pairs = [[(i, i + 1) for i in range(at, size - 1, 2)] for at in (1, 0)]
    pairs = [[*some, *((j, i) for i, j in some)] for some in pairs]
    b = lax.ppermute(b, axes, pairs[1])
    return lax.ppermute(a, axes, pairs[0]), b


def body(tokens, norm_gain, qkv_weight, head_scale, out_weight, cotangent):
    row, col = lax.axis_index(ROWS), lax.axis_index(GRP)
    odd_row, odd_col = row % 2, col % 2
    place = jnp.stack([row * BR, col * BC, lax.axis_index("core"), odd_row, odd_col]).astype(jnp.int32)
    gain = norm_gain[None]
    factor = jnp.repeat(head_scale / HEAD, HEAD)[None]
    cores = [(0, 1), (1, 0)]

    rows_a, rows_b = swap(
        lax.dynamic_slice_in_dim(tokens, odd_row, WIN, 0), lax.dynamic_slice_in_dim(tokens, 1 - odd_row, WIN, 0), ROWS
    )
    own = run_own(place, tokens, cotangent, gain, factor, qkv_weight, out_weight)
    edges = [((ER, PAD, C), BF16)] * 2
    cols_a, cols_b = call(edge_kernel, edges, [((ER, PAD, C), F32)] * 2, 8, 1, place, rows_b, rows_a, tokens)
    cols_a, cols_b = swap(cols_a, cols_b, GRP)
    halo = (*run_halo(rows_a, gain, qkv_weight), *run_halo(rows_b, gain, qkv_weight))
    keep, send, att_b, g_q, g_kv_own, rows_a, rows_b = run_attention(
        place, cols_a, cols_b, cotangent, gain, factor, qkv_weight, own, halo
    )

    received = lax.ppermute(send, "core", cores)
    rows = 2 * PART + EXTRA
    (parts,) = call(chip_kernel, [((PARTS, rows, 128), BF16)], [], 8, 1, keep, received)
    parts, rows_a, rows_b = lax.optimization_barrier((parts, rows_a, rows_b))
    parts = lax.all_to_all(parts, SPLIT, 0, 0)
    rows_a, rows_b = swap(rows_a, rows_b, ROWS)
    (copies,) = call(part_kernel, [((RESTS, rows, 128), BF16)], [], 8, 1, parts)
    copies, att_b, g_kv_own = lax.optimization_barrier((copies, att_b, g_kv_own))
    parts = lax.all_to_all(copies, REST, 0, 0)
    out, grad_normed, cols_a, cols_b = run_own_grad(
        place, tokens, qkv_weight, out_weight, att_b, g_q, g_kv_own, rows_a, rows_b
    )
    copies, small = call(whole_kernel, [((PARTS, 2 * PART, 128), BF16), ((EXTRA // 2, 128), F32)], [], 8, 1, parts)
    copies, cols_a, cols_b = lax.optimization_barrier((copies, cols_a, cols_b))
    mine = lax.all_to_all(copies, SPLIT, 0, 0)
    small = small.reshape(2, C)
    scale_grad, gain_grad = small[0].reshape(HEADS, HEAD)[:, 0], small[1]
    cols_a, cols_b = swap(cols_a, cols_b, GRP)
    token_grad = run_tokens(place, tokens, cotangent, gain, grad_normed, cols_a, cols_b)
    mine, token_grad = lax.optimization_barrier((mine, token_grad))
    other = lax.ppermute(mine, "core", cores)
    qkv_grad, out_grad = run_result(place, mine, other)
    return out, token_grad, gain_grad, qkv_grad, scale_grad, out_grad


def solution(mesh):
    fine = Mesh(mesh.devices.reshape(AXIS_SIZES), AXES)
    tiles = P(ROWS, GRP, None)
    return jax.shard_map(
        body,
        mesh=fine,
        in_specs=(tiles, P(), P(), P(), P(), tiles),
        out_specs=(tiles, tiles, P(), P(), P(), P()),
        check_vma=False,
    )
```

```python
import math

import jax
import jax.numpy as jnp
from jax import lax
from jax.experimental import pallas as pl
from jax.experimental.pallas import tpu as pltpu
from jax.sharding import Mesh, PartitionSpec as P

HEADS = 4
HEAD = 64
C = 256
WIN = 3
BR = 4
BC = 128
GRID = 512

EPS = 1e-06

PAD = 8
ER = BR + 2 * WIN
EC = BC + 2 * PAD
QC = 32
KC = 48
BLOCKS = BC // QC
NQ = BR * QC
NK = ER * KC
PAIRS = HEADS // 2
LANES = 2 * HEAD

AXES = ("z", "xh", "y", "xl", "core")
AXIS_SIZES = (8, 2, 8, 2, 2)
ROWS = ("z", "xh", "y")
GRP = ("xl", "core")
SPLIT = ("xh", "y", "xl")
REST = ("z",)
PARTS = 32
RESTS = 8
HALF = 2 * C
PART = HALF // PARTS
EXTRA = 8

F32 = jnp.float32
BF16 = jnp.bfloat16


def mm(a, b, dims=((1,), (0,))):
    return lax.dot_general(a, b, (dims, ((), ())), preferred_element_type=F32)


def split_bf16(a):
    high = a.astype(BF16)
    return high, (a - high.astype(F32)).astype(BF16)


def row_stats(t):
    n = lax.rsqrt(jnp.mean(t * t, axis=-1, keepdims=True) + EPS)
    return n, t * n


def norm_grad(u, n, hat):
    return n * (u - hat * jnp.mean(u * hat, axis=-1, keepdims=True))


def ones_per_head():
    lane_head = lax.broadcasted_iota(jnp.int32, (C, C), 1) // HEAD
    row_head = lax.broadcasted_iota(jnp.int32, (C, C), 0) // HEAD
    return jnp.where(lane_head == row_head, 1.0 / HEAD, 0.0).astype(BF16)


def per_head_mean(a, ones):
    return mm(a.astype(BF16), ones)


def normalise(raw, ones):
    high, low = split_bf16(raw * raw)
    inv = lax.rsqrt(mm(high, ones) + mm(low, ones) + EPS)
    return raw * inv, inv


def widen(a, rows):
    edge = jnp.zeros((rows, PAD, C), F32)
    return jnp.concatenate([edge, a.reshape(rows, BC, C), edge], axis=1).astype(BF16)


def own_kernel(
    place, own, cot, gain, factor, wqkv, wo, q_b, d_b, normed_own, q_inv, near_mask, normed_ext, k_b, v_b, k_inv, ones
):
    ones[...] = ones_per_head()

    key_row = lax.broadcasted_iota(jnp.int32, (ER, KC, NQ), 0)
    key_col = lax.broadcasted_iota(jnp.int32, (ER, KC, NQ), 1)
    query = lax.broadcasted_iota(jnp.int32, (ER, KC, NQ), 2)
    row_gap = key_row - query // QC
    col_gap = key_col - query % QC - (PAD - WIN)
    in_rows = (key_row + place[0] - WIN >= 0) & (key_row + place[0] - WIN < GRID)
    near = (row_gap >= 0) & (row_gap <= 2 * WIN) & (col_gap >= 0) & (col_gap <= 2 * WIN)
    near_mask[...] = jnp.where(near & in_rows, 1.0, 0.0)

    @pl.loop(0, BR // 2)
    def _(i):
        rows = pl.ds(2 * i, 2)
        shape = (2, BC, C)
        _, hat = row_stats(own[rows].reshape(2 * BC, C).astype(F32))
        scaled = hat * gain[...]
        normed = scaled.astype(BF16)
        projected = mm(normed, wqkv[...])
        q, inv = normalise(projected[:, :C], ones[...])
        k, inv_k = normalise(projected[:, C : 2 * C], ones[...])
        normed_own[rows] = normed.reshape(shape)
        q_inv[rows] = inv.reshape(shape)
        q_b[rows] = (q * factor[...]).astype(BF16).reshape(shape)
        normed_ext[rows] = widen(scaled, 2)
        k_b[rows] = widen(k, 2)
        k_inv[rows] = widen(inv_k, 2)
        v_b[rows] = widen(projected[:, 2 * C :], 2)
        d = mm(cot[rows].reshape(2 * BC, C), wo[...], ((1,), (1,)))
        d_b[rows] = d.astype(BF16).reshape(shape)


def halo_kernel(rows, gain, wqkv, normed_ext, k_b, v_b, k_inv, ones):
    ones[...] = ones_per_head()
    _, hat = row_stats(rows[...].reshape(WIN * BC, C).astype(F32))
    scaled = hat * gain[...]
    projected = mm(scaled.astype(BF16), wqkv[:, C:])
    k, inv_k = normalise(projected[:, :C], ones[...])
    normed_ext[...] = widen(scaled, WIN)
    k_b[...] = widen(k, WIN)
    k_inv[...] = widen(inv_k, WIN)
    v_b[...] = widen(projected[:, C:], WIN)


def attention_kernel(
    place,
    from_a,
    from_b,
    cot,
    gain,
    factor,
    wqkv,
    q_b,
    d_b,
    normed_own,
    q_inv,
    near_mask,
    normed_mid,
    k_mid,
    v_mid,
    k_inv_mid,
    normed_a,
    k_a,
    v_a,
    k_inv_a,
    normed_b,
    k_from_b,
    v_from_b,
    k_inv_b,
    keep,
    send,
    att_b,
    g_q,
    g_kv_own,
    to_a,
    to_b,
    normed_ext,
    k_b,
    v_b,
    k_inv,
    gk,
    gv,
    gq,
    g_kv,
    acc,
    ones,
):
    ones[...] = ones_per_head()

    odd = place[4] == 1
    left = jnp.where(odd, from_b[...].astype(F32), from_a[...].astype(F32))
    right = jnp.where(odd, from_a[...].astype(F32), from_b[...].astype(F32))
    edges = jnp.concatenate([left, right], axis=0)
    _, hat = row_stats(edges.reshape(2 * ER * PAD, C))
    scaled = hat * gain[...]
    projected = mm(scaled.astype(BF16), wqkv[:, C:])
    k, inv_k = normalise(projected[:, :C], ones[...])
    for ext, mid, halo_a, halo_b, edge in (
        (normed_ext, normed_mid, normed_a, normed_b, scaled),
        (k_b, k_mid, k_a, k_from_b, k),
        (v_b, v_mid, v_a, v_from_b, projected[:, C:]),
        (k_inv, k_inv_mid, k_inv_a, k_inv_b, inv_k),
    ):
        edge = edge.reshape(2 * ER, PAD, C)
        ext[pl.ds(place[3] * (WIN + BR), WIN)] = halo_a[...]
        ext[pl.ds((1 - place[3]) * (WIN + BR), WIN)] = halo_b[...]
        ext[WIN : WIN + BR] = mid[...]
        near = ext[:, 0 : 2 * PAD].astype(F32)[:, PAD:]
        ext[:, 0 : 2 * PAD] = jnp.concatenate([edge[:ER], near], axis=1).astype(BF16)
        near = ext[:, EC - 2 * PAD : EC].astype(F32)[:, :PAD]
        ext[:, EC - 2 * PAD : EC] = jnp.concatenate([near, edge[ER:]], axis=1).astype(BF16)

    gk[...] = jnp.zeros_like(gk)
    gv[...] = jnp.zeros_like(gv)

    first = lax.broadcasted_iota(jnp.int32, (NQ, LANES), 1) < HEAD
    top = lax.broadcasted_iota(jnp.int32, (LANES, NQ), 0) < HEAD

    def both(a):
        zero = jnp.zeros_like(a)
        return jnp.concatenate([jnp.where(first, a, zero), jnp.where(first, zero, a)], axis=0)

    def own_head(a):
        return jnp.where(top, a[:, :NQ], a[:, NQ:]).T

    @pl.loop(0, BLOCKS, unroll=BLOCKS)
    def _(b):
        q_cols = pl.ds(pl.multiple_of(b * QC, QC), QC)
        k_cols = pl.ds(pl.multiple_of(b * QC, QC), KC)
        col = lax.broadcasted_iota(jnp.int32, (ER, KC, NQ), 1) + (place[1] - PAD + b * QC)
        mask = jnp.where((col >= 0) & (col < GRID), near_mask[...], 0.0).reshape(NK, NQ)
        mask = jnp.concatenate([mask, mask], axis=1)
        for p in range(PAIRS):
            lanes = slice(p * LANES, (p + 1) * LANES)
            k2 = k_b[:, k_cols, lanes].reshape(NK, LANES)
            v2 = v_b[:, k_cols, lanes].reshape(NK, LANES)
            q2 = both(q_b[:, q_cols, lanes].reshape(NQ, LANES))
            d2 = both(d_b[:, q_cols, lanes].reshape(NQ, LANES))
            e = jnp.exp(mm(k2, q2, ((1,), (1,)))) * mask
            attend = e * (1.0 / jnp.sum(e, axis=0, keepdims=True))
            attend_b = attend.astype(BF16)
            grad_probs = mm(v2, d2, ((1,), (1,)))
            delta = jnp.sum(attend * grad_probs, axis=0, keepdims=True)
            grad_scores = (attend * (grad_probs - delta)).astype(BF16)
            attended = own_head(mm(v2, attend_b, ((0,), (0,))))
            att_b[:, q_cols, lanes] = attended.astype(BF16).reshape(BR, QC, LANES)
            grad_query = own_head(mm(k2, grad_scores, ((0,), (0,))))
            gq[:, q_cols, lanes] = grad_query.reshape(BR, QC, LANES)
            gk[:, k_cols, lanes] += mm(grad_scores, q2).reshape(ER, KC, LANES)
            gv[:, k_cols, lanes] += mm(attend_b, d2).reshape(ER, KC, LANES)

    inv_factor = 1.0 / factor[...]
    grad_query = gq[...].reshape(BR * BC, C)
    q_f = q_b[...].reshape(BR * BC, C).astype(F32)
    high, low = split_bf16(grad_query * q_f)
    mean = (mm(high, ones[...]) + mm(low, ones[...])) * inv_factor
    scale_sum = jnp.sum(mean, axis=0, keepdims=True)
    g = q_inv[...].reshape(BR * BC, C) * (factor[...] * grad_query - q_f * mean)
    g = g.astype(BF16)
    g_q[...] = g.reshape(BR, BC, C)
    acc[3 * C :] = mm(att_b[...].reshape(BR * BC, C), cot[...].reshape(BR * BC, C), ((0,), (0,)))
    acc[:C] = mm(normed_own[...].reshape(BR * BC, C), g, ((0,), (0,)))

    @pl.loop(0, ER // 2, unroll=ER // 2)
    def _(i):
        rows = pl.ds(2 * i, 2)
        shape = (2, EC, C)
        grad_key = gk[rows].reshape(2 * EC, C)
        k_f = k_b[rows].reshape(2 * EC, C).astype(F32)
        mean = per_head_mean(grad_key * k_f, ones[...])
        g_k = k_inv[rows].reshape(2 * EC, C).astype(F32) * (grad_key - k_f * mean)
        g_kv[rows, :, :C] = g_k.astype(BF16).reshape(shape)
        g_kv[rows, :, C:] = gv[rows].astype(BF16)

    g_kv_own[...] = g_kv[WIN : WIN + BR]
    for ref, at in ((to_a, place[3]), (to_b, 1 - place[3])):
        g = g_kv[pl.ds(at * (WIN + BR), WIN)].reshape(WIN * EC, 2 * C)
        ref[...] = mm(g, wqkv[:, C:], ((1,), (1,))).astype(BF16).reshape(WIN, EC, C)

    acc_kv = mm(normed_ext[...].reshape(ER * EC, C), g_kv[...].reshape(ER * EC, 2 * C), ((0,), (0,)))
    acc[C : 2 * C] = acc_kv[:, :C]
    acc[2 * C : 3 * C] = acc_kv[:, C:]

    by_feature = (
        wqkv[:, :C].astype(F32) * acc[:C]
        + wqkv[:, C : 2 * C].astype(F32) * acc[C : 2 * C]
        + wqkv[:, 2 * C :].astype(F32) * acc[2 * C : 3 * C]
    )
    high, low = split_bf16(by_feature)
    every = jnp.ones((8, C), BF16)
    gain_sum = mm(every, high, ((1,), (1,))) + mm(every, low, ((1,), (1,)))
    gain_sum = gain_sum[0:1] / gain[...]

    for ref, half in ((keep, place[2]), (send, 1 - place[2])):
        for part in range(PARTS):
            rows = pl.ds(pl.multiple_of(half * HALF + part * PART, PART), PART)
            for h in (0, 1):
                piece = acc[rows, h * 128 : h * 128 + 128]
                ref[part, h * PART : h * PART + PART] = piece.astype(ref.dtype)
    small = [part.astype(F32) for part in split_bf16(jnp.concatenate([scale_sum, gain_sum], axis=0))]
    small = [a[i : i + 1, h * 128 : h * 128 + 128] for a in small for i in (0, 1) for h in (0, 1)]
    small = jnp.concatenate(small + [jnp.zeros((2 * PART - EXTRA, 128), F32)], axis=0)
    keep[PARTS] = small
    send[PARTS] = small.astype(BF16)


def own_grad_kernel(
    place, own, wqkv, wo, att_b, g_q, g_kv_own, from_a, from_b, out, grad_normed, to_a, to_b, total
):
    total[...] = mm(g_kv_own[...].reshape(BR * EC, 2 * C), wqkv[:, C:], ((1,), (1,))).reshape(BR, EC, C)
    total[pl.ds(place[3], WIN)] += from_a[...].astype(F32)
    total[pl.ds(1 - place[3], WIN)] += from_b[...].astype(F32)
    left = total[:, :PAD]
    right = total[:, PAD + BC :]
    odd = place[4] == 1
    to_a[...] = jnp.where(odd, right, left).astype(BF16)
    to_b[...] = jnp.where(odd, left, right).astype(BF16)
    by_query = mm(g_q[...].reshape(BR * BC, C), wqkv[:, :C], ((1,), (1,)))
    grad_normed[...] = by_query.reshape(OWN) + total[:, PAD : PAD + BC]
    projected = mm(att_b[...].reshape(BR * BC, C), wo[...])
    out[...] = (own[...].astype(F32) + projected.reshape(OWN)).astype(BF16)


def token_kernel(place, own, cot, gain, grad_normed, from_a, from_b, token_grad, total):
    odd = place[4] == 1
    total[...] = grad_normed[...]
    total[:, :PAD] += jnp.where(odd, from_b[...].astype(F32), from_a[...].astype(F32))
    total[:, BC - PAD :] += jnp.where(odd, from_a[...].astype(F32), from_b[...].astype(F32))
    n, hat = row_stats(own[...].reshape(BR * BC, C).astype(F32))
    grad = norm_grad(gain[...] * total[...].reshape(BR * BC, C), n, hat)
    token_grad[...] = cot[...].astype(F32) + grad.reshape(OWN)


def edge_kernel(place, rows_b, rows_a, own, to_a, to_b, last, first):
    parts = ((rows_a, place[3] * (WIN + BR)), (rows_b, (1 - place[3]) * (WIN + BR)), (own, WIN))
    for ref, at in parts:
        rows = pl.ds(at, ref.shape[0])
        last[rows] = ref[:, BC - 2 * PAD :].astype(F32)[:, PAD:]
        first[rows] = ref[:, : 2 * PAD].astype(F32)[:, :PAD]
    odd = place[4] == 1
    to_a[...] = jnp.where(odd, last[...], first[...]).astype(BF16)
    to_b[...] = jnp.where(odd, first[...], last[...]).astype(BF16)


def resplit(small):
    total = small[: EXTRA // 2] + small[EXTRA // 2 :]
    high, low = split_bf16(total)
    return jnp.concatenate([high.astype(F32), low.astype(F32)], axis=0)


def chip_kernel(keep, received, parts):
    total = keep[:PARTS] + received[:PARTS].astype(F32)
    small = resplit((keep[PARTS] + received[PARTS].astype(F32))[:EXTRA])
    small = jnp.broadcast_to(small[None], (PARTS, EXTRA, 128))
    parts[...] = jnp.concatenate([total, small], axis=1).astype(BF16)


def part_kernel(parts, copies):
    part = jnp.sum(parts[...].astype(F32), axis=0)
    part = jnp.concatenate([part[: 2 * PART], resplit(part[2 * PART :])], axis=0)
    copies[...] = jnp.broadcast_to(part[None], copies.shape).astype(BF16)


def whole_kernel(parts, copies, small):
    part = jnp.sum(parts[...].astype(F32), axis=0)
    copies[...] = jnp.broadcast_to(part[None, : 2 * PART], copies.shape).astype(BF16)
    last = part[2 * PART :]
    small[...] = (last[: EXTRA // 2] + last[EXTRA // 2 :]) / GRID


def result_kernel(place, mine, other, qkv, out):
    def write(halves):
        for block in range(4):
            half = halves[block // 2]
            for part in range(C // PART):
                rows = slice(part * PART, part * PART + PART)
                for h in (0, 1):
                    piece = half[block % 2 * (C // PART) + part, h * PART : h * PART + PART].astype(F32) / GRID
                    if block < 3:
                        qkv[rows, block * C + h * 128 : block * C + h * 128 + 128] = piece
                    else:
                        out[rows, h * 128 : h * 128 + 128] = piece

    @pl.when(place[2] == 0)
    def _():
        write((mine, other))

    @pl.when(place[2] == 1)
    def _():
        write((other, mine))


def call(fn, out_shape, scratch, megabytes, microseconds, *args):
    vmem = pl.BlockSpec(memory_space=pltpu.VMEM)
    smem = pl.BlockSpec(memory_space=pltpu.SMEM)
    return pl.pallas_call(
        fn,
        out_shape=tuple(jax.ShapeDtypeStruct(s, d) for s, d in out_shape),
        in_specs=[smem if a.dtype == jnp.int32 else vmem for a in args],
        out_specs=tuple(vmem for _ in out_shape),
        scratch_shapes=[pltpu.VMEM(s, d) for s, d in scratch],
        compiler_params=pltpu.CompilerParams(vmem_limit_bytes=megabytes * 1024 * 1024),
        cost_estimate=pl.CostEstimate(flops=microseconds * 1_000_000_000, bytes_accessed=1_000_000, transcendentals=0),
    )(*args)


OWN = (BR, BC, C)
EXT = (ER, EC, C)
ONES = ((C, C), BF16)


def run_own(place, tokens, cotangent, gain, factor, wqkv, wo):
    mid = ((BR, EC, C), BF16)
    outs = [(OWN, BF16), (OWN, BF16), (OWN, BF16), (OWN, F32), ((ER, KC, NQ), F32), mid, mid, mid, mid]
    return call(own_kernel, outs, [ONES], 12, 3, place, tokens, cotangent, gain, factor, wqkv, wo)


def run_halo(rows, gain, wqkv):
    halo = ((WIN, EC, C), BF16)
    return call(halo_kernel, [halo] * 4, [ONES], 12, 1, rows, gain, wqkv)


def run_attention(place, from_a, from_b, cot, gain, factor, wqkv, own, halo):
    half = (PARTS + 1, 2 * PART, 128)
    to_rows = ((WIN, EC, C), BF16)
    outs = [(half, F32), (half, BF16), (OWN, BF16), (OWN, BF16), ((BR, EC, 2 * C), BF16), to_rows, to_rows]
    scratch = [(EXT, BF16)] * 4 + [(EXT, F32)] * 2 + [(OWN, F32), ((ER, EC, 2 * C), BF16)]
    scratch += [((4 * C, C), F32), ONES]
    return call(attention_kernel, outs, scratch, 28, 9, place, from_a, from_b, cot, gain, factor, wqkv, *own, *halo)


def run_own_grad(place, own, wqkv, wo, att_b, g_q, g_kv_own, from_a, from_b):
    to_cols = ((BR, PAD, C), BF16)
    outs = [(OWN, BF16), (OWN, F32), to_cols, to_cols]
    scratch = [((BR, EC, C), F32)]
    return call(own_grad_kernel, outs, scratch, 12, 3, place, own, wqkv, wo, att_b, g_q, g_kv_own, from_a, from_b)


def run_tokens(place, own, cot, gain, grad_normed, from_a, from_b):
    return call(token_kernel, [(OWN, F32)], [(OWN, F32)], 12, 2, place, own, cot, gain, grad_normed, from_a, from_b)[0]


def run_result(place, mine, other):
    return call(result_kernel, [((C, 3 * C), F32), ((C, C), F32)], [], 8, 1, place, mine, other)


def swap(a, b, axes):
    size = math.prod(AXIS_SIZES[AXES.index(axis)] for axis in axes)
    pairs = [[(i, i + 1) for i in range(at, size - 1, 2)] for at in (1, 0)]
    pairs = [[*some, *((j, i) for i, j in some)] for some in pairs]
    b = lax.ppermute(b, axes, pairs[1])
    return lax.ppermute(a, axes, pairs[0]), b


def body(tokens, norm_gain, qkv_weight, head_scale, out_weight, cotangent):
    row, col = lax.axis_index(ROWS), lax.axis_index(GRP)
    odd_row, odd_col = row % 2, col % 2
    place = jnp.stack([row * BR, col * BC, lax.axis_index("core"), odd_row, odd_col]).astype(jnp.int32)
    gain = norm_gain[None]
    factor = jnp.repeat(head_scale / HEAD, HEAD)[None]
    cores = [(0, 1), (1, 0)]

    rows_a, rows_b = swap(
        lax.dynamic_slice_in_dim(tokens, odd_row, WIN, 0), lax.dynamic_slice_in_dim(tokens, 1 - odd_row, WIN, 0), ROWS
    )
    own = run_own(place, tokens, cotangent, gain, factor, qkv_weight, out_weight)
    edges = [((ER, PAD, C), BF16)] * 2
    cols_a, cols_b = call(edge_kernel, edges, [((ER, PAD, C), F32)] * 2, 8, 1, place, rows_b, rows_a, tokens)
    cols_a, cols_b = swap(cols_a, cols_b, GRP)
    halo = (*run_halo(rows_a, gain, qkv_weight), *run_halo(rows_b, gain, qkv_weight))
    keep, send, att_b, g_q, g_kv_own, rows_a, rows_b = run_attention(
        place, cols_a, cols_b, cotangent, gain, factor, qkv_weight, own, halo
    )

    received = lax.ppermute(send, "core", cores)
    rows = 2 * PART + EXTRA
    (parts,) = call(chip_kernel, [((PARTS, rows, 128), BF16)], [], 8, 1, keep, received)
    parts, rows_a, rows_b = lax.optimization_barrier((parts, rows_a, rows_b))
    parts = lax.all_to_all(parts, SPLIT, 0, 0)
    rows_a, rows_b = swap(rows_a, rows_b, ROWS)
    (copies,) = call(part_kernel, [((RESTS, rows, 128), BF16)], [], 8, 1, parts)
    copies, att_b, g_kv_own = lax.optimization_barrier((copies, att_b, g_kv_own))
    parts = lax.all_to_all(copies, REST, 0, 0)
    out, grad_normed, cols_a, cols_b = run_own_grad(
        place, tokens, qkv_weight, out_weight, att_b, g_q, g_kv_own, rows_a, rows_b
    )
    copies, small = call(whole_kernel, [((PARTS, 2 * PART, 128), BF16), ((EXTRA // 2, 128), F32)], [], 8, 1, parts)
    copies, cols_a, cols_b = lax.optimization_barrier((copies, cols_a, cols_b))
    mine = lax.all_to_all(copies, SPLIT, 0, 0)
    small = small.reshape(2, C)
    scale_grad, gain_grad = small[0].reshape(HEADS, HEAD)[:, 0], small[1]
    cols_a, cols_b = swap(cols_a, cols_b, GRP)
    token_grad = run_tokens(place, tokens, cotangent, gain, grad_normed, cols_a, cols_b)
    mine, token_grad = lax.optimization_barrier((mine, token_grad))
    other = lax.ppermute(mine, "core", cores)
    qkv_grad, out_grad = run_result(place, mine, other)
    return out, token_grad, gain_grad, qkv_grad, scale_grad, out_grad


def solution(mesh):
    fine = Mesh(mesh.devices.reshape(AXIS_SIZES), AXES)
    tiles = P(ROWS, GRP, None)
    return jax.shard_map(
        body,
        mesh=fine,
        in_specs=(tiles, P(), P(), P(), P(), tiles),
        out_specs=(tiles, tiles, P(), P(), P(), P()),
        check_vma=False,
    )
```

```python
import math

import jax
import jax.numpy as jnp
from jax import lax
from jax.experimental import pallas as pl
from jax.experimental.pallas import tpu as pltpu
from jax.sharding import Mesh, PartitionSpec as P

HEADS = 4
HEAD = 64
C = 256
WIN = 3
BR = 4
BC = 128
GRID = 512

EPS = 1e-06

PAD = 8
ER = BR + 2 * WIN
EC = BC + 2 * PAD
QC = 32
KC = 48
BLOCKS = BC // QC
NQ = BR * QC
NK = ER * KC
PAIRS = HEADS // 2
LANES = 2 * HEAD

AXES = ("z", "xh", "y", "xl", "core")
AXIS_SIZES = (8, 2, 8, 2, 2)
ROWS = ("z", "xh", "y")
GRP = ("xl", "core")
SPLIT = ("xl", "xh", "y")
REST = ("z",)
PARTS = 32
RESTS = 8
HALF = 2 * C
PART = HALF // PARTS
EXTRA = 8

F32 = jnp.float32
BF16 = jnp.bfloat16


def mm(a, b, dims=((1,), (0,))):
    return lax.dot_general(a, b, (dims, ((), ())), preferred_element_type=F32)


def split_bf16(a):
    high = a.astype(BF16)
    return high, (a - high.astype(F32)).astype(BF16)


def row_stats(t):
    n = lax.rsqrt(jnp.mean(t * t, axis=-1, keepdims=True) + EPS)
    return n, t * n


def norm_grad(u, n, hat):
    return n * (u - hat * jnp.mean(u * hat, axis=-1, keepdims=True))


def ones_per_head():
    lane_head = lax.broadcasted_iota(jnp.int32, (C, C), 1) // HEAD
    row_head = lax.broadcasted_iota(jnp.int32, (C, C), 0) // HEAD
    return jnp.where(lane_head == row_head, 1.0 / HEAD, 0.0).astype(BF16)


def per_head_mean(a, ones):
    return mm(a.astype(BF16), ones)


def normalise(raw, ones):
    high, low = split_bf16(raw * raw)
    inv = lax.rsqrt(mm(high, ones) + mm(low, ones) + EPS)
    return raw * inv, inv


def widen(a, rows):
    edge = jnp.zeros((rows, PAD, C), F32)
    return jnp.concatenate([edge, a.reshape(rows, BC, C), edge], axis=1).astype(BF16)


def own_kernel(
    place, own, cot, gain, factor, wqkv, wo, q_b, d_b, normed_own, q_inv, near_mask, normed_ext, k_b, v_b, k_inv, ones
):
    ones[...] = ones_per_head()

    key_row = lax.broadcasted_iota(jnp.int32, (ER, KC, NQ), 0)
    key_col = lax.broadcasted_iota(jnp.int32, (ER, KC, NQ), 1)
    query = lax.broadcasted_iota(jnp.int32, (ER, KC, NQ), 2)
    row_gap = key_row - query // QC
    col_gap = key_col - query % QC - (PAD - WIN)
    in_rows = (key_row + place[0] - WIN >= 0) & (key_row + place[0] - WIN < GRID)
    near = (row_gap >= 0) & (row_gap <= 2 * WIN) & (col_gap >= 0) & (col_gap <= 2 * WIN)
    near_mask[...] = jnp.where(near & in_rows, 1.0, 0.0)

    @pl.loop(0, BR // 2)
    def _(i):
        rows = pl.ds(2 * i, 2)
        shape = (2, BC, C)
        _, hat = row_stats(own[rows].reshape(2 * BC, C).astype(F32))
        scaled = hat * gain[...]
        normed = scaled.astype(BF16)
        projected = mm(normed, wqkv[...])
        q, inv = normalise(projected[:, :C], ones[...])
        k, inv_k = normalise(projected[:, C : 2 * C], ones[...])
        normed_own[rows] = normed.reshape(shape)
        q_inv[rows] = inv.reshape(shape)
        q_b[rows] = (q * factor[...]).astype(BF16).reshape(shape)
        normed_ext[rows] = widen(scaled, 2)
        k_b[rows] = widen(k, 2)
        k_inv[rows] = widen(inv_k, 2)
        v_b[rows] = widen(projected[:, 2 * C :], 2)
        d = mm(cot[rows].reshape(2 * BC, C), wo[...], ((1,), (1,)))
        d_b[rows] = d.astype(BF16).reshape(shape)


def halo_kernel(rows, gain, wqkv, normed_ext, k_b, v_b, k_inv, ones):
    ones[...] = ones_per_head()
    _, hat = row_stats(rows[...].reshape(WIN * BC, C).astype(F32))
    scaled = hat * gain[...]
    projected = mm(scaled.astype(BF16), wqkv[:, C:])
    k, inv_k = normalise(projected[:, :C], ones[...])
    normed_ext[...] = widen(scaled, WIN)
    k_b[...] = widen(k, WIN)
    k_inv[...] = widen(inv_k, WIN)
    v_b[...] = widen(projected[:, C:], WIN)


def attention_kernel(
    place,
    from_a,
    from_b,
    cot,
    gain,
    factor,
    wqkv,
    q_b,
    d_b,
    normed_own,
    q_inv,
    near_mask,
    normed_mid,
    k_mid,
    v_mid,
    k_inv_mid,
    normed_a,
    k_a,
    v_a,
    k_inv_a,
    normed_b,
    k_from_b,
    v_from_b,
    k_inv_b,
    keep,
    send,
    att_b,
    g_q,
    g_kv_own,
    to_a,
    to_b,
    normed_ext,
    k_b,
    v_b,
    k_inv,
    gk,
    gv,
    gq,
    g_kv,
    acc,
    ones,
):
    ones[...] = ones_per_head()

    odd = place[4] == 1
    left = jnp.where(odd, from_b[...].astype(F32), from_a[...].astype(F32))
    right = jnp.where(odd, from_a[...].astype(F32), from_b[...].astype(F32))
    edges = jnp.concatenate([left, right], axis=0)
    _, hat = row_stats(edges.reshape(2 * ER * PAD, C))
    scaled = hat * gain[...]
    projected = mm(scaled.astype(BF16), wqkv[:, C:])
    k, inv_k = normalise(projected[:, :C], ones[...])
    for ext, mid, halo_a, halo_b, edge in (
        (normed_ext, normed_mid, normed_a, normed_b, scaled),
        (k_b, k_mid, k_a, k_from_b, k),
        (v_b, v_mid, v_a, v_from_b, projected[:, C:]),
        (k_inv, k_inv_mid, k_inv_a, k_inv_b, inv_k),
    ):
        edge = edge.reshape(2 * ER, PAD, C)
        ext[pl.ds(place[3] * (WIN + BR), WIN)] = halo_a[...]
        ext[pl.ds((1 - place[3]) * (WIN + BR), WIN)] = halo_b[...]
        ext[WIN : WIN + BR] = mid[...]
        near = ext[:, 0 : 2 * PAD].astype(F32)[:, PAD:]
        ext[:, 0 : 2 * PAD] = jnp.concatenate([edge[:ER], near], axis=1).astype(BF16)
        near = ext[:, EC - 2 * PAD : EC].astype(F32)[:, :PAD]
        ext[:, EC - 2 * PAD : EC] = jnp.concatenate([near, edge[ER:]], axis=1).astype(BF16)

    gk[...] = jnp.zeros_like(gk)
    gv[...] = jnp.zeros_like(gv)

    first = lax.broadcasted_iota(jnp.int32, (NQ, LANES), 1) < HEAD
    top = lax.broadcasted_iota(jnp.int32, (LANES, NQ), 0) < HEAD

    def both(a):
        zero = jnp.zeros_like(a)
        return jnp.concatenate([jnp.where(first, a, zero), jnp.where(first, zero, a)], axis=0)

    def own_head(a):
        return jnp.where(top, a[:, :NQ], a[:, NQ:]).T

    @pl.loop(0, BLOCKS, unroll=BLOCKS)
    def _(b):
        q_cols = pl.ds(pl.multiple_of(b * QC, QC), QC)
        k_cols = pl.ds(pl.multiple_of(b * QC, QC), KC)
        col = lax.broadcasted_iota(jnp.int32, (ER, KC, NQ), 1) + (place[1] - PAD + b * QC)
        mask = jnp.where((col >= 0) & (col < GRID), near_mask[...], 0.0).reshape(NK, NQ)
        mask = jnp.concatenate([mask, mask], axis=1)
        for p in range(PAIRS):
            lanes = slice(p * LANES, (p + 1) * LANES)
            k2 = k_b[:, k_cols, lanes].reshape(NK, LANES)
            v2 = v_b[:, k_cols, lanes].reshape(NK, LANES)
            q2 = both(q_b[:, q_cols, lanes].reshape(NQ, LANES))
            d2 = both(d_b[:, q_cols, lanes].reshape(NQ, LANES))
            e = jnp.exp(mm(k2, q2, ((1,), (1,)))) * mask
            attend = e * (1.0 / jnp.sum(e, axis=0, keepdims=True))
            attend_b = attend.astype(BF16)
            grad_probs = mm(v2, d2, ((1,), (1,)))
            delta = jnp.sum(attend * grad_probs, axis=0, keepdims=True)
            grad_scores = (attend * (grad_probs - delta)).astype(BF16)
            attended = own_head(mm(v2, attend_b, ((0,), (0,))))
            att_b[:, q_cols, lanes] = attended.astype(BF16).reshape(BR, QC, LANES)
            grad_query = own_head(mm(k2, grad_scores, ((0,), (0,))))
            gq[:, q_cols, lanes] = grad_query.reshape(BR, QC, LANES)
            gk[:, k_cols, lanes] += mm(grad_scores, q2).reshape(ER, KC, LANES)
            gv[:, k_cols, lanes] += mm(attend_b, d2).reshape(ER, KC, LANES)

    inv_factor = 1.0 / factor[...]
    grad_query = gq[...].reshape(BR * BC, C)
    q_f = q_b[...].reshape(BR * BC, C).astype(F32)
    high, low = split_bf16(grad_query * q_f)
    mean = (mm(high, ones[...]) + mm(low, ones[...])) * inv_factor
    scale_sum = jnp.sum(mean, axis=0, keepdims=True)
    g = q_inv[...].reshape(BR * BC, C) * (factor[...] * grad_query - q_f * mean)
    g = g.astype(BF16)
    g_q[...] = g.reshape(BR, BC, C)
    acc[3 * C :] = mm(att_b[...].reshape(BR * BC, C), cot[...].reshape(BR * BC, C), ((0,), (0,)))
    acc[:C] = mm(normed_own[...].reshape(BR * BC, C), g, ((0,), (0,)))

    @pl.loop(0, ER // 2, unroll=ER // 2)
    def _(i):
        rows = pl.ds(2 * i, 2)
        shape = (2, EC, C)
        grad_key = gk[rows].reshape(2 * EC, C)
        k_f = k_b[rows].reshape(2 * EC, C).astype(F32)
        mean = per_head_mean(grad_key * k_f, ones[...])
        g_k = k_inv[rows].reshape(2 * EC, C).astype(F32) * (grad_key - k_f * mean)
        g_kv[rows, :, :C] = g_k.astype(BF16).reshape(shape)
        g_kv[rows, :, C:] = gv[rows].astype(BF16)

    g_kv_own[...] = g_kv[WIN : WIN + BR]
    for ref, at in ((to_a, place[3]), (to_b, 1 - place[3])):
        g = g_kv[pl.ds(at * (WIN + BR), WIN)].reshape(WIN * EC, 2 * C)
        ref[...] = mm(g, wqkv[:, C:], ((1,), (1,))).astype(BF16).reshape(WIN, EC, C)

    acc_kv = mm(normed_ext[...].reshape(ER * EC, C), g_kv[...].reshape(ER * EC, 2 * C), ((0,), (0,)))
    acc[C : 2 * C] = acc_kv[:, :C]
    acc[2 * C : 3 * C] = acc_kv[:, C:]

    by_feature = (
        wqkv[:, :C].astype(F32) * acc[:C]
        + wqkv[:, C : 2 * C].astype(F32) * acc[C : 2 * C]
        + wqkv[:, 2 * C :].astype(F32) * acc[2 * C : 3 * C]
    )
    high, low = split_bf16(by_feature)
    every = jnp.ones((8, C), BF16)
    gain_sum = mm(every, high, ((1,), (1,))) + mm(every, low, ((1,), (1,)))
    gain_sum = gain_sum[0:1] / gain[...]

    for ref, half in ((keep, place[2]), (send, 1 - place[2])):
        for part in range(PARTS):
            rows = pl.ds(pl.multiple_of(half * HALF + part * PART, PART), PART)
            for h in (0, 1):
                piece = acc[rows, h * 128 : h * 128 + 128]
                ref[part, h * PART : h * PART + PART] = piece.astype(ref.dtype)
    small = [part.astype(F32) for part in split_bf16(jnp.concatenate([scale_sum, gain_sum], axis=0))]
    small = [a[i : i + 1, h * 128 : h * 128 + 128] for a in small for i in (0, 1) for h in (0, 1)]
    small = jnp.concatenate(small + [jnp.zeros((2 * PART - EXTRA, 128), F32)], axis=0)
    keep[PARTS] = small
    send[PARTS] = small.astype(BF16)


def own_grad_kernel(
    place, own, wqkv, wo, att_b, g_q, g_kv_own, from_a, from_b, out, grad_normed, to_a, to_b, total
):
    total[...] = mm(g_kv_own[...].reshape(BR * EC, 2 * C), wqkv[:, C:], ((1,), (1,))).reshape(BR, EC, C)
    total[pl.ds(place[3], WIN)] += from_a[...].astype(F32)
    total[pl.ds(1 - place[3], WIN)] += from_b[...].astype(F32)
    left = total[:, :PAD]
    right = total[:, PAD + BC :]
    odd = place[4] == 1
    to_a[...] = jnp.where(odd, right, left).astype(BF16)
    to_b[...] = jnp.where(odd, left, right).astype(BF16)
    by_query = mm(g_q[...].reshape(BR * BC, C), wqkv[:, :C], ((1,), (1,)))
    grad_normed[...] = by_query.reshape(OWN) + total[:, PAD : PAD + BC]
    projected = mm(att_b[...].reshape(BR * BC, C), wo[...])
    out[...] = (own[...].astype(F32) + projected.reshape(OWN)).astype(BF16)


def token_kernel(place, own, cot, gain, grad_normed, from_a, from_b, token_grad, total):
    odd = place[4] == 1
    total[...] = grad_normed[...]
    total[:, :PAD] += jnp.where(odd, from_b[...].astype(F32), from_a[...].astype(F32))
    total[:, BC - PAD :] += jnp.where(odd, from_a[...].astype(F32), from_b[...].astype(F32))
    n, hat = row_stats(own[...].reshape(BR * BC, C).astype(F32))
    grad = norm_grad(gain[...] * total[...].reshape(BR * BC, C), n, hat)
    token_grad[...] = cot[...].astype(F32) + grad.reshape(OWN)


def edge_kernel(place, rows_b, rows_a, own, to_a, to_b, last, first):
    parts = ((rows_a, place[3] * (WIN + BR)), (rows_b, (1 - place[3]) * (WIN + BR)), (own, WIN))
    for ref, at in parts:
        rows = pl.ds(at, ref.shape[0])
        last[rows] = ref[:, BC - 2 * PAD :].astype(F32)[:, PAD:]
        first[rows] = ref[:, : 2 * PAD].astype(F32)[:, :PAD]
    odd = place[4] == 1
    to_a[...] = jnp.where(odd, last[...], first[...]).astype(BF16)
    to_b[...] = jnp.where(odd, first[...], last[...]).astype(BF16)


def resplit(small):
    total = small[: EXTRA // 2] + small[EXTRA // 2 :]
    high, low = split_bf16(total)
    return jnp.concatenate([high.astype(F32), low.astype(F32)], axis=0)


def chip_kernel(keep, received, parts):
    total = keep[:PARTS] + received[:PARTS].astype(F32)
    small = resplit((keep[PARTS] + received[PARTS].astype(F32))[:EXTRA])
    small = jnp.broadcast_to(small[None], (PARTS, EXTRA, 128))
    parts[...] = jnp.concatenate([total, small], axis=1).astype(BF16)


def part_kernel(parts, copies):
    part = jnp.sum(parts[...].astype(F32), axis=0)
    part = jnp.concatenate([part[: 2 * PART], resplit(part[2 * PART :])], axis=0)
    copies[...] = jnp.broadcast_to(part[None], copies.shape).astype(BF16)


def whole_kernel(parts, copies, small):
    part = jnp.sum(parts[...].astype(F32), axis=0)
    copies[...] = jnp.broadcast_to(part[None, : 2 * PART], copies.shape).astype(BF16)
    last = part[2 * PART :]
    small[...] = (last[: EXTRA // 2] + last[EXTRA // 2 :]) / GRID


def result_kernel(place, mine, other, qkv, out):
    def write(halves):
        for block in range(4):
            half = halves[block // 2]
            for part in range(C // PART):
                rows = slice(part * PART, part * PART + PART)
                for h in (0, 1):
                    piece = half[block % 2 * (C // PART) + part, h * PART : h * PART + PART].astype(F32) / GRID
                    if block < 3:
                        qkv[rows, block * C + h * 128 : block * C + h * 128 + 128] = piece
                    else:
                        out[rows, h * 128 : h * 128 + 128] = piece

    @pl.when(place[2] == 0)
    def _():
        write((mine, other))

    @pl.when(place[2] == 1)
    def _():
        write((other, mine))


def call(fn, out_shape, scratch, megabytes, microseconds, *args):
    vmem = pl.BlockSpec(memory_space=pltpu.VMEM)
    smem = pl.BlockSpec(memory_space=pltpu.SMEM)
    return pl.pallas_call(
        fn,
        out_shape=tuple(jax.ShapeDtypeStruct(s, d) for s, d in out_shape),
        in_specs=[smem if a.dtype == jnp.int32 else vmem for a in args],
        out_specs=tuple(vmem for _ in out_shape),
        scratch_shapes=[pltpu.VMEM(s, d) for s, d in scratch],
        compiler_params=pltpu.CompilerParams(vmem_limit_bytes=megabytes * 1024 * 1024),
        cost_estimate=pl.CostEstimate(flops=microseconds * 1_000_000_000, bytes_accessed=1_000_000, transcendentals=0),
    )(*args)


OWN = (BR, BC, C)
EXT = (ER, EC, C)
ONES = ((C, C), BF16)


def run_own(place, tokens, cotangent, gain, factor, wqkv, wo):
    mid = ((BR, EC, C), BF16)
    outs = [(OWN, BF16), (OWN, BF16), (OWN, BF16), (OWN, F32), ((ER, KC, NQ), F32), mid, mid, mid, mid]
    return call(own_kernel, outs, [ONES], 12, 3, place, tokens, cotangent, gain, factor, wqkv, wo)


def run_halo(rows, gain, wqkv):
    halo = ((WIN, EC, C), BF16)
    return call(halo_kernel, [halo] * 4, [ONES], 12, 1, rows, gain, wqkv)


def run_attention(place, from_a, from_b, cot, gain, factor, wqkv, own, halo):
    half = (PARTS + 1, 2 * PART, 128)
    to_rows = ((WIN, EC, C), BF16)
    outs = [(half, F32), (half, BF16), (OWN, BF16), (OWN, BF16), ((BR, EC, 2 * C), BF16), to_rows, to_rows]
    scratch = [(EXT, BF16)] * 4 + [(EXT, F32)] * 2 + [(OWN, F32), ((ER, EC, 2 * C), BF16)]
    scratch += [((4 * C, C), F32), ONES]
    return call(attention_kernel, outs, scratch, 28, 9, place, from_a, from_b, cot, gain, factor, wqkv, *own, *halo)


def run_own_grad(place, own, wqkv, wo, att_b, g_q, g_kv_own, from_a, from_b):
    to_cols = ((BR, PAD, C), BF16)
    outs = [(OWN, BF16), (OWN, F32), to_cols, to_cols]
    scratch = [((BR, EC, C), F32)]
    return call(own_grad_kernel, outs, scratch, 12, 3, place, own, wqkv, wo, att_b, g_q, g_kv_own, from_a, from_b)


def run_tokens(place, own, cot, gain, grad_normed, from_a, from_b):
    return call(token_kernel, [(OWN, F32)], [(OWN, F32)], 12, 2, place, own, cot, gain, grad_normed, from_a, from_b)[0]


def run_result(place, mine, other):
    return call(result_kernel, [((C, 3 * C), F32), ((C, C), F32)], [], 8, 1, place, mine, other)


def swap(a, b, axes):
    size = math.prod(AXIS_SIZES[AXES.index(axis)] for axis in axes)
    pairs = [[(i, i + 1) for i in range(at, size - 1, 2)] for at in (1, 0)]
    pairs = [[*some, *((j, i) for i, j in some)] for some in pairs]
    b = lax.ppermute(b, axes, pairs[1])
    return lax.ppermute(a, axes, pairs[0]), b


def body(tokens, norm_gain, qkv_weight, head_scale, out_weight, cotangent):
    row, col = lax.axis_index(ROWS), lax.axis_index(GRP)
    odd_row, odd_col = row % 2, col % 2
    place = jnp.stack([row * BR, col * BC, lax.axis_index("core"), odd_row, odd_col]).astype(jnp.int32)
    gain = norm_gain[None]
    factor = jnp.repeat(head_scale / HEAD, HEAD)[None]
    cores = [(0, 1), (1, 0)]

    rows_a, rows_b = swap(
        lax.dynamic_slice_in_dim(tokens, odd_row, WIN, 0), lax.dynamic_slice_in_dim(tokens, 1 - odd_row, WIN, 0), ROWS
    )
    own = run_own(place, tokens, cotangent, gain, factor, qkv_weight, out_weight)
    edges = [((ER, PAD, C), BF16)] * 2
    cols_a, cols_b = call(edge_kernel, edges, [((ER, PAD, C), F32)] * 2, 8, 1, place, rows_b, rows_a, tokens)
    cols_a, cols_b = swap(cols_a, cols_b, GRP)
    halo = (*run_halo(rows_a, gain, qkv_weight), *run_halo(rows_b, gain, qkv_weight))
    keep, send, att_b, g_q, g_kv_own, rows_a, rows_b = run_attention(
        place, cols_a, cols_b, cotangent, gain, factor, qkv_weight, own, halo
    )

    received = lax.ppermute(send, "core", cores)
    rows = 2 * PART + EXTRA
    (parts,) = call(chip_kernel, [((PARTS, rows, 128), BF16)], [], 8, 1, keep, received)
    parts, rows_a, rows_b = lax.optimization_barrier((parts, rows_a, rows_b))
    parts = lax.all_to_all(parts, SPLIT, 0, 0)
    rows_a, rows_b = swap(rows_a, rows_b, ROWS)
    (copies,) = call(part_kernel, [((RESTS, rows, 128), BF16)], [], 8, 1, parts)
    copies, att_b, g_kv_own = lax.optimization_barrier((copies, att_b, g_kv_own))
    parts = lax.all_to_all(copies, REST, 0, 0)
    out, grad_normed, cols_a, cols_b = run_own_grad(
        place, tokens, qkv_weight, out_weight, att_b, g_q, g_kv_own, rows_a, rows_b
    )
    copies, small = call(whole_kernel, [((PARTS, 2 * PART, 128), BF16), ((EXTRA // 2, 128), F32)], [], 8, 1, parts)
    copies, cols_a, cols_b = lax.optimization_barrier((copies, cols_a, cols_b))
    mine = lax.all_to_all(copies, SPLIT, 0, 0)
    small = small.reshape(2, C)
    scale_grad, gain_grad = small[0].reshape(HEADS, HEAD)[:, 0], small[1]
    cols_a, cols_b = swap(cols_a, cols_b, GRP)
    token_grad = run_tokens(place, tokens, cotangent, gain, grad_normed, cols_a, cols_b)
    mine, token_grad = lax.optimization_barrier((mine, token_grad))
    other = lax.ppermute(mine, "core", cores)
    qkv_grad, out_grad = run_result(place, mine, other)
    return out, token_grad, gain_grad, qkv_grad, scale_grad, out_grad


def solution(mesh):
    fine = Mesh(mesh.devices.reshape(AXIS_SIZES), AXES)
    tiles = P(ROWS, GRP, None)
    return jax.shard_map(
        body,
        mesh=fine,
        in_specs=(tiles, P(), P(), P(), P(), tiles),
        out_specs=(tiles, tiles, P(), P(), P(), P()),
        check_vma=False,
    )
```

```python
import math

import jax
import jax.numpy as jnp
from jax import lax
from jax.experimental import pallas as pl
from jax.experimental.pallas import tpu as pltpu
from jax.sharding import Mesh, PartitionSpec as P

HEADS = 4
HEAD = 64
C = 256
WIN = 3
BR = 4
BC = 128
GRID = 512

EPS = 1e-06

PAD = 8
ER = BR + 2 * WIN
EC = BC + 2 * PAD
QC = 32
KC = 48
BLOCKS = BC // QC
NQ = BR * QC
NK = ER * KC
PAIRS = HEADS // 2
LANES = 2 * HEAD

AXES = ("z", "xh", "y", "xl", "core")
AXIS_SIZES = (8, 2, 8, 2, 2)
ROWS = ("z", "xh", "y")
GRP = ("xl", "core")
SPLIT = ("xh", "xl", "y")
REST = ("z",)
PARTS = 32
RESTS = 8
HALF = 2 * C
PART = HALF // PARTS
EXTRA = 8

F32 = jnp.float32
BF16 = jnp.bfloat16


def mm(a, b, dims=((1,), (0,))):
    return lax.dot_general(a, b, (dims, ((), ())), preferred_element_type=F32)


def split_bf16(a):
    high = a.astype(BF16)
    return high, (a - high.astype(F32)).astype(BF16)


def row_stats(t):
    n = lax.rsqrt(jnp.mean(t * t, axis=-1, keepdims=True) + EPS)
    return n, t * n


def norm_grad(u, n, hat):
    return n * (u - hat * jnp.mean(u * hat, axis=-1, keepdims=True))


def ones_per_head():
    lane_head = lax.broadcasted_iota(jnp.int32, (C, C), 1) // HEAD
    row_head = lax.broadcasted_iota(jnp.int32, (C, C), 0) // HEAD
    return jnp.where(lane_head == row_head, 1.0 / HEAD, 0.0).astype(BF16)


def per_head_mean(a, ones):
    return mm(a.astype(BF16), ones)


def normalise(raw, ones):
    high, low = split_bf16(raw * raw)
    inv = lax.rsqrt(mm(high, ones) + mm(low, ones) + EPS)
    return raw * inv, inv


def widen(a, rows):
    edge = jnp.zeros((rows, PAD, C), F32)
    return jnp.concatenate([edge, a.reshape(rows, BC, C), edge], axis=1).astype(BF16)


def own_kernel(
    place, own, cot, gain, factor, wqkv, wo, q_b, d_b, normed_own, q_inv, near_mask, normed_ext, k_b, v_b, k_inv, ones
):
    ones[...] = ones_per_head()

    key_row = lax.broadcasted_iota(jnp.int32, (ER, KC, NQ), 0)
    key_col = lax.broadcasted_iota(jnp.int32, (ER, KC, NQ), 1)
    query = lax.broadcasted_iota(jnp.int32, (ER, KC, NQ), 2)
    row_gap = key_row - query // QC
    col_gap = key_col - query % QC - (PAD - WIN)
    in_rows = (key_row + place[0] - WIN >= 0) & (key_row + place[0] - WIN < GRID)
    near = (row_gap >= 0) & (row_gap <= 2 * WIN) & (col_gap >= 0) & (col_gap <= 2 * WIN)
    near_mask[...] = jnp.where(near & in_rows, 1.0, 0.0)

    @pl.loop(0, BR // 2)
    def _(i):
        rows = pl.ds(2 * i, 2)
        shape = (2, BC, C)
        _, hat = row_stats(own[rows].reshape(2 * BC, C).astype(F32))
        scaled = hat * gain[...]
        normed = scaled.astype(BF16)
        projected = mm(normed, wqkv[...])
        q, inv = normalise(projected[:, :C], ones[...])
        k, inv_k = normalise(projected[:, C : 2 * C], ones[...])
        normed_own[rows] = normed.reshape(shape)
        q_inv[rows] = inv.reshape(shape)
        q_b[rows] = (q * factor[...]).astype(BF16).reshape(shape)
        normed_ext[rows] = widen(scaled, 2)
        k_b[rows] = widen(k, 2)
        k_inv[rows] = widen(inv_k, 2)
        v_b[rows] = widen(projected[:, 2 * C :], 2)
        d = mm(cot[rows].reshape(2 * BC, C), wo[...], ((1,), (1,)))
        d_b[rows] = d.astype(BF16).reshape(shape)


def halo_kernel(rows, gain, wqkv, normed_ext, k_b, v_b, k_inv, ones):
    ones[...] = ones_per_head()
    _, hat = row_stats(rows[...].reshape(WIN * BC, C).astype(F32))
    scaled = hat * gain[...]
    projected = mm(scaled.astype(BF16), wqkv[:, C:])
    k, inv_k = normalise(projected[:, :C], ones[...])
    normed_ext[...] = widen(scaled, WIN)
    k_b[...] = widen(k, WIN)
    k_inv[...] = widen(inv_k, WIN)
    v_b[...] = widen(projected[:, C:], WIN)


def attention_kernel(
    place,
    from_a,
    from_b,
    cot,
    gain,
    factor,
    wqkv,
    q_b,
    d_b,
    normed_own,
    q_inv,
    near_mask,
    normed_mid,
    k_mid,
    v_mid,
    k_inv_mid,
    normed_a,
    k_a,
    v_a,
    k_inv_a,
    normed_b,
    k_from_b,
    v_from_b,
    k_inv_b,
    keep,
    send,
    att_b,
    g_q,
    g_kv_own,
    to_a,
    to_b,
    normed_ext,
    k_b,
    v_b,
    k_inv,
    gk,
    gv,
    gq,
    g_kv,
    acc,
    ones,
):
    ones[...] = ones_per_head()

    odd = place[4] == 1
    left = jnp.where(odd, from_b[...].astype(F32), from_a[...].astype(F32))
    right = jnp.where(odd, from_a[...].astype(F32), from_b[...].astype(F32))
    edges = jnp.concatenate([left, right], axis=0)
    _, hat = row_stats(edges.reshape(2 * ER * PAD, C))
    scaled = hat * gain[...]
    projected = mm(scaled.astype(BF16), wqkv[:, C:])
    k, inv_k = normalise(projected[:, :C], ones[...])
    for ext, mid, halo_a, halo_b, edge in (
        (normed_ext, normed_mid, normed_a, normed_b, scaled),
        (k_b, k_mid, k_a, k_from_b, k),
        (v_b, v_mid, v_a, v_from_b, projected[:, C:]),
        (k_inv, k_inv_mid, k_inv_a, k_inv_b, inv_k),
    ):
        edge = edge.reshape(2 * ER, PAD, C)
        ext[pl.ds(place[3] * (WIN + BR), WIN)] = halo_a[...]
        ext[pl.ds((1 - place[3]) * (WIN + BR), WIN)] = halo_b[...]
        ext[WIN : WIN + BR] = mid[...]
        near = ext[:, 0 : 2 * PAD].astype(F32)[:, PAD:]
        ext[:, 0 : 2 * PAD] = jnp.concatenate([edge[:ER], near], axis=1).astype(BF16)
        near = ext[:, EC - 2 * PAD : EC].astype(F32)[:, :PAD]
        ext[:, EC - 2 * PAD : EC] = jnp.concatenate([near, edge[ER:]], axis=1).astype(BF16)

    gk[...] = jnp.zeros_like(gk)
    gv[...] = jnp.zeros_like(gv)

    first = lax.broadcasted_iota(jnp.int32, (NQ, LANES), 1) < HEAD
    top = lax.broadcasted_iota(jnp.int32, (LANES, NQ), 0) < HEAD

    def both(a):
        zero = jnp.zeros_like(a)
        return jnp.concatenate([jnp.where(first, a, zero), jnp.where(first, zero, a)], axis=0)

    def own_head(a):
        return jnp.where(top, a[:, :NQ], a[:, NQ:]).T

    @pl.loop(0, BLOCKS, unroll=BLOCKS)
    def _(b):
        q_cols = pl.ds(pl.multiple_of(b * QC, QC), QC)
        k_cols = pl.ds(pl.multiple_of(b * QC, QC), KC)
        col = lax.broadcasted_iota(jnp.int32, (ER, KC, NQ), 1) + (place[1] - PAD + b * QC)
        mask = jnp.where((col >= 0) & (col < GRID), near_mask[...], 0.0).reshape(NK, NQ)
        mask = jnp.concatenate([mask, mask], axis=1)
        for p in range(PAIRS):
            lanes = slice(p * LANES, (p + 1) * LANES)
            k2 = k_b[:, k_cols, lanes].reshape(NK, LANES)
            v2 = v_b[:, k_cols, lanes].reshape(NK, LANES)
            q2 = both(q_b[:, q_cols, lanes].reshape(NQ, LANES))
            d2 = both(d_b[:, q_cols, lanes].reshape(NQ, LANES))
            e = jnp.exp(mm(k2, q2, ((1,), (1,)))) * mask
            attend = e * (1.0 / jnp.sum(e, axis=0, keepdims=True))
            attend_b = attend.astype(BF16)
            grad_probs = mm(v2, d2, ((1,), (1,)))
            delta = jnp.sum(attend * grad_probs, axis=0, keepdims=True)
            grad_scores = (attend * (grad_probs - delta)).astype(BF16)
            attended = own_head(mm(v2, attend_b, ((0,), (0,))))
            att_b[:, q_cols, lanes] = attended.astype(BF16).reshape(BR, QC, LANES)
            grad_query = own_head(mm(k2, grad_scores, ((0,), (0,))))
            gq[:, q_cols, lanes] = grad_query.reshape(BR, QC, LANES)
            gk[:, k_cols, lanes] += mm(grad_scores, q2).reshape(ER, KC, LANES)
            gv[:, k_cols, lanes] += mm(attend_b, d2).reshape(ER, KC, LANES)

    inv_factor = 1.0 / factor[...]
    grad_query = gq[...].reshape(BR * BC, C)
    q_f = q_b[...].reshape(BR * BC, C).astype(F32)
    high, low = split_bf16(grad_query * q_f)
    mean = (mm(high, ones[...]) + mm(low, ones[...])) * inv_factor
    scale_sum = jnp.sum(mean, axis=0, keepdims=True)
    g = q_inv[...].reshape(BR * BC, C) * (factor[...] * grad_query - q_f * mean)
    g = g.astype(BF16)
    g_q[...] = g.reshape(BR, BC, C)
    def put(block, total):
        parts = slice(block * (C // PART), (block + 1) * (C // PART))
        for h in (0, 1):
            acc[parts, h * PART : h * PART + PART] = total[:, h * 128 : h * 128 + 128].reshape(C // PART, PART, 128)

    put(3, mm(att_b[...].reshape(BR * BC, C), cot[...].reshape(BR * BC, C), ((0,), (0,))))
    acc_q = mm(normed_own[...].reshape(BR * BC, C), g, ((0,), (0,)))
    put(0, acc_q)

    @pl.loop(0, ER // 2, unroll=ER // 2)
    def _(i):
        rows = pl.ds(2 * i, 2)
        shape = (2, EC, C)
        grad_key = gk[rows].reshape(2 * EC, C)
        k_f = k_b[rows].reshape(2 * EC, C).astype(F32)
        mean = per_head_mean(grad_key * k_f, ones[...])
        g_k = k_inv[rows].reshape(2 * EC, C).astype(F32) * (grad_key - k_f * mean)
        g_kv[rows, :, :C] = g_k.astype(BF16).reshape(shape)
        g_kv[rows, :, C:] = gv[rows].astype(BF16)

    g_kv_own[...] = g_kv[WIN : WIN + BR]
    for ref, at in ((to_a, place[3]), (to_b, 1 - place[3])):
        g = g_kv[pl.ds(at * (WIN + BR), WIN)].reshape(WIN * EC, 2 * C)
        ref[...] = mm(g, wqkv[:, C:], ((1,), (1,))).astype(BF16).reshape(WIN, EC, C)

    acc_kv = mm(normed_ext[...].reshape(ER * EC, C), g_kv[...].reshape(ER * EC, 2 * C), ((0,), (0,)))
    put(1, acc_kv[:, :C])
    put(2, acc_kv[:, C:])

    by_feature = (
        wqkv[:, :C].astype(F32) * acc_q
        + wqkv[:, C : 2 * C].astype(F32) * acc_kv[:, :C]
        + wqkv[:, 2 * C :].astype(F32) * acc_kv[:, C:]
    )
    high, low = split_bf16(by_feature)
    every = jnp.ones((8, C), BF16)
    gain_sum = mm(every, high, ((1,), (1,))) + mm(every, low, ((1,), (1,)))
    gain_sum = gain_sum[0:1] / gain[...]

    for ref, half in ((keep, place[2]), (send, 1 - place[2])):
        ref[:PARTS] = acc[pl.ds(half * PARTS, PARTS)].astype(ref.dtype)
    small = [part.astype(F32) for part in split_bf16(jnp.concatenate([scale_sum, gain_sum], axis=0))]
    small = [a[i : i + 1, h * 128 : h * 128 + 128] for a in small for i in (0, 1) for h in (0, 1)]
    small = jnp.concatenate(small + [jnp.zeros((2 * PART - EXTRA, 128), F32)], axis=0)
    keep[PARTS] = small
    send[PARTS] = small.astype(BF16)


def own_grad_kernel(
    place, own, wqkv, wo, att_b, g_q, g_kv_own, from_a, from_b, out, grad_normed, to_a, to_b, total
):
    total[...] = mm(g_kv_own[...].reshape(BR * EC, 2 * C), wqkv[:, C:], ((1,), (1,))).reshape(BR, EC, C)
    total[pl.ds(place[3], WIN)] += from_a[...].astype(F32)
    total[pl.ds(1 - place[3], WIN)] += from_b[...].astype(F32)
    left = total[:, :PAD]
    right = total[:, PAD + BC :]
    odd = place[4] == 1
    to_a[...] = jnp.where(odd, right, left).astype(BF16)
    to_b[...] = jnp.where(odd, left, right).astype(BF16)
    by_query = mm(g_q[...].reshape(BR * BC, C), wqkv[:, :C], ((1,), (1,)))
    grad_normed[...] = by_query.reshape(OWN) + total[:, PAD : PAD + BC]
    projected = mm(att_b[...].reshape(BR * BC, C), wo[...])
    out[...] = (own[...].astype(F32) + projected.reshape(OWN)).astype(BF16)


def token_kernel(place, own, cot, gain, grad_normed, from_a, from_b, token_grad, total):
    odd = place[4] == 1
    total[...] = grad_normed[...]
    total[:, :PAD] += jnp.where(odd, from_b[...].astype(F32), from_a[...].astype(F32))
    total[:, BC - PAD :] += jnp.where(odd, from_a[...].astype(F32), from_b[...].astype(F32))
    n, hat = row_stats(own[...].reshape(BR * BC, C).astype(F32))
    grad = norm_grad(gain[...] * total[...].reshape(BR * BC, C), n, hat)
    token_grad[...] = cot[...].astype(F32) + grad.reshape(OWN)


def edge_kernel(place, rows_b, rows_a, own, to_a, to_b, last, first):
    parts = ((rows_a, place[3] * (WIN + BR)), (rows_b, (1 - place[3]) * (WIN + BR)), (own, WIN))
    for ref, at in parts:
        rows = pl.ds(at, ref.shape[0])
        last[rows] = ref[:, BC - 2 * PAD :].astype(F32)[:, PAD:]
        first[rows] = ref[:, : 2 * PAD].astype(F32)[:, :PAD]
    odd = place[4] == 1
    to_a[...] = jnp.where(odd, last[...], first[...]).astype(BF16)
    to_b[...] = jnp.where(odd, first[...], last[...]).astype(BF16)


def resplit(small):
    total = small[: EXTRA // 2] + small[EXTRA // 2 :]
    high, low = split_bf16(total)
    return jnp.concatenate([high.astype(F32), low.astype(F32)], axis=0)


def chip_kernel(keep, received, parts):
    total = keep[:PARTS] + received[:PARTS].astype(F32)
    small = resplit((keep[PARTS] + received[PARTS].astype(F32))[:EXTRA])
    small = jnp.broadcast_to(small[None], (PARTS, EXTRA, 128))
    parts[...] = jnp.concatenate([total, small], axis=1).astype(BF16)


def part_kernel(parts, copies):
    part = jnp.sum(parts[...].astype(F32), axis=0)
    part = jnp.concatenate([part[: 2 * PART], resplit(part[2 * PART :])], axis=0)
    copies[...] = jnp.broadcast_to(part[None], copies.shape).astype(BF16)


def whole_kernel(parts, copies, small):
    part = jnp.sum(parts[...].astype(F32), axis=0)
    copies[...] = jnp.broadcast_to(part[None, : 2 * PART], copies.shape).astype(BF16)
    last = part[2 * PART :]
    small[...] = (last[: EXTRA // 2] + last[EXTRA // 2 :]) / GRID


def result_kernel(place, mine, other, qkv, out):
    def write(halves):
        for block in range(4):
            half = halves[block // 2]
            for part in range(C // PART):
                rows = slice(part * PART, part * PART + PART)
                for h in (0, 1):
                    piece = half[block % 2 * (C // PART) + part, h * PART : h * PART + PART].astype(F32) * (1.0 / GRID)
                    if block < 3:
                        qkv[rows, block * C + h * 128 : block * C + h * 128 + 128] = piece
                    else:
                        out[rows, h * 128 : h * 128 + 128] = piece

    @pl.when(place[2] == 0)
    def _():
        write((mine, other))

    @pl.when(place[2] == 1)
    def _():
        write((other, mine))


def call(fn, out_shape, scratch, megabytes, microseconds, *args):
    vmem = pl.BlockSpec(memory_space=pltpu.VMEM)
    smem = pl.BlockSpec(memory_space=pltpu.SMEM)
    return pl.pallas_call(
        fn,
        out_shape=tuple(jax.ShapeDtypeStruct(s, d) for s, d in out_shape),
        in_specs=[smem if a.dtype == jnp.int32 else vmem for a in args],
        out_specs=tuple(vmem for _ in out_shape),
        scratch_shapes=[pltpu.VMEM(s, d) for s, d in scratch],
        compiler_params=pltpu.CompilerParams(vmem_limit_bytes=megabytes * 1024 * 1024),
        cost_estimate=pl.CostEstimate(flops=microseconds * 1_000_000_000, bytes_accessed=1_000_000, transcendentals=0),
    )(*args)


OWN = (BR, BC, C)
EXT = (ER, EC, C)
ONES = ((C, C), BF16)


def run_own(place, tokens, cotangent, gain, factor, wqkv, wo):
    mid = ((BR, EC, C), BF16)
    outs = [(OWN, BF16), (OWN, BF16), (OWN, BF16), (OWN, F32), ((ER, KC, NQ), F32), mid, mid, mid, mid]
    return call(own_kernel, outs, [ONES], 12, 3, place, tokens, cotangent, gain, factor, wqkv, wo)


def run_halo(rows, gain, wqkv):
    halo = ((WIN, EC, C), BF16)
    return call(halo_kernel, [halo] * 4, [ONES], 12, 1, rows, gain, wqkv)


def run_attention(place, from_a, from_b, cot, gain, factor, wqkv, own, halo):
    half = (PARTS + 1, 2 * PART, 128)
    to_rows = ((WIN, EC, C), BF16)
    outs = [(half, F32), (half, BF16), (OWN, BF16), (OWN, BF16), ((BR, EC, 2 * C), BF16), to_rows, to_rows]
    scratch = [(EXT, BF16)] * 4 + [(EXT, F32)] * 2 + [(OWN, F32), ((ER, EC, 2 * C), BF16)]
    scratch += [((2 * PARTS, 2 * PART, 128), F32), ONES]
    return call(attention_kernel, outs, scratch, 28, 9, place, from_a, from_b, cot, gain, factor, wqkv, *own, *halo)


def run_own_grad(place, own, wqkv, wo, att_b, g_q, g_kv_own, from_a, from_b):
    to_cols = ((BR, PAD, C), BF16)
    outs = [(OWN, BF16), (OWN, F32), to_cols, to_cols]
    scratch = [((BR, EC, C), F32)]
    return call(own_grad_kernel, outs, scratch, 12, 3, place, own, wqkv, wo, att_b, g_q, g_kv_own, from_a, from_b)


def run_tokens(place, own, cot, gain, grad_normed, from_a, from_b):
    return call(token_kernel, [(OWN, F32)], [(OWN, F32)], 12, 2, place, own, cot, gain, grad_normed, from_a, from_b)[0]


def run_result(place, mine, other):
    return call(result_kernel, [((C, 3 * C), F32), ((C, C), F32)], [], 8, 1, place, mine, other)


def swap(a, b, axes):
    size = math.prod(AXIS_SIZES[AXES.index(axis)] for axis in axes)
    pairs = [[(i, i + 1) for i in range(at, size - 1, 2)] for at in (1, 0)]
    pairs = [[*some, *((j, i) for i, j in some)] for some in pairs]
    b = lax.ppermute(b, axes, pairs[1])
    return lax.ppermute(a, axes, pairs[0]), b


def body(tokens, norm_gain, qkv_weight, head_scale, out_weight, cotangent):
    row, col = lax.axis_index(ROWS), lax.axis_index(GRP)
    odd_row, odd_col = row % 2, col % 2
    place = jnp.stack([row * BR, col * BC, lax.axis_index("core"), odd_row, odd_col]).astype(jnp.int32)
    gain = norm_gain[None]
    factor = jnp.repeat(head_scale / HEAD, HEAD)[None]
    cores = [(0, 1), (1, 0)]

    rows_a, rows_b = swap(
        lax.dynamic_slice_in_dim(tokens, odd_row, WIN, 0), lax.dynamic_slice_in_dim(tokens, 1 - odd_row, WIN, 0), ROWS
    )
    own = run_own(place, tokens, cotangent, gain, factor, qkv_weight, out_weight)
    edges = [((ER, PAD, C), BF16)] * 2
    cols_a, cols_b = call(edge_kernel, edges, [((ER, PAD, C), F32)] * 2, 8, 1, place, rows_b, rows_a, tokens)
    cols_a, cols_b = swap(cols_a, cols_b, GRP)
    halo = (*run_halo(rows_a, gain, qkv_weight), *run_halo(rows_b, gain, qkv_weight))
    keep, send, att_b, g_q, g_kv_own, rows_a, rows_b = run_attention(
        place, cols_a, cols_b, cotangent, gain, factor, qkv_weight, own, halo
    )

    received = lax.ppermute(send, "core", cores)
    rows = 2 * PART + EXTRA
    (parts,) = call(chip_kernel, [((PARTS, rows, 128), BF16)], [], 8, 1, keep, received)
    parts, rows_a, rows_b = lax.optimization_barrier((parts, rows_a, rows_b))
    parts = lax.all_to_all(parts, SPLIT, 0, 0)
    rows_a, rows_b = swap(rows_a, rows_b, ROWS)
    (copies,) = call(part_kernel, [((RESTS, rows, 128), BF16)], [], 8, 1, parts)
    copies, att_b, g_kv_own = lax.optimization_barrier((copies, att_b, g_kv_own))
    parts = lax.all_to_all(copies, REST, 0, 0)
    out, grad_normed, cols_a, cols_b = run_own_grad(
        place, tokens, qkv_weight, out_weight, att_b, g_q, g_kv_own, rows_a, rows_b
    )
    copies, small = call(whole_kernel, [((PARTS, 2 * PART, 128), BF16), ((EXTRA // 2, 128), F32)], [], 8, 1, parts)
    copies, cols_a, cols_b = lax.optimization_barrier((copies, cols_a, cols_b))
    mine = lax.all_to_all(copies, SPLIT, 0, 0)
    small = small.reshape(2, C)
    scale_grad, gain_grad = small[0].reshape(HEADS, HEAD)[:, 0], small[1]
    cols_a, cols_b = swap(cols_a, cols_b, GRP)
    token_grad = run_tokens(place, tokens, cotangent, gain, grad_normed, cols_a, cols_b)
    mine, token_grad = lax.optimization_barrier((mine, token_grad))
    other = lax.ppermute(mine, "core", cores)
    qkv_grad, out_grad = run_result(place, mine, other)
    return out, token_grad, gain_grad, qkv_grad, scale_grad, out_grad


def solution(mesh):
    fine = Mesh(mesh.devices.reshape(AXIS_SIZES), AXES)
    tiles = P(ROWS, GRP, None)
    return jax.shard_map(
        body,
        mesh=fine,
        in_specs=(tiles, P(), P(), P(), P(), tiles),
        out_specs=(tiles, tiles, P(), P(), P(), P()),
        check_vma=False,
    )
```
